32 devices in a mesh: expert: 8 (over z, core), shard: 4 (over y, x).
Axes of the slice: x: 2, y: 2, z: 4, core: 2. Of those that a mesh axis runs over, the one named last changes fastest.
Arguments:
- tokens: bfloat16 [16384, 1024], P(('expert', 'shard')), may hold values from -6 to 6
- gain_attn: bfloat16 [1024], P('shard'), may hold values from 0.099609375 to 1.8984375
- w_query: bfloat16 [1024, 1024], P('shard'), may hold values from -0.1875 to 0.1875
- key_weight: bfloat16 [1024, 512], P('shard'), may hold values from -0.1875 to 0.1875
- value_weight: bfloat16 [1024, 512], P('shard'), may hold values from -0.1875 to 0.1875
- w_out: bfloat16 [1024, 1024], P('shard'), may hold values from -1.5 to 1.5
- gain_mix: bfloat16 [1024], P('shard'), may hold values from 0.099609375 to 1.8984375
- router: bfloat16 [1024, 16], P('shard'), may hold values from -0.09375 to 0.09375
- w_gate: bfloat16 [16, 1024, 512], P('expert', 'shard'), may hold values from -0.1875 to 0.1875
- w_up: bfloat16 [16, 1024, 512], P('expert', 'shard'), may hold values from -0.1875 to 0.1875
- w_down: bfloat16 [16, 512, 1024], P('expert', 'shard'), may hold values from -0.75 to 0.75
- routes: int32 [16384, 8], P(('expert', 'shard')), may hold values from 0 to 15, all different within a row; in each aligned block of 512 rows (0 to 511, 512 to 1023, ...) at most 384 rows name the same one
- lengths: int32 [32, 4], P(('expert', 'shard')), may hold values from 1 to 256, 512 in all within a row
- cotangent: bfloat16 [16384, 1024], P(('expert', 'shard')), may hold values from -6 to 6
Outputs:
- out_tokens: bfloat16 [16384, 1024], P(('expert', 'shard'))
- grad_tokens: bfloat16 [16384, 1024], P(('expert', 'shard'))
- grad_gain_attn: float32 [1024], P('shard')
- grad_w_query: float32 [1024, 1024], P('shard')
- grad_w_key: float32 [1024, 512], P('shard')
- grad_w_value: float32 [1024, 512], P('shard')
- grad_w_out: float32 [1024, 1024], P('shard')
- grad_gain_mix: float32 [1024], P('shard')
- grad_router: float32 [1024, 16], P('shard')
- grad_w_gate: float32 [16, 1024, 512], P('expert', 'shard')
- grad_w_up: float32 [16, 1024, 512], P('expert', 'shard')
- grad_w_down: float32 [16, 512, 1024], P('expert', 'shard')
The draws below stay inside these ranges and needn't reach their ends.
Inputs may be any that keep to these rules, and one draw needn't show every extreme that they name: `routes`: each row names 8 different experts. The 512 rows of one device name no expert more than 384 times, and in every draw some device's rows name some expert exactly 384 times. Row b holds, in order, the lengths of the 4 documents of token block b; each row sums to 512 and its longest is exactly 256.
All inputs are finite; a program needn't handle non-finite values.
Results may differ from the reference program's by a relative error of at most 0.02.
Values may be sent and summed in bfloat16 or wider, within the bound.
No kernel may reach another device: no remote copies, remote signals or barrier semaphores. Data moves between devices by JAX's collectives and lax.ppermute only.
A program may use at most 256 MiB of HBM per device.

```python
import math
import jax
import jax.numpy as jnp
import numpy as np
from jax import lax

MODEL_DIM = 1024
QUERY_HEADS = 16
KEY_VALUE_HEADS = 8
HEAD_DIM = 64
FF = 512
TOP = 8
DEVICE_TOKENS = 512
DOCS = 4
EXPERTS = 16
CAP = 384
BLOCKS = 32
TOKENS = 16384


def steps_of(own_key, shape, cuts, low, largest):
    gain, own = 1.0, jax.random.fold_in(own_key, 6)
    for dim, shards_of in cuts:
        heights = jnp.exp(jax.random.uniform(jax.random.fold_in(own, dim), (shards_of,), jnp.float32, low / len(cuts), largest / len(cuts)))
        gain = gain * jnp.repeat(heights, shape[dim] // shards_of).reshape([-1 if axis == dim else 1 for axis in range(len(shape))])
    return gain


def length_profile(count, total, limit, lean):
    portions = [(1 << 20) // math.isqrt(rank ** lean) + 1 for rank in range(2, count + 1)]
    rest, counts = total - limit - (count - 1), [1] * (count - 1)
    while rest > 0:
        candidates = [i for i in range(count - 1) if counts[i] < limit]
        pool, budget = sum([portions[i] for i in candidates]), rest
        for i in candidates:
            addition = min(limit - counts[i], max(1, budget * portions[i] // pool), rest)
            counts[i] = counts[i] + addition
            rest = rest - addition
    return np.array([limit] + counts)


def uneven(stream_key, amount, total, limit, slope):
    if amount == 2:
        one = jax.random.randint(stream_key, (), max(1, total - limit), min(limit, total - 1) + 1)
        return jnp.stack([one, total - one])
    sizes = jnp.asarray(length_profile(amount, total, limit, slope), jnp.int32)
    pairs = (amount - 1) // 2
    donor, sink = sizes[1:1 + 2 * pairs:2], sizes[2:2 + 2 * pairs:2]
    room = jnp.minimum(donor - 1, limit - sink)
    moved = jax.random.randint(jax.random.fold_in(stream_key, 1), (pairs,), 0, 1 << 20) % (room + 1)
    sizes = sizes.at[1:1 + 2 * pairs:2].set(donor - moved).at[2:2 + 2 * pairs:2].set(sink + moved)
    return sizes[jax.random.permutation(jax.random.fold_in(stream_key, 2), amount)]


def shared_out(own_key, own, number, rows, amount, top, most, lean):
    order = jax.random.permutation(own_key, amount)
    packed, ordinary = portions_of(amount, rows * top, most, lean, True), portions_of(amount, rows * top, most, lean, False)
    places = jnp.arange(amount)

    def named(sizes, offset_by):
        used = int((sizes > 0).sum())
        fixed = max(1, used // 4)
        shifted = fixed + (places - fixed + offset_by * (used - fixed)) % max(1, amount - fixed)
        return jnp.zeros((amount,), jnp.int32).at[order[jnp.where(places < fixed, places, shifted)]].set(jnp.asarray(sizes, jnp.int32))

    sizes = jnp.where(number % 4 == 0, named(packed, number // 4), named(ordinary, number - number // 4 - 1))
    mixed = jax.random.permutation(jax.random.fold_in(own, 3), amount)
    giver, taker = mixed[0:amount // 2 * 2:2], mixed[1:amount // 2 * 2:2]
    margin = jnp.minimum(sizes[giver] - 1, most - sizes[taker]) // 2
    margin = jnp.where((giver == order[0]) | (taker == order[0]) | (sizes[taker] == 0), 0, jnp.maximum(margin, 0))
    shifted = jax.random.randint(jax.random.fold_in(own, 4), (amount // 2,), 0, 1 << 20) % (margin + 1)
    sizes = sizes.at[giver].add(-shifted).at[taker].add(shifted)
    labels = jnp.searchsorted(jnp.cumsum(sizes), jnp.arange(rows * top), side="right").astype(jnp.int32)
    grid = labels.reshape(top, rows).T
    grid = grid[jax.random.permutation(jax.random.fold_in(own, 1), rows)]
    offset_by = jax.random.randint(jax.random.fold_in(own, 2), (rows, 1), 0, top)
    return jnp.take_along_axis(grid, (jnp.arange(top)[None, :] + offset_by) % top, axis=1)


def portions_of(count, total, most, lean, full):
    portions = [(1 << 20) // math.isqrt(grade ** lean) + 1 for grade in range(1, count + 1)]
    largest = most if full else min(most, max(-(-total // count), total * portions[0] // sum(portions)))
    least = 1 if total - largest >= count - 1 else 0
    holding, surplus = [largest] + [least] * (count - 1), total - largest - least * (count - 1)
    while surplus > 0:
        movable = [i for i in range(1, count) if holding[i] < largest] or [i for i in range(1, count) if holding[i] < most]
        mass, left = sum([portions[i] for i in movable]), surplus
        for i in movable:
            addition = min(most - holding[i], max(1, left * portions[i] // mass), surplus)
            holding[i] = holding[i] + addition
            surplus = surplus - addition
    return np.array(holding)


def scatter_about(stream_key, shape, spread, reach, shards=(), kind=jnp.bfloat16):
    drawn = jax.random.normal(stream_key, shape, jnp.float32) * spread
    if len(shards) > 0:
        drawn = steps_of(stream_key, shape, shards, -0.22, 0.18) * drawn
    return jnp.clip(drawn, min=-reach, max=reach).astype(kind)


def setup_inputs(seed: int = 0) -> dict:
    seeds = jax.random.split(jax.random.key(seed), 15)
    tokens = scatter_about(seeds[0], (TOKENS, MODEL_DIM), 1.0, 6.0, ((0, 32),))
    gain_attn = jnp.clip(1.0 + 0.18 * jax.random.normal(seeds[1], (MODEL_DIM,), jnp.float32), 0.099609375, 1.8984375).astype(jnp.bfloat16)
    w_query = scatter_about(seeds[2], (MODEL_DIM, QUERY_HEADS * HEAD_DIM), MODEL_DIM ** -0.5, 0.1875, ((0, 4),))
    key_weight = scatter_about(seeds[3], (MODEL_DIM, KEY_VALUE_HEADS * HEAD_DIM), MODEL_DIM ** -0.5, 0.1875, ((0, 4),))
    value_weight = scatter_about(seeds[4], (MODEL_DIM, KEY_VALUE_HEADS * HEAD_DIM), MODEL_DIM ** -0.5, 0.1875, ((0, 4),))
    w_out = scatter_about(seeds[5], (QUERY_HEADS * HEAD_DIM, MODEL_DIM), (QUERY_HEADS * HEAD_DIM // 64) ** -0.5, 1.5, ((0, 4),))
    gain_mix = jnp.clip(1.0 + 0.18 * jax.random.normal(seeds[6], (MODEL_DIM,), jnp.float32), 0.099609375, 1.8984375).astype(jnp.bfloat16)
    router = scatter_about(seeds[7], (MODEL_DIM, EXPERTS), (4 * MODEL_DIM) ** -0.5, 0.09375, ((0, 4),))
    w_gate = scatter_about(seeds[8], (EXPERTS, MODEL_DIM, FF), MODEL_DIM ** -0.5, 0.1875, ((0, 8), (1, 4)))
    w_up = scatter_about(seeds[9], (EXPERTS, MODEL_DIM, FF), MODEL_DIM ** -0.5, 0.1875, ((0, 8), (1, 4)))
    w_down = scatter_about(seeds[10], (EXPERTS, FF, MODEL_DIM), (FF // 8) ** -0.5, 0.75, ((0, 8), (1, 4)))
    routes_keys = jax.random.split(jax.random.fold_in(seeds[11], 1), TOKENS // DEVICE_TOKENS)
    routes_turns = jax.random.permutation(jax.random.fold_in(seeds[11], 3), TOKENS // DEVICE_TOKENS)
    routes = jax.vmap(lambda own, number: shared_out(jax.random.fold_in(seeds[11], 2), own, number, DEVICE_TOKENS, EXPERTS, TOP, CAP, 1))(routes_keys, routes_turns).reshape((TOKENS, TOP))
    lengths = jax.vmap(lambda own: uneven(own, DOCS, DEVICE_TOKENS, DEVICE_TOKENS // 2, 2))(jax.random.split(seeds[12], BLOCKS)).reshape((BLOCKS, DOCS)).astype(jnp.int32)
    cotangent = scatter_about(seeds[13], (TOKENS, MODEL_DIM), 1.0, 6.0, ((0, 32),))
    return dict(tokens=tokens, gain_attn=gain_attn, w_query=w_query, key_weight=key_weight, value_weight=value_weight, w_out=w_out, gain_mix=gain_mix, router=router, w_gate=w_gate, w_up=w_up, w_down=w_down, routes=routes, lengths=lengths, cotangent=cotangent)


@jax.custom_vjp
def lower_precision(v):
    return lax.optimization_barrier(v.astype(jnp.bfloat16)).astype(jnp.float32)

@jax.custom_vjp
def lower_precision_backward(v):
    return v

def low_keep(v):
    return (lower_precision(v), None)

def low_pass(kept, grad):
    return (grad,)

def back_keep(v):
    return (v, None)

def back_low(kept, grad):
    return (lower_precision(grad),)
lower_precision.defvjp(low_keep, low_pass)
lower_precision_backward.defvjp(back_keep, back_low)

def precise_product(left_side, right_side):
    return jnp.dot(left_side, right_side, precision=lax.Precision.HIGHEST, preferred_element_type=jnp.float32)

def normalize(values, gain_vector):
    return values * lax.rsqrt(lax.optimization_barrier(jnp.mean(values * values, axis=-1, keepdims=True)) + 1e-06) * gain_vector

def apply_rotary(values, cosine_table, sine_lookup):
    half_width = values.shape[-1] // 2
    first_half = values[..., :half_width]
    second_half = values[..., half_width:]
    return jnp.concatenate([first_half * cosine_table - second_half * sine_lookup, second_half * cosine_table + first_half * sine_lookup], axis=-1)

def place_tables(lengths_row, total_rows, head_width):
    doc_ends = jnp.cumsum(lengths_row)
    token_index = jnp.arange(total_rows, dtype=jnp.int32)
    past_end = token_index[:, None] >= doc_ends[None, :]
    document = lax.optimization_barrier(jnp.sum(past_end.astype(jnp.int32), axis=1))
    doc_start = lax.optimization_barrier(jnp.sum(jnp.where(past_end, lengths_row[None, :], 0), axis=1))
    position = (token_index - doc_start).astype(jnp.float32)
    half_width = head_width // 2
    inverse = 10000.0 ** (-(jnp.arange(half_width, dtype=jnp.float32) * 2.0 / head_width))
    angles = position[:, None] * inverse[None, :]
    allowed = (document[:, None] == document[None, :]) & (token_index[None, :] <= token_index[:, None])
    return (jnp.cos(angles)[:, None, :], jnp.sin(angles)[:, None, :], allowed)

def reference(tokens, gain_attn, w_query, key_weight, value_weight, w_out, gain_mix, router, w_gate, w_up, w_down, routes, lengths, cotangent):
    query_group_width = QUERY_HEADS // KEY_VALUE_HEADS
    score_scale = 1.0 / math.sqrt(HEAD_DIM)
    flat_routes = routes.reshape(BLOCKS, DEVICE_TOKENS * TOP)
    expert_ids = jnp.arange(EXPERTS, dtype=jnp.int32)
    onehot = (flat_routes[:, :, None] == expert_ids[None, None, :]).astype(jnp.int32)
    earlier = lax.optimization_barrier(jnp.sum((jnp.cumsum(onehot, axis=1) - onehot) * onehot, axis=2))
    slot_index = (jnp.arange(BLOCKS, dtype=jnp.int32)[:, None] * CAP + earlier).astype(jnp.int32)
    source = jnp.arange(TOKENS * TOP, dtype=jnp.int32).reshape(BLOCKS, DEVICE_TOKENS * TOP)
    slot_table = jnp.full((EXPERTS, BLOCKS * CAP), -1, jnp.int32).at[flat_routes.reshape(-1), slot_index.reshape(-1)].set(source.reshape(-1))
    combine_index = (flat_routes * (BLOCKS * CAP) + slot_index).reshape(-1).astype(jnp.int32)

    def attend_block(pieces, query_w, key_matrix, value_matrix):
        normalized_block, lengths_row = pieces
        cosine_table, sine_lookup, allowed = place_tables(lengths_row, DEVICE_TOKENS, HEAD_DIM)
        query_rows = lower_precision(apply_rotary(lower_precision_backward(precise_product(normalized_block, query_w)).reshape(DEVICE_TOKENS, QUERY_HEADS, HEAD_DIM), cosine_table, sine_lookup))
        key_matrix_rows = lower_precision(apply_rotary(lower_precision_backward(precise_product(normalized_block, key_matrix)).reshape(DEVICE_TOKENS, KEY_VALUE_HEADS, HEAD_DIM), cosine_table, sine_lookup))
        value_matrix_rows = lower_precision(lower_precision_backward(precise_product(normalized_block, value_matrix))).reshape(DEVICE_TOKENS, KEY_VALUE_HEADS, HEAD_DIM)
        key_matrix_rows = jnp.repeat(key_matrix_rows, query_group_width, axis=1)
        value_matrix_rows = jnp.repeat(value_matrix_rows, query_group_width, axis=1)
        scores = lower_precision_backward(jnp.einsum('qhd,khd->hqk', query_rows, key_matrix_rows, precision=lax.Precision.HIGHEST) * score_scale)
        scores = jnp.where(allowed[None], scores, -1e+30)
        probability = lower_precision(jax.nn.softmax(scores, axis=-1))
        mixed_heads = jnp.einsum('hqk,khd->qhd', probability, value_matrix_rows, precision=lax.Precision.HIGHEST)
        return lower_precision(lower_precision_backward(mixed_heads)).reshape(DEVICE_TOKENS, QUERY_HEADS * HEAD_DIM)

    def forward(inputs, gain_one, query_w, key_matrix, value_matrix, output_matrix, gain_two, router_w, gate_w, up_w, down_w):
        normalized_input = lower_precision(normalize(inputs, gain_one))

        def attend(pieces):
            return attend_block(pieces, query_w, key_matrix, value_matrix)
        mixed_heads = lax.map(jax.checkpoint(attend), (normalized_input.reshape(BLOCKS, DEVICE_TOKENS, MODEL_DIM), lengths)).reshape(TOKENS, QUERY_HEADS * HEAD_DIM)
        hidden_state = inputs + lower_precision_backward(precise_product(mixed_heads, output_matrix))
        mixed_in = lower_precision(normalize(hidden_state, gain_two))
        logits = lower_precision_backward(precise_product(mixed_in, router_w))
        gate_probs = jax.nn.softmax(jnp.take_along_axis(logits, routes, axis=1), axis=-1)

        def expert_apply(pieces):
            slot_rows, gate_one, up_one, down_one = pieces
            live_slot = slot_rows >= 0
            token_rows = jnp.where(live_slot, slot_rows, 0) // TOP
            arrived = lower_precision_backward(mixed_in[token_rows]) * live_slot[:, None].astype(jnp.float32)
            gate_val = lower_precision_backward(precise_product(arrived, gate_one))
            up_val = lower_precision_backward(precise_product(arrived, up_one))
            inner_act = lower_precision(jax.nn.silu(gate_val) * up_val)
            return lower_precision(lower_precision_backward(precise_product(inner_act, down_one)))
        expert_out = lax.map(jax.checkpoint(expert_apply), (slot_table, gate_w, up_w, down_w))
        gathered = expert_out.reshape(EXPERTS * BLOCKS * CAP, MODEL_DIM)[combine_index].reshape(TOKENS, TOP, MODEL_DIM)
        return hidden_state + lax.optimization_barrier(jnp.sum(gate_probs[:, :, None] * gathered, axis=1))
    primals = (tokens.astype(jnp.float32), gain_attn.astype(jnp.float32), w_query.astype(jnp.float32), key_weight.astype(jnp.float32), value_weight.astype(jnp.float32), w_out.astype(jnp.float32), gain_mix.astype(jnp.float32), router.astype(jnp.float32), w_gate.astype(jnp.float32), w_up.astype(jnp.float32), w_down.astype(jnp.float32))
    output, pull_back = jax.vjp(forward, *primals)
    gradients = pull_back(cotangent.astype(jnp.float32))
    return (output.astype(jnp.bfloat16), gradients[0].astype(jnp.bfloat16), gradients[1], gradients[2], gradients[3], gradients[4], gradients[5], gradients[6], gradients[7], gradients[8], gradients[9], gradients[10])
```

```python
import functools
import math

import jax
import jax.numpy as jnp
from jax import lax
from jax.experimental import pallas as pl
from jax.experimental.pallas import tpu as pltpu
from jax.sharding import PartitionSpec as P

QUERY_HEADS = 16
KEY_VALUE_HEADS = 8
HEAD_DIM = 64
LANES = 128
F32 = jnp.float32
BF16 = jnp.bfloat16


def normalize(values, gain_vector):
    return (
        values * lax.rsqrt(jnp.mean(values * values, axis=-1, keepdims=True) + 1e-06) * gain_vector
    )


def apply_rotary(values, cosine_table, sine_lookup):
    half_width = values.shape[-1] // 2
    first_half = values[..., :half_width]
    second_half = values[..., half_width:]
    return jnp.concatenate(
        [
            first_half * cosine_table - second_half * sine_lookup,
            second_half * cosine_table + first_half * sine_lookup,
        ],
        axis=-1,
    )


def place_tables(lengths_row, total_rows, head_width):
    doc_ends = jnp.cumsum(lengths_row)
    token_index = jnp.arange(total_rows, dtype=jnp.int32)
    past_end = token_index[:, None] >= doc_ends[None, :]
    document = jnp.sum(past_end.astype(jnp.int32), axis=1)
    doc_start = jnp.sum(jnp.where(past_end, lengths_row[None, :], 0), axis=1)
    position = (token_index - doc_start).astype(jnp.float32)
    half_width = head_width // 2
    inverse = 10000.0 ** (-(jnp.arange(half_width, dtype=jnp.float32) * 2.0 / head_width))
    angles = position[:, None] * inverse[None, :]
    allowed = (document[:, None] == document[None, :]) & (
        token_index[None, :] <= token_index[:, None]
    )
    return (jnp.cos(angles)[:, None, :], jnp.sin(angles)[:, None, :], allowed)


def matrix_product(left_side, right_side):
    return jnp.dot(left_side, right_side, preferred_element_type=jnp.float32)


def product_tn(left_side, right_side):
    return lax.dot_general(
        left_side, right_side, (((0,), (0,)), ((), ())), preferred_element_type=jnp.float32
    )


def product_transposed_right(left_side, right_side):
    return lax.dot_general(
        left_side, right_side, (((1,), (1,)), ((), ())), preferred_element_type=jnp.float32
    )


def pick(blocks, index):
    return lax.dynamic_index_in_dim(blocks, index, 0, keepdims=False)


def gather_pieces(piece):
    count = lax.axis_size("shard")
    if count == 4:
        me = lax.axis_index("shard")
        pieces = [(piece, me)]
        for flip in (1, 2, 3):
            got = lax.ppermute(piece, "shard", [(i, i ^ flip) for i in range(4)])
            pieces.append((got, me ^ flip))
        return pieces
    every = lax.all_gather(piece, "shard", axis=0)
    return [(every[i], jnp.int32(i)) for i in range(count)]


def swap_cores(value):
    size = lax.axis_size("expert")
    return lax.ppermute(value, "expert", [(i, i ^ 1) for i in range(size)])


def gather_rows(rows):
    core = lax.axis_index("expert") % 2
    half = rows.shape[0] // 2
    mine = lax.dynamic_slice_in_dim(rows, core * half, half, 0)
    pieces = gather_pieces(mine)
    count = len(pieces)
    kept = jnp.stack([piece for piece, _ in pieces])
    other = swap_cores(kept)
    low = jnp.where(core == 0, kept, other)
    high = jnp.where(core == 0, other, kept)
    both = jnp.stack([low, high], axis=1).reshape(count, rows.shape[0], rows.shape[1])
    me = lax.axis_index("shard")
    if count == 4:
        both = jnp.concatenate([pick(both, me ^ i) for i in range(4)], axis=0)
    return both.reshape(count * rows.shape[0], rows.shape[1])


def scatter_sum(blocks):
    count = lax.axis_size("shard")
    if count != 4:
        return lax.psum_scatter(blocks.astype(BF16), "shard", scatter_dimension=0).astype(F32)
    me = lax.axis_index("shard")
    total = pick(blocks, me).astype(F32)
    for flip in (1, 2, 3):
        sent = pick(blocks, me ^ flip).astype(BF16)
        got = lax.ppermute(sent, "shard", [(i, i ^ flip) for i in range(4)])
        total = total + got.astype(F32)
    return total


def sum_everywhere(grad):
    count = lax.axis_size("shard")
    size = lax.axis_size("expert")
    layers = size // 2
    place = lax.axis_index("expert")
    core, layer = place % 2, place // 2
    width = grad.shape[1]
    half = grad.shape[0] // count // 2
    blocks = grad.reshape(count, 2, half, width)
    mine = lax.dynamic_index_in_dim(blocks, core, 1, keepdims=False)
    away = lax.dynamic_index_in_dim(blocks, 1 - core, 1, keepdims=False)
    paired = mine + swap_cores(away.astype(BF16)).astype(F32)
    local = scatter_sum(paired).reshape(layers, half // layers, width)
    total = pick(local, layer)
    for step in range(1, layers):
        perm = [(i, (i + 2 * step) % size) for i in range(size)]
        sent = pick(local, (layer + step) % layers).astype(BF16)
        total = total + lax.ppermute(sent, "expert", perm).astype(F32)
    total = total.astype(BF16)
    parts = jnp.zeros((layers, half // layers, width), BF16)
    parts = lax.dynamic_update_index_in_dim(parts, total, layer, 0)
    for step in range(1, layers):
        perm = [(i, (i + 2 * step) % size) for i in range(size)]
        got = lax.ppermute(total, "expert", perm)
        parts = lax.dynamic_update_index_in_dim(parts, got, (layer - step) % layers, 0)
    mine = parts.reshape(half, width)
    other = swap_cores(mine)
    low = jnp.where(core == 0, mine, other)
    high = jnp.where(core == 0, other, mine)
    return jnp.concatenate([low, high], axis=0).astype(F32)


def expert_kernel(count, experts, place_ref, x_ref, dy_ref, mask_ref, router_ref, *refs):
    pieces = refs[:count]
    out_ref, row_ref, act_ref, gate_ref, up_ref, score_ref, gu, down, sem = refs[count:]
    local, rows, width = pieces[0].shape
    third = rows // 3
    hidden = width // 2

    @pl.when(pl.program_id(0) == 0)
    def _():
        copies = []
        for i in range(count):
            at = place_ref[i]
            copies.append(
                pltpu.make_async_copy(
                    pieces[i].at[:, pl.ds(0, 2 * third), :],
                    gu.at[:, pl.ds(pl.multiple_of(at * (2 * third), 16), 2 * third), :],
                    sem.at[2 * i],
                )
            )
            copies.append(
                pltpu.make_async_copy(
                    pieces[i].at[:, pl.ds(2 * third, third), :],
                    down.at[:, pl.ds(pl.multiple_of(at * third, 16), third), :],
                    sem.at[2 * i + 1],
                )
            )
        for copy in copies:
            copy.start()
        for copy in copies:
            copy.wait()

    x = x_ref[...]
    dy = dy_ref[...]
    lane = lax.broadcasted_iota(jnp.int32, (x.shape[0], LANES), 1)
    logits = jnp.where(
        mask_ref[...] > 0, jnp.dot(x, router_ref[...], preferred_element_type=F32), -1e30
    )
    powers = jnp.exp(logits - jnp.max(logits, axis=1, keepdims=True))
    chances = powers / jnp.sum(powers, axis=1, keepdims=True)
    out = None
    row = None
    scores = jnp.zeros((x.shape[0], LANES), F32)
    for j in range(local):
        own = place_ref[count] * local + j
        gate = jnp.sum(jnp.where(lane == own, chances, 0.0), axis=1, keepdims=True)
        left = gu[j, :, :hidden]
        right = gu[j, :, hidden:]
        back = down[j]
        gate_val = jnp.dot(x, left, preferred_element_type=F32)
        up_val = jnp.dot(x, right, preferred_element_type=F32)
        inner_grad = product_transposed_right(dy, back)
        sigmoid = 1.0 / (1.0 + jnp.exp(-gate_val))
        swish = gate_val * sigmoid
        inner = (swish * up_val).astype(BF16).astype(F32)
        score = jnp.sum(inner * inner_grad, axis=1, keepdims=True)
        scores = jnp.where(lane == j, score, scores)
        act = (gate * inner).astype(BF16)
        scaled = gate * inner_grad
        gate_back = (scaled * up_val * sigmoid * (1.0 + gate_val * (1.0 - sigmoid))).astype(BF16)
        up_back = (scaled * swish).astype(BF16)
        act_ref[:, j * hidden : (j + 1) * hidden] = act
        gate_ref[:, j * hidden : (j + 1) * hidden] = gate_back
        up_ref[:, j * hidden : (j + 1) * hidden] = up_back
        part = jnp.dot(act, back, preferred_element_type=F32)
        out = part if out is None else out + part
        part = product_transposed_right(gate_back, left) + product_transposed_right(up_back, right)
        row = part if row is None else row + part
    out_ref[...] = out.astype(BF16)
    row_ref[...] = row.astype(BF16)
    score_ref[...] = scores


def run_experts(every_x, every_dy, mask, router, pieces, tile):
    count = len(pieces)
    total, width = every_x.shape
    local, rows, _ = pieces[0][0].shape
    third = rows // 3
    hidden = width // 2
    place = jnp.stack([index for _, index in pieces] + [lax.axis_index("expert")]).astype(jnp.int32)
    block = pl.BlockSpec((tile, width), lambda i, p: (i, 0))
    thin = pl.BlockSpec((tile, LANES), lambda i, p: (i, 0))
    steps = every_dy.shape[1] // tile
    return pl.pallas_call(
        functools.partial(expert_kernel, count, router.shape[1]),
        grid_spec=pltpu.PrefetchScalarGridSpec(
            num_scalar_prefetch=1,
            grid=(total // tile,),
            in_specs=[
                block,
                pl.BlockSpec((None, tile, width), lambda i, p: (i // steps, i % steps, 0)),
                thin,
                pl.BlockSpec((width, LANES), lambda i, p: (0, 0)),
            ]
            + [pl.BlockSpec(memory_space=pl.ANY)] * count,
            out_specs=[block, block, block, block, block, thin],
            scratch_shapes=[
                pltpu.VMEM((local, 2 * third * count, width), BF16),
                pltpu.VMEM((local, third * count, width), BF16),
                pltpu.SemaphoreType.DMA((2 * count,)),
            ],
        ),
        out_shape=[jax.ShapeDtypeStruct((total, width), BF16)] * 5
        + [jax.ShapeDtypeStruct((total, LANES), F32)],
        compiler_params=pltpu.CompilerParams(vmem_limit_bytes=58 * 1024 * 1024),
        cost_estimate=pl.CostEstimate(
            flops=2 * total * width * width * 6, bytes_accessed=total * width * 14, transcendentals=0
        ),
        name="experts",
    )(place, every_x, every_dy, mask, router, *[piece for piece, _ in pieces])


def per_device(
    tokens,
    gain_attn,
    w_query,
    key_weight,
    value_weight,
    w_out,
    gain_mix,
    router,
    w_gate,
    w_up,
    w_down,
    routes,
    lengths,
    cotangent,
):
    total_rows, model_width = tokens.shape
    query_group_width = QUERY_HEADS // KEY_VALUE_HEADS
    experts = router.shape[1]
    local_experts, _, hidden = w_gate.shape
    peers = lax.axis_size("expert")
    count = lax.axis_size("shard")
    part_rows = w_query.shape[0]
    kv_width = key_weight.shape[1]
    score_scale = 1.0 / math.sqrt(HEAD_DIM)

    small = jnp.concatenate(
        [
            router,
            gain_attn[:, None],
            gain_mix[:, None],
            jnp.zeros((part_rows, LANES - experts - 2), BF16),
        ],
        axis=1,
    )
    first_weights = gather_rows(
        jnp.concatenate([w_query, key_weight, value_weight, small], axis=1)
    )
    q_end = w_query.shape[1]
    query_w = first_weights[:, :q_end]
    key_matrix = first_weights[:, q_end : q_end + kv_width]
    value_matrix = first_weights[:, q_end + kv_width : q_end + 2 * kv_width]
    small_all = first_weights[:, q_end + 2 * kv_width :]
    gain_first = small_all[:, experts].astype(F32)
    gain_second = small_all[:, experts + 1].astype(F32)
    router_lanes = jnp.where(jnp.arange(LANES)[None, :] < experts, small_all, jnp.zeros((), BF16))
    router_w = small_all[:, :experts]
    output_matrix = gather_rows(w_out)
    packed = jnp.concatenate([jnp.concatenate([w_gate, w_up], axis=2), w_down], axis=1)
    pieces = gather_pieces(packed)

    expert_ids = jnp.arange(experts, dtype=jnp.int32)
    chosen = jnp.any(routes[:, :, None] == expert_ids[None, None, :], axis=1)
    mask_rows = total_rows * experts // model_width
    mask_space = -(-mask_rows // 16) * 16
    every_dy = lax.all_gather(
        jnp.concatenate(
            [
                cotangent,
                jnp.pad(
                    chosen.astype(BF16).reshape(mask_rows, model_width),
                    ((0, mask_space - mask_rows), (0, 0)),
                ),
            ],
            axis=0,
        ),
        "expert",
        axis=0,
    )
    every_mask = jnp.pad(
        every_dy[:, total_rows : total_rows + mask_rows].reshape(peers * total_rows, experts),
        ((0, 0), (0, LANES - experts)),
    )

    inputs = tokens.astype(jnp.float32)
    normalized_input = normalize(inputs, gain_first).astype(jnp.bfloat16)
    cosine_table, sine_lookup, allowed = place_tables(lengths[0], total_rows, HEAD_DIM)
    query_raw = matrix_product(normalized_input, query_w).reshape(total_rows, QUERY_HEADS, HEAD_DIM)
    unrotated_keys = matrix_product(normalized_input, key_matrix).reshape(
        total_rows, KEY_VALUE_HEADS, HEAD_DIM
    )
    query_rows = (
        apply_rotary(query_raw, cosine_table, sine_lookup)
        .astype(jnp.bfloat16)
        .reshape(total_rows, KEY_VALUE_HEADS, query_group_width, HEAD_DIM)
    )
    key_matrix_rows = apply_rotary(unrotated_keys, cosine_table, sine_lookup).astype(jnp.bfloat16)
    value_matrix_rows = (
        matrix_product(normalized_input, value_matrix)
        .astype(jnp.bfloat16)
        .reshape(total_rows, KEY_VALUE_HEADS, HEAD_DIM)
    )

    def score_table():
        raw_scores = (
            jnp.einsum(
                "vuol,mul->uovm", query_rows, key_matrix_rows, preferred_element_type=jnp.float32
            )
            * score_scale
        )
        return jnp.where(allowed[None, None], raw_scores, -1e30)

    scores = score_table()
    top_score = jnp.max(scores, axis=-1, keepdims=True)
    weights = jnp.exp(scores - top_score)
    sum_weights = jnp.sum(weights, axis=-1, keepdims=True)
    probability = weights / sum_weights
    log_total = top_score + jnp.log(sum_weights)
    lower_probabilities = probability.astype(jnp.bfloat16)
    attended = (
        jnp.einsum(
            "yjvu,uyw->vyjw",
            lower_probabilities,
            value_matrix_rows,
            preferred_element_type=jnp.float32,
        )
        .astype(jnp.bfloat16)
        .reshape(total_rows, QUERY_HEADS * HEAD_DIM)
    )
    hidden_state = inputs + matrix_product(attended, output_matrix)
    mixed_in = normalize(hidden_state, gain_second).astype(jnp.bfloat16)
    logits = matrix_product(mixed_in, router_w)
    gates = jax.nn.softmax(jnp.where(chosen, logits, -1e30), axis=-1)

    every_x = lax.all_gather(mixed_in, "expert", axis=0, tiled=True)
    out_part, row_part, act, gate_back, up_back, scores_part = run_experts(
        every_x, every_dy, every_mask, router_lanes, pieces, 512 if total_rows % 512 == 0 else 128
    )
    out_sum = lax.psum_scatter(out_part, "expert", scatter_dimension=0, tiled=True)
    row_sum = lax.psum_scatter(row_part, "expert", scatter_dimension=0, tiled=True)
    sent_scores = scores_part[:, :local_experts].reshape(peers, -1, LANES)
    gate_grad = lax.all_to_all(sent_scores, "expert", split_axis=0, concat_axis=0, tiled=True)
    gate_grad = (
        gate_grad.reshape(peers, total_rows, local_experts)
        .transpose(1, 0, 2)
        .reshape(total_rows, experts)
    )
    output = hidden_state + out_sum.astype(F32)
    upstream = cotangent.astype(jnp.float32)

    flat_dy = every_dy[:, :total_rows].reshape(peers * total_rows, model_width)
    down_grad = product_tn(act, flat_dy).astype(BF16)
    gate_grad_w = product_tn(every_x, gate_back).astype(BF16)
    up_grad_w = product_tn(every_x, up_back).astype(BF16)
    gu_grad = jnp.stack(
        [gate_grad_w.reshape(model_width, local_experts, hidden),
         up_grad_w.reshape(model_width, local_experts, hidden)], axis=2
    )
    gu_blocks = gu_grad.reshape(count, part_rows, local_experts, 2 * hidden).transpose(0, 2, 1, 3)
    down_blocks = down_grad.reshape(
        local_experts, count, hidden // count, model_width
    ).transpose(1, 0, 2, 3)
    expert_sum = scatter_sum(jnp.concatenate([gu_blocks, down_blocks], axis=2))
    expert_gate_sum = expert_sum[:, :part_rows, :hidden]
    expert_up_sum = expert_sum[:, :part_rows, hidden:]
    expert_down_sum = expert_sum[:, part_rows:, :]

    logit_grad = (
        gates * (gate_grad - jnp.sum(gates * gate_grad, axis=1, keepdims=True))
    ).astype(jnp.bfloat16)
    router_grad = product_tn(mixed_in, logit_grad)
    mixed_grad = product_transposed_right(logit_grad, router_w) + row_sum.astype(F32)
    _, second_back = jax.vjp(normalize, hidden_state, gain_second)
    state_part, gain_two_grad = second_back(mixed_grad)
    state_grad = upstream + state_part
    branch_gradient = state_grad.astype(jnp.bfloat16)
    out_grad_w = product_tn(attended, branch_gradient)
    early = sum_everywhere(
        jnp.concatenate(
            [
                out_grad_w,
                router_grad,
                gain_two_grad[:, None],
                jnp.zeros((model_width, LANES - experts - 1), F32),
            ],
            axis=1,
        )
    )
    attended_gradient = (
        product_transposed_right(branch_gradient, output_matrix)
        .astype(jnp.bfloat16)
        .reshape(total_rows, KEY_VALUE_HEADS, query_group_width, HEAD_DIM)
    )
    probability = jnp.exp(score_table() - log_total)
    prob_grad = jnp.einsum(
        "vuol,mul->uovm", attended_gradient, value_matrix_rows, preferred_element_type=jnp.float32
    )
    score_gradient = (
        probability * (prob_grad - jnp.sum(probability * prob_grad, axis=-1, keepdims=True))
    ).astype(jnp.bfloat16)
    query_grad = (
        jnp.einsum(
            "yjvu,uyw->vyjw", score_gradient, key_matrix_rows, preferred_element_type=jnp.float32
        )
        * score_scale
    )
    key_gradient = (
        jnp.einsum("cuyf,ycul->fcl", score_gradient, query_rows, preferred_element_type=jnp.float32)
        * score_scale
    )
    value_gradient = jnp.einsum(
        "cuyf,ycul->fcl", lower_probabilities, attended_gradient, preferred_element_type=jnp.float32
    )
    query_back = (
        apply_rotary(
            query_grad.reshape(total_rows, QUERY_HEADS, HEAD_DIM), cosine_table, -sine_lookup
        )
        .astype(jnp.bfloat16)
        .reshape(total_rows, QUERY_HEADS * HEAD_DIM)
    )
    key_back = (
        apply_rotary(key_gradient, cosine_table, -sine_lookup)
        .astype(jnp.bfloat16)
        .reshape(total_rows, KEY_VALUE_HEADS * HEAD_DIM)
    )
    value_backward = value_gradient.astype(jnp.bfloat16).reshape(
        total_rows, KEY_VALUE_HEADS * HEAD_DIM
    )
    all_back = jnp.concatenate([query_back, key_back, value_backward], axis=1)
    first_grad_w = product_tn(normalized_input, all_back)
    normed_grad = product_transposed_right(all_back, first_weights[:, : q_end + 2 * kv_width])
    _, first_back = jax.vjp(normalize, inputs, gain_first)
    input_part, gain_one_grad = first_back(normed_grad)
    input_grad = state_grad + input_part
    late = sum_everywhere(
        jnp.concatenate(
            [first_grad_w, gain_one_grad[:, None], jnp.zeros((model_width, LANES - 1), F32)], axis=1
        )
    )
    return (
        output.astype(jnp.bfloat16),
        input_grad.astype(jnp.bfloat16),
        late[:, q_end + 2 * kv_width],
        late[:, :q_end],
        late[:, q_end : q_end + kv_width],
        late[:, q_end + kv_width : q_end + 2 * kv_width],
        early[:, :model_width],
        early[:, model_width + experts],
        early[:, model_width : model_width + experts],
        expert_gate_sum,
        expert_up_sum,
        expert_down_sum,
    )


def solution(mesh):
    in_specs = (
        P(("expert", "shard"), None),
        P("shard"),
        P("shard", None),
        P("shard", None),
        P("shard", None),
        P("shard", None),
        P("shard"),
        P("shard", None),
        P("expert", "shard", None),
        P("expert", "shard", None),
        P("expert", "shard", None),
        P(("expert", "shard"), None),
        P(("expert", "shard"), None),
        P(("expert", "shard"), None),
    )
    out_specs = (
        P(("expert", "shard"), None),
        P(("expert", "shard"), None),
        P("shard"),
        P("shard", None),
        P("shard", None),
        P("shard", None),
        P("shard", None),
        P("shard"),
        P("shard", None),
        P("expert", "shard", None),
        P("expert", "shard", None),
        P("expert", "shard", None),
    )
    return jax.shard_map(
        per_device, mesh=mesh, in_specs=in_specs, out_specs=out_specs, check_vma=False
    )
```

```python
import functools
import math

import jax
import jax.numpy as jnp
from jax import lax
from jax.experimental import pallas as pl
from jax.experimental.pallas import tpu as pltpu
from jax.sharding import PartitionSpec as P

QUERY_HEADS = 16
KEY_VALUE_HEADS = 8
HEAD_DIM = 64
LANES = 128
VMEM_LIMIT = 58 * 1024 * 1024
CHUNKS = 2
F32 = jnp.float32
BF16 = jnp.bfloat16


def normalize(values, gain_vector):
    return (
        values * lax.rsqrt(jnp.mean(values * values, axis=-1, keepdims=True) + 1e-06) * gain_vector
    )


def apply_rotary(values, cosine_table, sine_lookup):
    half_width = values.shape[-1] // 2
    first_half = values[..., :half_width]
    second_half = values[..., half_width:]
    return jnp.concatenate(
        [
            first_half * cosine_table - second_half * sine_lookup,
            second_half * cosine_table + first_half * sine_lookup,
        ],
        axis=-1,
    )


def place_tables(lengths_row, total_rows, head_width):
    doc_ends = jnp.cumsum(lengths_row)
    token_index = jnp.arange(total_rows, dtype=jnp.int32)
    past_end = token_index[:, None] >= doc_ends[None, :]
    document = jnp.sum(past_end.astype(jnp.int32), axis=1)
    doc_start = jnp.sum(jnp.where(past_end, lengths_row[None, :], 0), axis=1)
    position = (token_index - doc_start).astype(jnp.float32)
    half_width = head_width // 2
    inverse = 10000.0 ** (-(jnp.arange(half_width, dtype=jnp.float32) * 2.0 / head_width))
    angles = position[:, None] * inverse[None, :]
    allowed = (document[:, None] == document[None, :]) & (
        token_index[None, :] <= token_index[:, None]
    )
    return (jnp.cos(angles)[:, None, :], jnp.sin(angles)[:, None, :], allowed)


def matrix_product(left_side, right_side):
    return jnp.dot(left_side, right_side, preferred_element_type=jnp.float32)


def product_tn(left_side, right_side):
    return lax.dot_general(
        left_side, right_side, (((0,), (0,)), ((), ())), preferred_element_type=jnp.float32
    )


def product_transposed_right(left_side, right_side):
    return lax.dot_general(
        left_side, right_side, (((1,), (1,)), ((), ())), preferred_element_type=jnp.float32
    )


def pick(blocks, index):
    return lax.dynamic_index_in_dim(blocks, index, 0, keepdims=False)


def gather_pieces(piece):
    count = lax.axis_size("shard")
    if count == 4:
        me = lax.axis_index("shard")
        pieces = [(piece, me)]
        for flip in (1, 2, 3):
            got = lax.ppermute(piece, "shard", [(i, i ^ flip) for i in range(4)])
            pieces.append((got, me ^ flip))
        return pieces
    every = lax.all_gather(piece, "shard", axis=0)
    return [(every[i], jnp.int32(i)) for i in range(count)]


def swap_cores(value):
    size = lax.axis_size("expert")
    return lax.ppermute(value, "expert", [(i, i ^ 1) for i in range(size)])


def gather_rows(rows):
    core = lax.axis_index("expert") % 2
    half = rows.shape[0] // 2
    mine = lax.dynamic_slice_in_dim(rows, core * half, half, 0)
    pieces = gather_pieces(mine)
    count = len(pieces)
    kept = jnp.stack([piece for piece, _ in pieces])
    other = swap_cores(kept)
    low = jnp.where(core == 0, kept, other)
    high = jnp.where(core == 0, other, kept)
    both = jnp.stack([low, high], axis=1).reshape(count, rows.shape[0], rows.shape[1])
    me = lax.axis_index("shard")
    if count == 4:
        both = jnp.concatenate([pick(both, me ^ i) for i in range(4)], axis=0)
    return both.reshape(count * rows.shape[0], rows.shape[1])


def scatter_sum(values, axis):
    count = lax.axis_size("shard")
    if count != 4:
        return lax.psum_scatter(
            values.astype(BF16), "shard", scatter_dimension=axis, tiled=True
        ).astype(F32)
    me = lax.axis_index("shard")
    size = values.shape[axis] // count
    total = lax.dynamic_slice_in_dim(values, me * size, size, axis).astype(F32)
    for flip in (1, 2, 3):
        sent = lax.dynamic_slice_in_dim(values, (me ^ flip) * size, size, axis).astype(BF16)
        got = lax.ppermute(sent, "shard", [(i, i ^ flip) for i in range(4)])
        total = total + got.astype(F32)
    return total


def sum_everywhere(grad):
    count = lax.axis_size("shard")
    size = lax.axis_size("expert")
    layers = size // 2
    place = lax.axis_index("expert")
    core, layer = place % 2, place // 2
    width = grad.shape[1]
    half = grad.shape[0] // count // 2
    blocks = grad.reshape(count, 2, half, width)
    mine = lax.dynamic_index_in_dim(blocks, core, 1, keepdims=False)
    away = lax.dynamic_index_in_dim(blocks, 1 - core, 1, keepdims=False)
    paired = mine + swap_cores(away.astype(BF16)).astype(F32)
    local = scatter_sum(paired, 0).reshape(layers, half // layers, width)
    total = pick(local, layer)
    for step in range(1, layers):
        perm = [(i, (i + 2 * step) % size) for i in range(size)]
        sent = pick(local, (layer + step) % layers).astype(BF16)
        total = total + lax.ppermute(sent, "expert", perm).astype(F32)
    total = total.astype(BF16)
    parts = jnp.zeros((layers, half // layers, width), BF16)
    parts = lax.dynamic_update_index_in_dim(parts, total, layer, 0)
    for step in range(1, layers):
        perm = [(i, (i + 2 * step) % size) for i in range(size)]
        got = lax.ppermute(total, "expert", perm)
        parts = lax.dynamic_update_index_in_dim(parts, got, (layer - step) % layers, 0)
    mine = parts.reshape(half, width)
    other = swap_cores(mine)
    low = jnp.where(core == 0, mine, other)
    high = jnp.where(core == 0, other, mine)
    return jnp.concatenate([low, high], axis=0).astype(F32)


def expert_kernel(count, place_ref, x_ref, dy_ref, mask_ref, router_ref, *refs):
    pieces = refs[:count]
    out_ref, row_ref, act_ref, gate_ref, up_ref, score_ref, gu, down, sem = refs[count:]
    local, rows, width = pieces[0].shape
    third = rows // 3
    hidden = width // 2

    @pl.when(pl.program_id(0) == 0)
    def _():
        copies = []
        for i in range(count):
            at = place_ref[i]
            copies.append(
                pltpu.make_async_copy(
                    pieces[i].at[:, pl.ds(0, 2 * third), :],
                    gu.at[:, pl.ds(pl.multiple_of(at * (2 * third), 16), 2 * third), :],
                    sem.at[2 * i],
                )
            )
            copies.append(
                pltpu.make_async_copy(
                    pieces[i].at[:, pl.ds(2 * third, third), :],
                    down.at[:, pl.ds(pl.multiple_of(at * third, 16), third), :],
                    sem.at[2 * i + 1],
                )
            )
        for copy in copies:
            copy.start()
        for copy in copies:
            copy.wait()

    x = x_ref[...]
    tile = x.shape[0]
    dy = dy_ref[...].reshape(tile, width)
    mask = mask_ref[...].reshape(tile, LANES)
    lane = lax.broadcasted_iota(jnp.int32, (tile, LANES), 1)
    logits = jnp.where(mask > 0, jnp.dot(x, router_ref[...], preferred_element_type=F32), -1e30)
    powers = jnp.exp(logits - jnp.max(logits, axis=1, keepdims=True))
    chances = powers / jnp.sum(powers, axis=1, keepdims=True)
    out = None
    row = None
    scores = jnp.zeros((tile, LANES), F32)
    for j in range(local):
        own = place_ref[count] * local + j
        gate = jnp.sum(jnp.where(lane == own, chances, 0.0), axis=1, keepdims=True)
        left = gu[j, :, :hidden]
        right = gu[j, :, hidden:]
        back = down[j]
        gate_val = jnp.dot(x, left, preferred_element_type=F32)
        up_val = jnp.dot(x, right, preferred_element_type=F32)
        inner_grad = product_transposed_right(dy, back)
        sigmoid = 0.5 + 0.5 * jnp.tanh(0.5 * gate_val)
        swish = gate_val * sigmoid
        inner = (swish * up_val).astype(BF16).astype(F32)
        score = jnp.sum(inner * inner_grad, axis=1, keepdims=True)
        scores = jnp.where(lane == j, score, scores)
        act = (gate * inner).astype(BF16)
        scaled = gate * inner_grad
        gate_back = (scaled * up_val * (sigmoid + swish * (1.0 - sigmoid))).astype(BF16)
        up_back = (scaled * swish).astype(BF16)
        act_ref[:, j * hidden : (j + 1) * hidden] = act
        gate_ref[:, j * hidden : (j + 1) * hidden] = gate_back
        up_ref[:, j * hidden : (j + 1) * hidden] = up_back
        part = jnp.dot(act, back, preferred_element_type=F32)
        out = part if out is None else out + part
        part = product_transposed_right(gate_back, left) + product_transposed_right(up_back, right)
        row = part if row is None else row + part
    out_ref[...] = out.astype(BF16)
    row_ref[...] = row.astype(BF16)
    score_ref[...] = scores


def run_experts(every_x, every_dy, mask, router, pieces, chunk):
    count = len(pieces)
    total, width = every_x.shape
    local, rows, _ = pieces[0][0].shape
    third = rows // 3
    peers = every_dy.shape[0]
    rows_each = total // peers
    group = 2
    tile = group * rows_each
    place = jnp.stack([index for _, index in pieces] + [lax.axis_index("expert")]).astype(jnp.int32)
    block = pl.BlockSpec((tile, width), lambda i, p: (i, 0))
    thin = pl.BlockSpec((tile, LANES), lambda i, p: (i, 0))
    return pl.pallas_call(
        functools.partial(expert_kernel, count),
        grid_spec=pltpu.PrefetchScalarGridSpec(
            num_scalar_prefetch=1,
            grid=(peers // group,),
            in_specs=[
                block,
                pl.BlockSpec((group, rows_each, width), lambda i, p: (i, chunk, 0)),
                pl.BlockSpec((group, rows_each, LANES), lambda i, p: (i, chunk, 0)),
                pl.BlockSpec((width, LANES), lambda i, p: (0, 0)),
            ]
            + [pl.BlockSpec(memory_space=pl.ANY)] * count,
            out_specs=[block, block, block, block, block, thin],
            scratch_shapes=[
                pltpu.VMEM((local, 2 * third * count, width), BF16),
                pltpu.VMEM((local, third * count, width), BF16),
                pltpu.SemaphoreType.DMA((2 * count,)),
            ],
        ),
        out_shape=[jax.ShapeDtypeStruct((total, width), BF16)] * 5
        + [jax.ShapeDtypeStruct((total, LANES), F32)],
        compiler_params=pltpu.CompilerParams(vmem_limit_bytes=VMEM_LIMIT),
        cost_estimate=pl.CostEstimate(
            flops=2 * total * width * width * 6, bytes_accessed=total * width * 14, transcendentals=0
        ),
        name="experts",
    )(place, every_x, every_dy, mask, router, *[piece for piece, _ in pieces])


def columns_kernel(chunks, local, *refs):
    xs, gates, ups = refs[:chunks], refs[chunks : 2 * chunks], refs[2 * chunks : 3 * chunks]
    out_ref = refs[3 * chunks]
    hidden = out_ref.shape[2] // 2
    for j in range(local):
        for side, values in ((0, gates), (1, ups)):
            total = None
            for x_ref, value_ref in zip(xs, values):
                part = product_tn(x_ref[...], value_ref[:, j * hidden : (j + 1) * hidden])
                total = part if total is None else total + part
            out_ref[j, :, side * hidden : (side + 1) * hidden] = total.astype(BF16)


def gate_up_gradient(xs, gates, ups, local):
    rows, width = xs[0].shape
    chunks = len(xs)
    piece = width // 4
    whole = pl.BlockSpec((rows, width), lambda i: (0, 0), pipeline_mode=pl.Buffered(1))
    return pl.pallas_call(
        functools.partial(columns_kernel, chunks, local),
        grid=(4,),
        in_specs=[pl.BlockSpec((rows, piece), lambda i: (0, i))] * chunks + [whole] * (2 * chunks),
        out_specs=pl.BlockSpec((local, piece, width), lambda i: (0, i, 0)),
        out_shape=jax.ShapeDtypeStruct((local, width, width), BF16),
        compiler_params=pltpu.CompilerParams(vmem_limit_bytes=VMEM_LIMIT),
        cost_estimate=pl.CostEstimate(
            flops=4 * chunks * rows * width * width, bytes_accessed=chunks * rows * width * 6, transcendentals=0
        ),
        name="gate_up_gradient",
    )(*xs, *gates, *ups)


def down_kernel(chunks, *refs):
    total = None
    for act_ref, dy_ref in zip(refs[:chunks], refs[chunks : 2 * chunks]):
        dy = dy_ref[...].reshape(act_ref.shape[0], dy_ref.shape[2])
        part = product_tn(act_ref[...], dy)
        total = part if total is None else total + part
    refs[2 * chunks][...] = total.astype(BF16)


def down_gradient(acts, every_dy, local):
    rows, width = acts[0].shape
    chunks = len(acts)
    peers = every_dy.shape[0]
    piece = width // 4

    def spec(chunk):
        return pl.BlockSpec(
            (peers, rows // peers, width),
            lambda i: (0, chunk, 0),
            pipeline_mode=pl.Buffered(1),
        )

    return pl.pallas_call(
        functools.partial(down_kernel, chunks),
        grid=(4,),
        in_specs=[pl.BlockSpec((rows, piece), lambda i: (0, i))] * chunks
        + [spec(chunk) for chunk in range(chunks)],
        out_specs=pl.BlockSpec((piece, width), lambda i: (i, 0)),
        out_shape=jax.ShapeDtypeStruct((width, width), BF16),
        compiler_params=pltpu.CompilerParams(vmem_limit_bytes=VMEM_LIMIT),
        cost_estimate=pl.CostEstimate(
            flops=2 * chunks * rows * width * width, bytes_accessed=chunks * rows * width * 4, transcendentals=0
        ),
        name="down_gradient",
    )(*acts, *([every_dy] * chunks)).reshape(local, width // local, width)


def per_device(
    tokens,
    gain_attn,
    w_query,
    key_weight,
    value_weight,
    w_out,
    gain_mix,
    router,
    w_gate,
    w_up,
    w_down,
    routes,
    lengths,
    cotangent,
):
    total_rows, model_width = tokens.shape
    query_group_width = QUERY_HEADS // KEY_VALUE_HEADS
    experts = router.shape[1]
    local_experts, _, hidden = w_gate.shape
    peers = lax.axis_size("expert")
    count = lax.axis_size("shard")
    part_rows = w_query.shape[0]
    kv_width = key_weight.shape[1]
    score_scale = 1.0 / math.sqrt(HEAD_DIM)

    small = jnp.concatenate(
        [
            router,
            gain_attn[:, None],
            gain_mix[:, None],
            jnp.zeros((part_rows, LANES - experts - 2), BF16),
        ],
        axis=1,
    )
    first_weights = gather_rows(
        jnp.concatenate([w_query, key_weight, value_weight, small], axis=1)
    )
    q_end = w_query.shape[1]
    query_w = first_weights[:, :q_end]
    key_matrix = first_weights[:, q_end : q_end + kv_width]
    value_matrix = first_weights[:, q_end + kv_width : q_end + 2 * kv_width]
    small_all = first_weights[:, q_end + 2 * kv_width :]
    gain_first = small_all[:, experts].astype(F32)
    gain_second = small_all[:, experts + 1].astype(F32)
    router_lanes = jnp.where(jnp.arange(LANES)[None, :] < experts, small_all, jnp.zeros((), BF16))
    router_w = small_all[:, :experts]
    output_matrix = gather_rows(w_out)
    packed = jnp.concatenate([jnp.concatenate([w_gate, w_up], axis=2), w_down], axis=1)
    pieces = gather_pieces(packed)

    expert_ids = jnp.arange(experts, dtype=jnp.int32)
    chosen = jnp.any(routes[:, :, None] == expert_ids[None, None, :], axis=1)
    mask_rows = total_rows * experts // model_width
    mask_space = -(-mask_rows // 16) * 16
    every_dy = lax.all_gather(
        jnp.concatenate(
            [
                cotangent,
                jnp.pad(
                    chosen.astype(BF16).reshape(mask_rows, model_width),
                    ((0, mask_space - mask_rows), (0, 0)),
                ),
            ],
            axis=0,
        ),
        "expert",
        axis=0,
    )
    every_mask = jnp.pad(
        every_dy[:, total_rows : total_rows + mask_rows].reshape(peers, total_rows, experts),
        ((0, 0), (0, 0), (0, LANES - experts)),
    )

    inputs = tokens.astype(jnp.float32)
    normalized_input = normalize(inputs, gain_first).astype(jnp.bfloat16)
    cosine_table, sine_lookup, allowed = place_tables(lengths[0], total_rows, HEAD_DIM)
    query_raw = matrix_product(normalized_input, query_w).reshape(total_rows, QUERY_HEADS, HEAD_DIM)
    unrotated_keys = matrix_product(normalized_input, key_matrix).reshape(
        total_rows, KEY_VALUE_HEADS, HEAD_DIM
    )
    query_rows = (
        apply_rotary(query_raw, cosine_table, sine_lookup)
        .astype(jnp.bfloat16)
        .reshape(total_rows, KEY_VALUE_HEADS, query_group_width, HEAD_DIM)
    )
    key_matrix_rows = apply_rotary(unrotated_keys, cosine_table, sine_lookup).astype(jnp.bfloat16)
    value_matrix_rows = (
        matrix_product(normalized_input, value_matrix)
        .astype(jnp.bfloat16)
        .reshape(total_rows, KEY_VALUE_HEADS, HEAD_DIM)
    )

    def score_table():
        raw_scores = (
            jnp.einsum(
                "vuol,mul->uovm", query_rows, key_matrix_rows, preferred_element_type=jnp.float32
            )
            * score_scale
        )
        return jnp.where(allowed[None, None], raw_scores, -1e30)

    scores = score_table()
    top_score = jnp.max(scores, axis=-1, keepdims=True)
    weights = jnp.exp(scores - top_score)
    sum_weights = jnp.sum(weights, axis=-1, keepdims=True)
    probability = weights / sum_weights
    log_total = top_score + jnp.log(sum_weights)
    lower_probabilities = probability.astype(jnp.bfloat16)
    attended = (
        jnp.einsum(
            "yjvu,uyw->vyjw",
            lower_probabilities,
            value_matrix_rows,
            preferred_element_type=jnp.float32,
        )
        .astype(jnp.bfloat16)
        .reshape(total_rows, QUERY_HEADS * HEAD_DIM)
    )
    hidden_state = inputs + matrix_product(attended, output_matrix)
    mixed_in = normalize(hidden_state, gain_second).astype(jnp.bfloat16)
    logits = matrix_product(mixed_in, router_w)
    gates = jax.nn.softmax(jnp.where(chosen, logits, -1e30), axis=-1)

    part = total_rows // CHUNKS
    every_x, out_part, row_part, act, gate_back, up_back, scores_part = [], [], [], [], [], [], []
    for chunk in range(CHUNKS):
        gathered = lax.all_gather(
            mixed_in[chunk * part : (chunk + 1) * part], "expert", axis=0, tiled=True
        )
        results = run_experts(gathered, every_dy, every_mask, router_lanes, pieces, chunk)
        every_x.append(gathered)
        for kept, result in zip((out_part, row_part, act, gate_back, up_back, scores_part), results):
            kept.append(result)
    row_sum = [
        lax.psum_scatter(rows, "expert", scatter_dimension=0, tiled=True) for rows in row_part
    ]
    sent_scores = jnp.concatenate(
        [
            values[:, :local_experts].reshape(peers, -1, LANES)
            for values in scores_part
        ],
        axis=1,
    )
    gate_grad = lax.all_to_all(sent_scores, "expert", split_axis=0, concat_axis=0, tiled=True)
    gate_grad = (
        gate_grad.reshape(peers, total_rows, local_experts)
        .transpose(1, 0, 2)
        .reshape(total_rows, experts)
    )
    *out_part, row_last = lax.optimization_barrier((*out_part, row_sum[-1]))
    row_sum = jnp.concatenate([*row_sum[:-1], row_last], axis=0)
    out_sum = jnp.concatenate(
        [lax.psum_scatter(rows, "expert", scatter_dimension=0, tiled=True) for rows in out_part],
        axis=0,
    )
    output = hidden_state + out_sum.astype(F32)
    upstream = cotangent.astype(jnp.float32)

    expert_down_sum = scatter_sum(down_gradient(act, every_dy, local_experts), 1)
    gu_sum = scatter_sum(gate_up_gradient(every_x, gate_back, up_back, local_experts), 1)
    expert_gate_sum = gu_sum[:, :, :hidden]
    expert_up_sum = gu_sum[:, :, hidden:]

    logit_grad = (
        gates * (gate_grad - jnp.sum(gates * gate_grad, axis=1, keepdims=True))
    ).astype(jnp.bfloat16)
    router_grad = product_tn(mixed_in, logit_grad)
    mixed_grad = product_transposed_right(logit_grad, router_w) + row_sum.astype(F32)
    _, second_back = jax.vjp(normalize, hidden_state, gain_second)
    state_part, gain_two_grad = second_back(mixed_grad)
    state_grad = upstream + state_part
    branch_gradient = state_grad.astype(jnp.bfloat16)
    out_grad_w = product_tn(attended, branch_gradient)
    early = sum_everywhere(
        jnp.concatenate(
            [
                out_grad_w,
                router_grad,
                gain_two_grad[:, None],
                jnp.zeros((model_width, LANES - experts - 1), F32),
            ],
            axis=1,
        )
    )
    attended_gradient = (
        product_transposed_right(branch_gradient, output_matrix)
        .astype(jnp.bfloat16)
        .reshape(total_rows, KEY_VALUE_HEADS, query_group_width, HEAD_DIM)
    )
    probability = jnp.exp(score_table() - log_total)
    prob_grad = jnp.einsum(
        "vuol,mul->uovm", attended_gradient, value_matrix_rows, preferred_element_type=jnp.float32
    )
    score_gradient = (
        probability * (prob_grad - jnp.sum(probability * prob_grad, axis=-1, keepdims=True))
    ).astype(jnp.bfloat16)
    query_grad = (
        jnp.einsum(
            "yjvu,uyw->vyjw", score_gradient, key_matrix_rows, preferred_element_type=jnp.float32
        )
        * score_scale
    )
    key_gradient = (
        jnp.einsum("cuyf,ycul->fcl", score_gradient, query_rows, preferred_element_type=jnp.float32)
        * score_scale
    )
    value_gradient = jnp.einsum(
        "cuyf,ycul->fcl", lower_probabilities, attended_gradient, preferred_element_type=jnp.float32
    )
    query_back = (
        apply_rotary(
            query_grad.reshape(total_rows, QUERY_HEADS, HEAD_DIM), cosine_table, -sine_lookup
        )
        .astype(jnp.bfloat16)
        .reshape(total_rows, QUERY_HEADS * HEAD_DIM)
    )
    key_back = (
        apply_rotary(key_gradient, cosine_table, -sine_lookup)
        .astype(jnp.bfloat16)
        .reshape(total_rows, KEY_VALUE_HEADS * HEAD_DIM)
    )
    value_backward = value_gradient.astype(jnp.bfloat16).reshape(
        total_rows, KEY_VALUE_HEADS * HEAD_DIM
    )
    all_back = jnp.concatenate([query_back, key_back, value_backward], axis=1)
    first_grad_w = product_tn(normalized_input, all_back)
    normed_grad = product_transposed_right(all_back, first_weights[:, : q_end + 2 * kv_width])
    _, first_back = jax.vjp(normalize, inputs, gain_first)
    input_part, gain_one_grad = first_back(normed_grad)
    input_grad = state_grad + input_part
    late = sum_everywhere(
        jnp.concatenate(
            [first_grad_w, gain_one_grad[:, None], jnp.zeros((model_width, LANES - 1), F32)], axis=1
        )
    )
    return (
        output.astype(jnp.bfloat16),
        input_grad.astype(jnp.bfloat16),
        late[:, q_end + 2 * kv_width],
        late[:, :q_end],
        late[:, q_end : q_end + kv_width],
        late[:, q_end + kv_width : q_end + 2 * kv_width],
        early[:, :model_width],
        early[:, model_width + experts],
        early[:, model_width : model_width + experts],
        expert_gate_sum,
        expert_up_sum,
        expert_down_sum,
    )


def solution(mesh):
    in_specs = (
        P(("expert", "shard"), None),
        P("shard"),
        P("shard", None),
        P("shard", None),
        P("shard", None),
        P("shard", None),
        P("shard"),
        P("shard", None),
        P("expert", "shard", None),
        P("expert", "shard", None),
        P("expert", "shard", None),
        P(("expert", "shard"), None),
        P(("expert", "shard"), None),
        P(("expert", "shard"), None),
    )
    out_specs = (
        P(("expert", "shard"), None),
        P(("expert", "shard"), None),
        P("shard"),
        P("shard", None),
        P("shard", None),
        P("shard", None),
        P("shard", None),
        P("shard"),
        P("shard", None),
        P("expert", "shard", None),
        P("expert", "shard", None),
        P("expert", "shard", None),
    )
    return jax.shard_map(
        per_device, mesh=mesh, in_specs=in_specs, out_specs=out_specs, check_vma=False
    )
```

```python
import functools
import math

import jax
import jax.numpy as jnp
from jax import lax
from jax.experimental import pallas as pl
from jax.experimental.pallas import tpu as pltpu
from jax.sharding import PartitionSpec as P

QUERY_HEADS = 16
KEY_VALUE_HEADS = 8
HEAD_DIM = 64
LANES = 128
VMEM_LIMIT = 58 * 1024 * 1024
CHUNKS = 2
SMALL_COST = pl.CostEstimate(flops=0, bytes_accessed=0, transcendentals=0)
F32 = jnp.float32
BF16 = jnp.bfloat16


def matrix_product(left_side, right_side):
    return jnp.dot(left_side, right_side, preferred_element_type=jnp.float32)


def product_tn(left_side, right_side):
    return lax.dot_general(
        left_side, right_side, (((0,), (0,)), ((), ())), preferred_element_type=jnp.float32
    )


def product_transposed_right(left_side, right_side):
    return lax.dot_general(
        left_side, right_side, (((1,), (1,)), ((), ())), preferred_element_type=jnp.float32
    )


def pick(blocks, index):
    return lax.dynamic_index_in_dim(blocks, index, 0, keepdims=False)


def gather_pieces(piece):
    count = lax.axis_size("shard")
    if count == 4:
        me = lax.axis_index("shard")
        pieces = [(piece, me)]
        for flip in (1, 2, 3):
            got = lax.ppermute(piece, "shard", [(i, i ^ flip) for i in range(4)])
            pieces.append((got, me ^ flip))
        return pieces
    every = lax.all_gather(piece, "shard", axis=0)
    return [(every[i], jnp.int32(i)) for i in range(count)]


def swap_cores(value):
    size = lax.axis_size("expert")
    return lax.ppermute(value, "expert", [(i, i ^ 1) for i in range(size)])


def fetch_rows(rows):
    count = lax.axis_size("shard")
    size = rows.shape[0]
    if count != 4:
        return [lax.all_gather(rows, "shard", axis=0, tiled=True)], jnp.zeros((1,), jnp.int32)
    me = lax.axis_index("shard")
    core = lax.axis_index("expert") % 2
    half = size // 2
    mine = lax.dynamic_slice_in_dim(rows, core * half, half, 0)
    pieces, places = [rows], [me * size]
    for flip in (1, 2, 3):
        got = lax.ppermute(mine, "shard", [(i, i ^ flip) for i in range(4)])
        first = (me ^ flip) * size
        pieces += [got, swap_cores(got)]
        places += [first + core * half, first + (1 - core) * half]
    return pieces, jnp.stack(places).astype(jnp.int32)


def scatter_sum(values, axis, after=None):
    count = lax.axis_size("shard")
    if count != 4:
        return lax.psum_scatter(
            values.astype(BF16), "shard", scatter_dimension=axis, tiled=True
        ).astype(F32)
    me = lax.axis_index("shard")
    size = values.shape[axis] // count
    own = lax.dynamic_slice_in_dim(values, me * size, size, axis)
    if after is not None:
        own, _ = lax.optimization_barrier((own, after))
    total = own.astype(F32)
    for flip in (1, 2, 3):
        sent = lax.dynamic_slice_in_dim(values, (me ^ flip) * size, size, axis).astype(BF16)
        got = lax.ppermute(sent, "shard", [(i, i ^ flip) for i in range(4)])
        total = total + got.astype(F32)
    return total


def sum_everywhere(grad):
    count = lax.axis_size("shard")
    size = lax.axis_size("expert")
    layers = size // 2
    place = lax.axis_index("expert")
    core, layer = place % 2, place // 2
    width = grad.shape[1]
    half = grad.shape[0] // count // 2
    blocks = grad.reshape(count, 2, half, width)
    mine = lax.dynamic_index_in_dim(blocks, core, 1, keepdims=False)
    away = lax.dynamic_index_in_dim(blocks, 1 - core, 1, keepdims=False)
    paired = mine.astype(F32) + swap_cores(away).astype(F32)
    local = scatter_sum(paired, 0).reshape(layers, half // layers, width)
    total = pick(local, layer)
    for step in range(1, layers):
        perm = [(i, (i + 2 * step) % size) for i in range(size)]
        sent = pick(local, (layer + step) % layers).astype(BF16)
        total = total + lax.ppermute(sent, "expert", perm).astype(F32)
    total = total.astype(BF16)
    parts = jnp.zeros((layers, half // layers, width), BF16)
    parts = lax.dynamic_update_index_in_dim(parts, total, layer, 0)
    for step in range(1, layers):
        perm = [(i, (i + 2 * step) % size) for i in range(size)]
        got = lax.ppermute(total, "expert", perm)
        parts = lax.dynamic_update_index_in_dim(parts, got, (layer - step) % layers, 0)
    mine = parts.reshape(half, width)
    other = swap_cores(mine)
    low = jnp.where(core == 0, mine, other)
    high = jnp.where(core == 0, other, mine)
    return jnp.concatenate([low, high], axis=0).astype(F32)


def expert_kernel(count, place_ref, x_ref, dy_ref, mask_ref, router_ref, *refs):
    pieces = refs[:count]
    out_ref, row_ref, act_ref, gate_ref, up_ref, score_ref, gu, down, sem = refs[count:]
    local, rows, width = pieces[0].shape
    third = rows // 3
    hidden = width // 2

    @pl.when(pl.program_id(0) == 0)
    def _():
        copies = []
        for i in range(count):
            at = place_ref[i]
            copies.append(
                pltpu.make_async_copy(
                    pieces[i].at[:, pl.ds(0, 2 * third), :],
                    gu.at[:, pl.ds(pl.multiple_of(at * (2 * third), 16), 2 * third), :],
                    sem.at[2 * i],
                )
            )
            copies.append(
                pltpu.make_async_copy(
                    pieces[i].at[:, pl.ds(2 * third, third), :],
                    down.at[:, pl.ds(pl.multiple_of(at * third, 16), third), :],
                    sem.at[2 * i + 1],
                )
            )
        for copy in copies:
            copy.start()
        for copy in copies:
            copy.wait()

    x = x_ref[...]
    tile = x.shape[0]
    dy = dy_ref[...].reshape(tile, width)
    mask = mask_ref[...].reshape(tile, LANES)
    lane = lax.broadcasted_iota(jnp.int32, (tile, LANES), 1)
    logits = jnp.where(mask > 0, jnp.dot(x, router_ref[...], preferred_element_type=F32), -1e30)
    powers = jnp.exp(logits - jnp.max(logits, axis=1, keepdims=True))
    chances = powers / jnp.sum(powers, axis=1, keepdims=True)
    out = None
    row = None
    scores = jnp.zeros((tile, LANES), F32)
    for j in range(local):
        own = place_ref[count] * local + j
        gate = jnp.sum(jnp.where(lane == own, chances, 0.0), axis=1, keepdims=True)
        left = gu[j, :, :hidden]
        right = gu[j, :, hidden:]
        back = down[j]
        gate_val = jnp.dot(x, left, preferred_element_type=F32)
        up_val = jnp.dot(x, right, preferred_element_type=F32)
        inner_grad = product_transposed_right(dy, back)
        sigmoid = 0.5 + 0.5 * jnp.tanh(0.5 * gate_val)
        swish = gate_val * sigmoid
        inner = (swish * up_val).astype(BF16).astype(F32)
        score = jnp.sum(inner * inner_grad, axis=1, keepdims=True)
        scores = jnp.where(lane == j, score, scores)
        act = (gate * inner).astype(BF16)
        scaled = gate * inner_grad
        gate_back = (scaled * up_val * (sigmoid + swish * (1.0 - sigmoid))).astype(BF16)
        up_back = (scaled * swish).astype(BF16)
        act_ref[:, j * hidden : (j + 1) * hidden] = act
        gate_ref[:, j * hidden : (j + 1) * hidden] = gate_back
        up_ref[:, j * hidden : (j + 1) * hidden] = up_back
        part = jnp.dot(act, back, preferred_element_type=F32)
        out = part if out is None else out + part
        part = product_transposed_right(gate_back, left) + product_transposed_right(up_back, right)
        row = part if row is None else row + part
    out_ref[...] = out.astype(BF16)
    row_ref[...] = row.astype(BF16)
    score_ref[...] = scores


def run_experts(every_x, every_dy, mask, router, pieces, chunk):
    count = len(pieces)
    total, width = every_x.shape
    local, rows, _ = pieces[0][0].shape
    third = rows // 3
    peers = every_dy.shape[0]
    rows_each = total // peers
    group = 2
    tile = group * rows_each
    place = jnp.stack([index for _, index in pieces] + [lax.axis_index("expert")]).astype(jnp.int32)
    block = pl.BlockSpec((tile, width), lambda i, p: (i, 0))
    thin = pl.BlockSpec((tile, LANES), lambda i, p: (i, 0))
    return pl.pallas_call(
        functools.partial(expert_kernel, count),
        grid_spec=pltpu.PrefetchScalarGridSpec(
            num_scalar_prefetch=1,
            grid=(peers // group,),
            in_specs=[
                block,
                pl.BlockSpec((group, rows_each, width), lambda i, p: (i, chunk, 0)),
                pl.BlockSpec((group, rows_each, LANES), lambda i, p: (i, chunk, 0)),
                pl.BlockSpec((width, LANES), lambda i, p: (0, 0)),
            ]
            + [pl.BlockSpec(memory_space=pl.ANY)] * count,
            out_specs=[block, block, block, block, block, thin],
            scratch_shapes=[
                pltpu.VMEM((local, 2 * third * count, width), BF16),
                pltpu.VMEM((local, third * count, width), BF16),
                pltpu.SemaphoreType.DMA((2 * count,)),
            ],
        ),
        out_shape=[jax.ShapeDtypeStruct((total, width), BF16)] * 5
        + [jax.ShapeDtypeStruct((total, LANES), F32)],
        compiler_params=pltpu.CompilerParams(vmem_limit_bytes=VMEM_LIMIT),
        cost_estimate=pl.CostEstimate(
            flops=2 * total * width * width * 6, bytes_accessed=total * width * 14, transcendentals=0
        ),
        name="experts",
    )(place, every_x, every_dy, mask, router, *[piece for piece, _ in pieces])


def columns_kernel(chunks, local, *refs):
    xs, gates, ups = refs[:chunks], refs[chunks : 2 * chunks], refs[2 * chunks : 3 * chunks]
    out_ref = refs[3 * chunks]
    hidden = out_ref.shape[2] // 2
    for j in range(local):
        for side, values in ((0, gates), (1, ups)):
            total = None
            for x_ref, value_ref in zip(xs, values):
                part = product_tn(x_ref[...], value_ref[:, j * hidden : (j + 1) * hidden])
                total = part if total is None else total + part
            out_ref[j, :, side * hidden : (side + 1) * hidden] = total.astype(BF16)


def gate_up_gradient(xs, gates, ups, local):
    rows, width = xs[0].shape
    chunks = len(xs)
    piece = width // 4
    whole = pl.BlockSpec((rows, width), lambda i: (0, 0), pipeline_mode=pl.Buffered(1))
    return pl.pallas_call(
        functools.partial(columns_kernel, chunks, local),
        grid=(4,),
        in_specs=[pl.BlockSpec((rows, piece), lambda i: (0, i))] * chunks + [whole] * (2 * chunks),
        out_specs=pl.BlockSpec((local, piece, width), lambda i: (0, i, 0)),
        out_shape=jax.ShapeDtypeStruct((local, width, width), BF16),
        compiler_params=pltpu.CompilerParams(vmem_limit_bytes=VMEM_LIMIT),
        cost_estimate=pl.CostEstimate(
            flops=4 * chunks * rows * width * width, bytes_accessed=chunks * rows * width * 6, transcendentals=0
        ),
        name="gate_up_gradient",
    )(*xs, *gates, *ups)


def down_kernel(chunks, *refs):
    total = None
    for act_ref, dy_ref in zip(refs[:chunks], refs[chunks : 2 * chunks]):
        dy = dy_ref[...].reshape(act_ref.shape[0], dy_ref.shape[2])
        part = product_tn(act_ref[...], dy)
        total = part if total is None else total + part
    refs[2 * chunks][...] = total.astype(BF16)


def down_gradient(acts, every_dy, local):
    rows, width = acts[0].shape
    chunks = len(acts)
    peers = every_dy.shape[0]
    piece = width // 4

    def spec(chunk):
        return pl.BlockSpec(
            (peers, rows // peers, width),
            lambda i: (0, chunk, 0),
            pipeline_mode=pl.Buffered(1),
        )

    return pl.pallas_call(
        functools.partial(down_kernel, chunks),
        grid=(4,),
        in_specs=[pl.BlockSpec((rows, piece), lambda i: (0, i))] * chunks
        + [spec(chunk) for chunk in range(chunks)],
        out_specs=pl.BlockSpec((piece, width), lambda i: (i, 0)),
        out_shape=jax.ShapeDtypeStruct((width, width), BF16),
        compiler_params=pltpu.CompilerParams(vmem_limit_bytes=VMEM_LIMIT),
        cost_estimate=pl.CostEstimate(
            flops=2 * chunks * rows * width * width, bytes_accessed=chunks * rows * width * 4, transcendentals=0
        ),
        name="down_gradient",
    )(*acts, *([every_dy] * chunks)).reshape(local, width // local, width)


def row_copies(place_ref, pieces, target, sem):
    copies = []
    for i, piece in enumerate(pieces):
        rows = piece.shape[0]
        first = pl.multiple_of(place_ref[i], 16)
        copies.append(
            pltpu.make_async_copy(piece, target.at[pl.ds(first, rows), :], sem.at[i])
        )
    for copy in copies:
        copy.start()
    return copies


def scale_of(values):
    return lax.rsqrt(jnp.mean(values * values, axis=-1, keepdims=True) + 1e-06)


def rotate(values, cosine, sine):
    lane = lax.broadcasted_iota(jnp.int32, values.shape, 1) % HEAD_DIM
    half = HEAD_DIM // 2
    turned = jnp.where(
        lane < half, pltpu.roll(values, LANES - half, 1), pltpu.roll(values, half, 1)
    )
    return values * cosine + turned * sine


def project_kernel(count, experts, place_ref, x_ref, cos_ref, sin_ref, *refs):
    pieces = refs[:count]
    normed_ref, q_ref, k_ref, v_ref, gains_ref, router_ref, weight, sem = refs[count:]
    copies = row_copies(place_ref, pieces, weight, sem)
    x = x_ref[...].astype(F32)
    scaled = x * scale_of(x)
    cosine, sine = cos_ref[...], sin_ref[...]
    for copy in copies:
        copy.wait()
    q_width, kv_width = q_ref.shape[1], k_ref.shape[1]
    small = weight[:, q_width + 2 * kv_width :]
    lane = lax.broadcasted_iota(jnp.int32, small.shape, 1)
    router_ref[...] = jnp.where(lane < experts, small.astype(F32), 0.0).astype(BF16)
    turned = small.astype(F32).T
    gains_ref[...] = jnp.concatenate(
        [turned[experts : experts + 2], jnp.zeros((6, turned.shape[1]), F32)], axis=0
    )
    normed = (scaled * turned[experts : experts + 1]).astype(BF16)
    normed_ref[...] = normed
    for first in range(0, q_width, 256):
        values = jnp.dot(normed, weight[:, first : first + 256], preferred_element_type=F32)
        for part in (0, LANES):
            q_ref[:, first + part : first + part + LANES] = rotate(
                values[:, part : part + LANES], cosine, sine
            ).astype(BF16)
    for first in range(0, kv_width, 256):
        at = q_width + first
        values = jnp.dot(normed, weight[:, at : at + 256], preferred_element_type=F32)
        for part in (0, LANES):
            k_ref[:, first + part : first + part + LANES] = rotate(
                values[:, part : part + LANES], cosine, sine
            ).astype(BF16)
    at = q_width + kv_width
    v_ref[...] = jnp.dot(
        normed, weight[:, at : at + kv_width], preferred_element_type=F32
    ).astype(BF16)


def simple_call(kernel, name, prefetch, inputs, pieces, outputs, scratch, cost=None):
    def whole(shape):
        return pl.BlockSpec(shape, lambda i, p: (0,) * len(shape))

    return pl.pallas_call(
        kernel,
        grid_spec=pltpu.PrefetchScalarGridSpec(
            num_scalar_prefetch=1,
            grid=(1,),
            in_specs=[whole(value.shape) for value in inputs]
            + [pl.BlockSpec(memory_space=pl.ANY)] * len(pieces),
            out_specs=[whole(shape) for shape, _ in outputs],
            scratch_shapes=scratch,
        ),
        out_shape=[jax.ShapeDtypeStruct(shape, kind) for shape, kind in outputs],
        compiler_params=pltpu.CompilerParams(vmem_limit_bytes=VMEM_LIMIT),
        cost_estimate=cost,
        name=name,
    )(prefetch, *inputs, *pieces)


def key_window(tile, size, rows):
    low = max(0, tile * size - (rows // 2 - 1)) // size * size
    return low, (tile + 1) * size


def tile_mask(start_ref, low, high, first, size):
    shape = (high - low, size)
    key = lax.broadcasted_iota(jnp.int32, shape, 0) + low
    query = lax.broadcasted_iota(jnp.int32, shape, 1) + first
    seen = (key >= start_ref[:, first : first + size]) & (key <= query)
    return jnp.concatenate([seen, seen], axis=1)


def two_heads(values):
    return jnp.concatenate([values[:, :HEAD_DIM], values[:, HEAD_DIM:]], axis=0)


def untwo(values):
    size = values.shape[1] // 2
    return jnp.concatenate([values[:, :size], values[:, size:]], axis=0).T


def attend_kernel(start_ref, q_ref, k_ref, v_ref, out_ref, log_ref):
    rows = q_ref.shape[0]
    size = LANES
    scale = 1.0 / math.sqrt(HEAD_DIM)
    logs = [[], []]
    for tile in range(rows // size):
        low, high = key_window(tile, size, rows)
        first = tile * size
        seen = tile_mask(start_ref, low, high, first, size)
        for pair in range(2):
            q = two_heads(q_ref[first : first + size, pair * LANES : (pair + 1) * LANES])
            q = (q.astype(F32) * scale).astype(BF16)
            at = pair * HEAD_DIM
            scores = product_transposed_right(k_ref[low:high, at : at + HEAD_DIM], q)
            scores = jnp.where(seen, scores, -1e30)
            top = jnp.max(scores, axis=0, keepdims=True)
            powers = jnp.exp(scores - top)
            total = jnp.sum(powers, axis=0, keepdims=True)
            low_chances = (powers * (1.0 / total)).astype(BF16)
            mixed = product_tn(v_ref[low:high, at : at + HEAD_DIM], low_chances)
            out_ref[first : first + size, pair * LANES : (pair + 1) * LANES] = untwo(mixed).astype(
                BF16
            )
            logs[pair].append(top + jnp.log(total))
    lines = []
    for pair in range(2):
        for head in range(2):
            lines.append(
                jnp.concatenate([v[:, head * size : (head + 1) * size] for v in logs[pair]], axis=1)
            )
    log_ref[...] = jnp.concatenate(lines + [jnp.zeros((4, rows), F32)], axis=0)


def attend_back_kernel(
    start_ref, q_ref, k_ref, v_ref, grad_ref, log_ref, cos_ref, sin_ref, qb_ref, kb_ref, vb_ref
):
    rows = q_ref.shape[0]
    size = LANES
    tiles = rows // size
    scale = 1.0 / math.sqrt(HEAD_DIM)
    key_sums = [[None] * tiles, [None] * tiles]
    value_sums = [[None] * tiles, [None] * tiles]

    def add(sums, low, part):
        for i in range(part.shape[0] // size):
            piece = part[i * size : (i + 1) * size]
            at = low // size + i
            sums[at] = piece if sums[at] is None else sums[at] + piece

    for tile in range(tiles):
        low, high = key_window(tile, size, rows)
        first = tile * size
        seen = tile_mask(start_ref, low, high, first, size)
        cosine, sine = cos_ref[first : first + size], sin_ref[first : first + size]
        for pair in range(2):
            lanes = slice(pair * LANES, (pair + 1) * LANES)
            q = two_heads(q_ref[first : first + size, lanes])
            q = (q.astype(F32) * scale).astype(BF16)
            grad = two_heads(grad_ref[first : first + size, lanes])
            at = pair * HEAD_DIM
            keys = k_ref[low:high, at : at + HEAD_DIM]
            scores = jnp.where(seen, product_transposed_right(keys, q), -1e30)
            log_total = jnp.concatenate(
                [
                    log_ref[2 * pair : 2 * pair + 1, first : first + size],
                    log_ref[2 * pair + 1 : 2 * pair + 2, first : first + size],
                ],
                axis=1,
            )
            chances = jnp.exp(scores - log_total)
            chance_grad = product_transposed_right(v_ref[low:high, at : at + HEAD_DIM], grad)
            mean = jnp.sum(chances * chance_grad, axis=0, keepdims=True)
            score_grad = (chances * (chance_grad - mean)).astype(BF16)
            add(value_sums[pair], low, jnp.dot(chances.astype(BF16), grad, preferred_element_type=F32))
            add(key_sums[pair], low, jnp.dot(score_grad, q, preferred_element_type=F32))
            query_grad = untwo(product_tn(keys, score_grad)) * scale
            qb_ref[first : first + size, lanes] = rotate(query_grad, cosine, -sine).astype(BF16)
    for tile in range(tiles):
        here = slice(tile * size, (tile + 1) * size)
        both = jnp.concatenate([key_sums[0][tile], key_sums[1][tile]], axis=1)
        kb_ref[here, :] = rotate(both, cos_ref[here], -sin_ref[here]).astype(BF16)
        both = jnp.concatenate([value_sums[0][tile], value_sums[1][tile]], axis=1)
        vb_ref[here, :] = both.astype(BF16)


def attention_specs(rows):
    return (
        pl.BlockSpec((1, rows), lambda i: (0, 0)),
        pl.BlockSpec((rows, 2 * LANES), lambda i: (0, i)),
        pl.BlockSpec((rows, LANES), lambda i: (0, i)),
        pl.BlockSpec((8, rows), lambda i: (i, 0)),
        pl.BlockSpec((rows, LANES), lambda i: (0, 0)),
    )


def attend(start, q, k, v):
    rows = q.shape[0]
    one, wide, thin, line, _ = attention_specs(rows)
    steps = k.shape[1] // LANES
    return pl.pallas_call(
        attend_kernel,
        grid=(steps,),
        in_specs=[one, wide, thin, thin],
        out_specs=[wide, line],
        out_shape=[
            jax.ShapeDtypeStruct(q.shape, BF16),
            jax.ShapeDtypeStruct((8 * steps, rows), F32),
        ],
        compiler_params=pltpu.CompilerParams(vmem_limit_bytes=VMEM_LIMIT),
        cost_estimate=SMALL_COST,
        name="attend",
    )(start, q, k, v)


def attend_back(start, q, k, v, grad, logs, cosine, sine):
    rows = q.shape[0]
    one, wide, thin, line, table = attention_specs(rows)
    return pl.pallas_call(
        attend_back_kernel,
        grid=(k.shape[1] // LANES,),
        in_specs=[one, wide, thin, thin, wide, line, table, table],
        out_specs=[wide, thin, thin],
        out_shape=[
            jax.ShapeDtypeStruct(q.shape, BF16),
            jax.ShapeDtypeStruct(k.shape, BF16),
            jax.ShapeDtypeStruct(v.shape, BF16),
        ],
        compiler_params=pltpu.CompilerParams(vmem_limit_bytes=VMEM_LIMIT),
        name="attend_back",
    )(start, q, k, v, grad, logs, cosine, sine)


def mix_kernel(count, place_ref, attended_ref, x_ref, mask_ref, router_ref, gains_ref, *refs):
    pieces = refs[:count]
    state_ref, mixed_ref, gates_ref, weight, sem = refs[count:]
    copies = row_copies(place_ref, pieces, weight, sem)
    for copy in copies:
        copy.wait()
    state = x_ref[...].astype(F32) + jnp.dot(
        attended_ref[...], weight[...], preferred_element_type=F32
    )
    state_ref[...] = state
    mixed = (state * scale_of(state) * gains_ref[1:2, :]).astype(BF16)
    mixed_ref[...] = mixed
    logits = jnp.dot(mixed, router_ref[...], preferred_element_type=F32)
    logits = jnp.where(mask_ref[...] > 0, logits, -1e30)
    powers = jnp.exp(logits - jnp.max(logits, axis=1, keepdims=True))
    gates_ref[...] = powers / jnp.sum(powers, axis=1, keepdims=True)


def mix_back_kernel(
    count,
    chunks,
    experts,
    place_ref,
    attended_ref,
    state_ref,
    mixed_ref,
    dy_ref,
    gates_ref,
    gate_grad_ref,
    router_ref,
    gains_ref,
    *refs,
):
    sums = refs[:chunks]
    pieces = refs[chunks : chunks + count]
    state_grad_ref, attended_grad_ref, pack_ref, weight, sem = refs[chunks + count :]
    copies = row_copies(place_ref, pieces, weight, sem)
    gates = gates_ref[...]
    gate_grad = gate_grad_ref[...]
    logit_grad = (
        gates * (gate_grad - jnp.sum(gates * gate_grad, axis=1, keepdims=True))
    ).astype(BF16)
    rows = jnp.concatenate([part[...] for part in sums], axis=0).astype(F32)
    mixed_grad = product_transposed_right(logit_grad, router_ref[...]) + rows
    state = state_ref[...]
    scale = scale_of(state)
    gain_grad = jnp.sum(mixed_grad * (state * scale), axis=0, keepdims=True)
    scaled = gains_ref[1:2, :] * mixed_grad
    mean = jnp.mean(scaled * state, axis=1, keepdims=True)
    state_grad = dy_ref[...].astype(F32) + scale * scaled - state * (scale * scale * scale * mean)
    state_grad_ref[...] = state_grad
    branch = state_grad.astype(BF16)
    for copy in copies:
        copy.wait()
    attended_grad_ref[...] = product_transposed_right(branch, weight[...]).astype(BF16)
    width = state.shape[1]
    pack_ref[:, :width] = product_tn(attended_ref[...], branch).astype(BF16)
    line = lax.broadcasted_iota(jnp.int32, (LANES, width), 0)
    column = jnp.where(line == experts, gain_grad, 0.0).T
    pack_ref[:, width:] = (product_tn(mixed_ref[...], logit_grad) + column).astype(BF16)


def project_back_kernel(
    count,
    place_ref,
    normed_ref,
    x_ref,
    state_grad_ref,
    gains_ref,
    qb_ref,
    kb_ref,
    vb_ref,
    *refs,
):
    pieces = refs[:count]
    out_ref, pack_ref, weight, sem = refs[count:]
    copies = row_copies(place_ref, pieces, weight, sem)
    normed = normed_ref[...]
    at = 0
    for back_ref in (qb_ref, kb_ref, vb_ref):
        width = back_ref.shape[1]
        pack_ref[:, at : at + width] = product_tn(normed, back_ref[...]).astype(BF16)
        at += width
    for copy in copies:
        copy.wait()
    grad = None
    first = 0
    for back_ref in (qb_ref, kb_ref, vb_ref):
        width = back_ref.shape[1]
        part = product_transposed_right(back_ref[...], weight[:, first : first + width])
        grad = part if grad is None else grad + part
        first += width
    x = x_ref[...].astype(F32)
    scale = scale_of(x)
    gain_grad = jnp.sum(grad * (x * scale), axis=0, keepdims=True)
    scaled = gains_ref[0:1, :] * grad
    mean = jnp.mean(scaled * x, axis=1, keepdims=True)
    out_ref[...] = (
        state_grad_ref[...] + scale * scaled - x * (scale * scale * scale * mean)
    ).astype(BF16)
    line = lax.broadcasted_iota(jnp.int32, (LANES, x.shape[1]), 0)
    pack_ref[:, at:] = jnp.where(line == 0, gain_grad, 0.0).T.astype(BF16)


def per_device(
    tokens,
    gain_attn,
    w_query,
    key_weight,
    value_weight,
    w_out,
    gain_mix,
    router,
    w_gate,
    w_up,
    w_down,
    routes,
    lengths,
    cotangent,
):
    total_rows, model_width = tokens.shape
    experts = router.shape[1]
    local_experts, _, hidden = w_gate.shape
    peers = lax.axis_size("expert")
    part_rows, q_width = w_query.shape
    kv_width = key_weight.shape[1]
    first_width = q_width + 2 * kv_width + LANES

    small = jnp.concatenate(
        [
            router,
            gain_attn[:, None],
            gain_mix[:, None],
            jnp.zeros((part_rows, LANES - experts - 2), BF16),
        ],
        axis=1,
    )
    first_pieces, first_places = fetch_rows(
        jnp.concatenate([w_query, key_weight, value_weight, small], axis=1)
    )
    out_pieces, out_places = fetch_rows(w_out)
    packed = jnp.concatenate([jnp.concatenate([w_gate, w_up], axis=2), w_down], axis=1)
    pieces = gather_pieces(packed)

    expert_ids = jnp.arange(experts, dtype=jnp.int32)
    chosen = jnp.any(routes[:, :, None] == expert_ids[None, None, :], axis=1)
    mask_rows = total_rows * experts // model_width
    mask_space = -(-mask_rows // 16) * 16
    every_dy = lax.all_gather(
        jnp.concatenate(
            [
                cotangent,
                jnp.pad(
                    chosen.astype(BF16).reshape(mask_rows, model_width),
                    ((0, mask_space - mask_rows), (0, 0)),
                ),
            ],
            axis=0,
        ),
        "expert",
        axis=0,
    )
    every_mask = jnp.pad(
        every_dy[:, total_rows : total_rows + mask_rows].reshape(peers, total_rows, experts),
        ((0, 0), (0, 0), (0, LANES - experts)),
    )

    own_mask = jnp.pad(chosen.astype(BF16), ((0, 0), (0, LANES - experts)))

    doc_ends = jnp.cumsum(lengths[0])
    token_index = jnp.arange(total_rows, dtype=jnp.int32)
    past_end = token_index[:, None] >= doc_ends[None, :]
    doc_start = jnp.sum(jnp.where(past_end, lengths[0][None, :], 0), axis=1)
    position = (token_index - doc_start).astype(F32)
    half_head = HEAD_DIM // 2
    inverse = 10000.0 ** (-(jnp.arange(half_head, dtype=F32) * 2.0 / HEAD_DIM))
    angles = position[:, None] * inverse[None, :]
    cosine, sine = jnp.cos(angles), jnp.sin(angles)
    cosine = jnp.concatenate([cosine] * (LANES // half_head), axis=1)
    sine = jnp.concatenate([-sine, sine] * (LANES // HEAD_DIM), axis=1)
    start = doc_start[None, :].astype(jnp.int32)

    normed, q, k, v, gains, router_lanes = simple_call(
        functools.partial(project_kernel, len(first_pieces), experts),
        "project",
        first_places,
        [tokens, cosine, sine],
        first_pieces,
        [
            (tokens.shape, BF16),
            ((total_rows, q_width), BF16),
            ((total_rows, kv_width), BF16),
            ((total_rows, kv_width), BF16),
            ((8, model_width), F32),
            ((model_width, LANES), BF16),
        ],
        [
            pltpu.VMEM((model_width, first_width), BF16),
            pltpu.SemaphoreType.DMA((len(first_pieces),)),
        ],
        SMALL_COST,
    )
    attended, logs = attend(start, q, k, v)
    state, mixed_in, gates = simple_call(
        functools.partial(mix_kernel, len(out_pieces)),
        "mix",
        out_places,
        [attended, tokens, own_mask, router_lanes, gains],
        out_pieces,
        [(tokens.shape, F32), (tokens.shape, BF16), ((total_rows, LANES), F32)],
        [
            pltpu.VMEM((q_width, model_width), BF16),
            pltpu.SemaphoreType.DMA((len(out_pieces),)),
        ],
        SMALL_COST,
    )

    part = total_rows // CHUNKS
    every_x, out_part, row_part, act, gate_back, up_back, scores_part = [], [], [], [], [], [], []
    for chunk in range(CHUNKS):
        gathered = lax.all_gather(
            mixed_in[chunk * part : (chunk + 1) * part], "expert", axis=0, tiled=True
        )
        results = run_experts(gathered, every_dy, every_mask, router_lanes, pieces, chunk)
        every_x.append(gathered)
        for kept, result in zip((out_part, row_part, act, gate_back, up_back, scores_part), results):
            kept.append(result)
    row_sum = [
        lax.psum_scatter(rows, "expert", scatter_dimension=0, tiled=True) for rows in row_part
    ]
    sent_scores = jnp.concatenate(
        [
            values[:, :local_experts].reshape(peers, -1, LANES)
            for values in scores_part
        ],
        axis=1,
    )
    gate_grad = lax.all_to_all(sent_scores, "expert", split_axis=0, concat_axis=0, tiled=True)
    gate_grad = (
        gate_grad.reshape(peers, total_rows, local_experts)
        .transpose(1, 0, 2)
        .reshape(total_rows, experts)
    )
    *out_part, row_last = lax.optimization_barrier((*out_part, row_sum[-1]))
    row_sum[-1] = row_last
    out_sum = [lax.psum_scatter(rows, "expert", scatter_dimension=0, tiled=True) for rows in out_part]

    down_grad = down_gradient(act, every_dy, local_experts)
    gu_grad = gate_up_gradient(every_x, gate_back, up_back, local_experts)

    state_grad, attended_grad, pack = simple_call(
        functools.partial(mix_back_kernel, len(out_pieces), CHUNKS, experts),
        "mix_back",
        out_places,
        [
            attended,
            state,
            mixed_in,
            cotangent,
            gates,
            jnp.pad(gate_grad, ((0, 0), (0, LANES - experts))),
            router_lanes,
            gains,
            *row_sum,
        ],
        out_pieces,
        [
            (tokens.shape, F32),
            ((total_rows, q_width), BF16),
            ((q_width, model_width + LANES), BF16),
        ],
        [
            pltpu.VMEM((q_width, model_width), BF16),
            pltpu.SemaphoreType.DMA((len(out_pieces),)),
        ],
    )
    early = sum_everywhere(pack)
    query_back, key_back, value_back = attend_back(
        start, q, k, v, attended_grad, logs, cosine, sine
    )
    input_grad, late_pack = simple_call(
        functools.partial(project_back_kernel, len(first_pieces)),
        "project_back",
        first_places,
        [normed, tokens, state_grad, gains, query_back, key_back, value_back],
        first_pieces,
        [(tokens.shape, BF16), ((model_width, first_width), BF16)],
        [
            pltpu.VMEM((model_width, first_width), BF16),
            pltpu.SemaphoreType.DMA((len(first_pieces),)),
        ],
    )
    expert_down_sum = scatter_sum(down_grad, 1, value_back)
    gu_sum = scatter_sum(gu_grad, 1, value_back)
    expert_gate_sum = gu_sum[:, :, :hidden]
    expert_up_sum = gu_sum[:, :, hidden:]
    late = sum_everywhere(late_pack)
    state, _ = lax.optimization_barrier((state, value_back))
    output = state + jnp.concatenate(out_sum, axis=0).astype(F32)
    q_end = q_width
    return (
        output.astype(BF16),
        input_grad,
        late[:, q_end + 2 * kv_width],
        late[:, :q_end],
        late[:, q_end : q_end + kv_width],
        late[:, q_end + kv_width : q_end + 2 * kv_width],
        early[:, :model_width],
        early[:, model_width + experts],
        early[:, model_width : model_width + experts],
        expert_gate_sum,
        expert_up_sum,
        expert_down_sum,
    )


def solution(mesh):
    in_specs = (
        P(("expert", "shard"), None),
        P("shard"),
        P("shard", None),
        P("shard", None),
        P("shard", None),
        P("shard", None),
        P("shard"),
        P("shard", None),
        P("expert", "shard", None),
        P("expert", "shard", None),
        P("expert", "shard", None),
        P(("expert", "shard"), None),
        P(("expert", "shard"), None),
        P(("expert", "shard"), None),
    )
    out_specs = (
        P(("expert", "shard"), None),
        P(("expert", "shard"), None),
        P("shard"),
        P("shard", None),
        P("shard", None),
        P("shard", None),
        P("shard", None),
        P("shard"),
        P("shard", None),
        P("expert", "shard", None),
        P("expert", "shard", None),
        P("expert", "shard", None),
    )
    return jax.shard_map(
        per_device, mesh=mesh, in_specs=in_specs, out_specs=out_specs, check_vma=False
    )
```

```python
import functools
import math

import jax
import jax.numpy as jnp
from jax import lax
from jax.experimental import pallas as pl
from jax.experimental.pallas import tpu as pltpu
from jax.sharding import PartitionSpec as P

QUERY_HEADS = 16
KEY_VALUE_HEADS = 8
HEAD_DIM = 64
LANES = 128
VMEM_LIMIT = 58 * 1024 * 1024
SMALL_COST = pl.CostEstimate(flops=0, bytes_accessed=0, transcendentals=0)
F32 = jnp.float32
BF16 = jnp.bfloat16


def matrix_product(left_side, right_side):
    return jnp.dot(left_side, right_side, preferred_element_type=jnp.float32)


def product_tn(left_side, right_side):
    return lax.dot_general(
        left_side, right_side, (((0,), (0,)), ((), ())), preferred_element_type=jnp.float32
    )


def product_transposed_right(left_side, right_side):
    return lax.dot_general(
        left_side, right_side, (((1,), (1,)), ((), ())), preferred_element_type=jnp.float32
    )


def pick(blocks, index):
    return lax.dynamic_index_in_dim(blocks, index, 0, keepdims=False)


def flip_shard(value, flip):
    return lax.ppermute(value, "shard", [(i, i ^ flip) for i in range(4)])


def flip_layer(value, flip):
    size = lax.axis_size("expert")
    return lax.ppermute(value, "expert", [(i, i ^ (2 * flip)) for i in range(size)])


def swap_cores(value):
    size = lax.axis_size("expert")
    return lax.ppermute(value, "expert", [(i, i ^ 1) for i in range(size)])


def both_ways(value, first, second):
    half = value.shape[0] // 2
    one, two = first(value), second(value)
    return one, two, first(two[:half]), second(one[half:])


def fetch_rows(rows, after=None):
    count = lax.axis_size("shard")
    size = rows.shape[0]
    if count != 4:
        return [lax.all_gather(rows, "shard", axis=0, tiled=True)], jnp.zeros((1,), jnp.int32)
    me = lax.axis_index("shard")
    core = lax.axis_index("expert") % 2
    half = size // 2
    mine = lax.dynamic_slice_in_dim(rows, core * half, half, 0)
    if after is not None:
        mine, _ = lax.optimization_barrier((mine, after))
    one, two, low, high = both_ways(mine, lambda v: flip_shard(v, 1), lambda v: flip_shard(v, 2))
    pieces, places = [rows], [me * size]
    for got, flip, skip in ((one, 1, 0), (two, 2, 0), (low, 3, 0), (high, 3, half // 2)):
        first = (me ^ flip) * size + skip
        pieces += [got, swap_cores(got)]
        places += [first + core * half, first + (1 - core) * half]
    return pieces, jnp.stack(places).astype(jnp.int32)


def fetch_experts(packed, after):
    count = lax.axis_size("shard")
    local = packed.shape[0]
    if count != 4 or local != 2:
        every = lax.all_gather(packed, "shard", axis=0)
        arrays = [every[i] for i in range(count)]
        sources = [[(i, j, i) for i in range(count)] for j in range(local)]
        return arrays, sources, [jnp.int32(i) for i in range(count)]
    me = lax.axis_index("shard")
    sent, _ = lax.optimization_barrier((packed, after))
    one, two, low, high = both_ways(sent, lambda v: flip_shard(v, 1), lambda v: flip_shard(v, 2))
    arrays = [packed, one, two, low, high]
    sources = [[(0, j, 0), (1, j, 1), (2, j, 2), (3 + j, 0, 3)] for j in range(2)]
    return arrays, sources, [me, me ^ 1, me ^ 2, me ^ 3]


def gather_layers(value):
    layers = lax.axis_size("expert") // 2
    if layers != 4:
        every = lax.all_gather(value, "expert", axis=0)
        me = lax.axis_index("expert")
        return [value] + [pick(every, me ^ (2 * flip)) for flip in range(1, layers)]
    one, three, low, high = both_ways(
        value, lambda v: flip_layer(v, 1), lambda v: flip_layer(v, 3)
    )
    return [value, one, jnp.concatenate([low, high], axis=0), three]


def sum_layers(mine, other):
    layers = lax.axis_size("expert") // 2
    arrived = [swap_cores(value) for value in other]
    arrived = [piece for value in arrived for piece in jnp.split(value, value.shape[0] // mine[0].shape[0])]

    def paired(flip):
        return mine[flip].astype(F32) + arrived[flip].astype(F32)

    if layers != 4:
        me = lax.axis_index("expert") // 2
        stack = jnp.stack([paired(flip).astype(BF16) for flip in range(layers)])
        blocks = jnp.stack([pick(stack, me ^ place) for place in range(layers)])
        groups = [[2 * i + core for i in range(layers)] for core in range(2)]
        return [
            lax.psum_scatter(
                blocks, "expert", scatter_dimension=0, axis_index_groups=groups
            )
        ]
    half = mine[0].shape[0] // 2
    far = paired(2).astype(BF16)
    low = flip_layer(far[:half], 1).astype(F32)
    high = flip_layer(far[half:], 3).astype(F32)
    three, one = paired(3), paired(1)
    three = jnp.concatenate([three[:half] + low, three[half:]], axis=0).astype(BF16)
    one = jnp.concatenate([one[:half], one[half:] + high], axis=0).astype(BF16)
    return [mine[0], arrived[0], flip_layer(one, 1), flip_layer(three, 3)]


def scatter_sum(values, axis, after=None):
    count = lax.axis_size("shard")
    if count != 4:
        return lax.psum_scatter(
            values.astype(BF16), "shard", scatter_dimension=axis, tiled=True
        ).astype(F32)
    me = lax.axis_index("shard")
    size = values.shape[axis] // count
    own = lax.dynamic_slice_in_dim(values, me * size, size, axis)
    if after is not None:
        own, _ = lax.optimization_barrier((own, after))
    total = own.astype(F32)
    for flip in (1, 2, 3):
        sent = lax.dynamic_slice_in_dim(values, (me ^ flip) * size, size, axis).astype(BF16)
        total = total + flip_shard(sent, flip).astype(F32)
    return total


def sum_everywhere(grad):
    count = lax.axis_size("shard")
    layers = lax.axis_size("expert") // 2
    core = lax.axis_index("expert") % 2
    width = grad.shape[1]
    half = grad.shape[0] // count // 2
    blocks = grad.reshape(count, 2, half, width)
    mine = lax.dynamic_index_in_dim(blocks, core, 1, keepdims=False)
    away = lax.dynamic_index_in_dim(blocks, 1 - core, 1, keepdims=False)
    paired = mine.astype(F32) + swap_cores(away).astype(F32)
    local = scatter_sum(paired, 0).reshape(half, width).astype(BF16)
    if layers != 4:
        groups = [[2 * i + side for i in range(layers)] for side in range(2)]
        total = lax.psum(local, "expert", axis_index_groups=groups)
    else:
        low, high = local[: half // 2], local[half // 2 :]
        for order in ((1, 3), (3, 1)):
            low, high = (
                (low.astype(F32) + flip_layer(low, order[0]).astype(F32)).astype(BF16),
                (high.astype(F32) + flip_layer(high, order[1]).astype(F32)).astype(BF16),
            )
        total = jnp.concatenate([low, high], axis=0)
    other = swap_cores(total)
    low = jnp.where(core == 0, total, other)
    high = jnp.where(core == 0, other, total)
    return jnp.concatenate([low, high], axis=0).astype(F32)


def expert_kernel(sources, pairs, arrays, place_ref, mask_ref, router_ref, *refs):
    xs, refs = refs[: 2 * pairs], refs[2 * pairs :]
    dys, refs = refs[: 2 * pairs], refs[2 * pairs :]
    pieces, refs = refs[:arrays], refs[arrays:]
    outs, rows_out = refs[0:2], refs[2:4]
    act_ref, gate_ref, up_ref, score_ref, gu, down, x_in, dy_in, sem, in_sem = refs[4:]
    local, rows, width = pieces[0].shape
    third = rows // 3
    hidden = width // 2
    step = pl.program_id(0)

    def weight_copies(j):
        copies = []
        for number, (array, index, slot) in enumerate(sources[j]):
            at = place_ref[slot]
            copies.append(
                pltpu.make_async_copy(
                    pieces[array].at[index, pl.ds(0, 2 * third), :],
                    gu.at[j, pl.ds(pl.multiple_of(at * (2 * third), 16), 2 * third), :],
                    sem.at[j, number, 0],
                )
            )
            copies.append(
                pltpu.make_async_copy(
                    pieces[array].at[index, pl.ds(2 * third, third), :],
                    down.at[j, pl.ds(pl.multiple_of(at * third, 16), third), :],
                    sem.at[j, number, 1],
                )
            )
        return copies

    def input_copies(i):
        slot = i % 2
        return [
            pltpu.make_async_copy(xs[i], x_in.at[slot], in_sem.at[slot, 0]),
            pltpu.make_async_copy(dys[i], dy_in.at[slot], in_sem.at[slot, 1]),
        ]

    @pl.when(step == 0)
    def _():
        for copy in input_copies(0):
            copy.start()
        for j in range(local):
            for copy in weight_copies(j):
                copy.start()

    for i in range(2 * pairs):

        @pl.when(step == i)
        def _(i=i):
            if i + 1 < 2 * pairs:
                for copy in input_copies(i + 1):
                    copy.start()
            for copy in input_copies(i):
                copy.wait()

    slot = lax.rem(step, 2)
    x = x_in[slot]
    tile = x.shape[0]
    dy = dy_in[slot]
    mask = mask_ref[...]
    lane = lax.broadcasted_iota(jnp.int32, (tile, LANES), 1)
    logits = jnp.where(mask > 0, jnp.dot(x, router_ref[...], preferred_element_type=F32), -1e30)
    powers = jnp.exp(logits - jnp.max(logits, axis=1, keepdims=True))
    chances = powers / jnp.sum(powers, axis=1, keepdims=True)
    out = None
    row = None
    scores = jnp.zeros((tile, LANES), F32)
    own_slot = max(slot for per in sources for _, _, slot in per) + 1
    for j in range(local):

        @pl.when(step == 0)
        def _(j=j):
            for copy in weight_copies(j):
                copy.wait()

        own = place_ref[own_slot] * local + j
        gate = jnp.sum(jnp.where(lane == own, chances, 0.0), axis=1, keepdims=True)
        left = gu[j, :, :hidden]
        right = gu[j, :, hidden:]
        back = down[j]
        gate_val = jnp.dot(x, left, preferred_element_type=F32)
        up_val = jnp.dot(x, right, preferred_element_type=F32)
        inner_grad = product_transposed_right(dy, back)
        sigmoid = 0.5 + 0.5 * jnp.tanh(0.5 * gate_val)
        swish = gate_val * sigmoid
        inner = (swish * up_val).astype(BF16).astype(F32)
        score = jnp.sum(inner * inner_grad, axis=1, keepdims=True)
        scores = jnp.where(lane == j, score, scores)
        act = (gate * inner).astype(BF16)
        scaled = gate * inner_grad
        gate_back = (scaled * up_val * (sigmoid + swish * (1.0 - sigmoid))).astype(BF16)
        up_back = (scaled * swish).astype(BF16)
        act_ref[:, j * hidden : (j + 1) * hidden] = act
        gate_ref[:, j * hidden : (j + 1) * hidden] = gate_back
        up_ref[:, j * hidden : (j + 1) * hidden] = up_back
        part = jnp.dot(act, back, preferred_element_type=F32)
        out = part if out is None else out + part
        part = product_transposed_right(gate_back, left) + product_transposed_right(up_back, right)
        row = part if row is None else row + part
    score_ref[...] = scores
    out, row = out.astype(BF16), row.astype(BF16)
    for side in range(2):

        @pl.when(slot == side)
        def _(side=side):
            outs[side][...] = out
            rows_out[side][...] = row


def run_experts(flips, xs, dys, mask, router, weights):
    arrays, sources, places = weights
    pairs = len(flips)
    size, width = xs[0].shape
    local, rows, _ = arrays[0].shape
    third = rows // 3
    count = len(sources[0])
    me = lax.axis_index("expert")
    devices = [me ^ (2 * flip + side) for flip in flips for side in range(2)]
    place = jnp.stack([*places, me, *devices]).astype(jnp.int32)
    skip = len(places) + 1
    block = pl.BlockSpec((size, width), lambda i, p: (i, 0))
    pair = pl.BlockSpec((size, width), lambda i, p: (i // 2, 0))
    anywhere = pl.BlockSpec(memory_space=pl.ANY)
    total = 2 * pairs * size
    return pl.pallas_call(
        functools.partial(expert_kernel, sources, pairs, len(arrays)),
        grid_spec=pltpu.PrefetchScalarGridSpec(
            num_scalar_prefetch=1,
            grid=(2 * pairs,),
            in_specs=[
                pl.BlockSpec((None, size, LANES), lambda i, p: (p[skip + i], 0, 0)),
                pl.BlockSpec((width, LANES), lambda i, p: (0, 0)),
            ]
            + [anywhere] * (4 * pairs + len(arrays)),
            out_specs=[pair] * 4
            + [block, block, block, pl.BlockSpec((size, LANES), lambda i, p: (i, 0))],
            scratch_shapes=[
                pltpu.VMEM((local, 2 * third * count, width), BF16),
                pltpu.VMEM((local, third * count, width), BF16),
                pltpu.VMEM((2, size, width), BF16),
                pltpu.VMEM((2, size, width), BF16),
                pltpu.SemaphoreType.DMA((local, count, 2)),
                pltpu.SemaphoreType.DMA((2, 2)),
            ],
        ),
        out_shape=[jax.ShapeDtypeStruct((pairs * size, width), BF16)] * 4
        + [jax.ShapeDtypeStruct((total, width), BF16)] * 3
        + [jax.ShapeDtypeStruct((total, LANES), F32)],
        compiler_params=pltpu.CompilerParams(vmem_limit_bytes=VMEM_LIMIT),
        cost_estimate=pl.CostEstimate(
            flops=2 * total * width * width * 6, bytes_accessed=total * width * 14, transcendentals=0
        ),
        name="experts",
    )(place, mask, router, *xs, *dys, *arrays)


def grouped(refs, groups):
    at = 0
    for group in groups:
        rows = 0
        taken = []
        while rows < group.shape[0]:
            taken.append(refs[at][...])
            rows += refs[at].shape[0]
            at += 1
        yield jnp.concatenate(taken, axis=0)


def columns_kernel(chunks, groups, local, *refs):
    xs, gates = refs[:chunks], refs[chunks : chunks + groups]
    ups, out_ref = refs[chunks + groups : chunks + 2 * groups], refs[chunks + 2 * groups]
    hidden = out_ref.shape[2] // 2
    totals = [None] * (2 * local)
    for x, gate_ref, up_ref in zip(grouped(xs, gates), gates, ups):
        for j in range(local):
            for side, value_ref in ((0, gate_ref), (1, up_ref)):
                part = product_tn(x, value_ref[:, j * hidden : (j + 1) * hidden])
                at = 2 * j + side
                totals[at] = part if totals[at] is None else totals[at] + part
    for j in range(local):
        for side in range(2):
            out_ref[j, :, side * hidden : (side + 1) * hidden] = totals[2 * j + side].astype(BF16)


def held(value):
    return pl.BlockSpec(value.shape, lambda i: (0, 0), pipeline_mode=pl.Buffered(1))


def gate_up_gradient(xs, gates, ups, local):
    width = xs[0].shape[1]
    piece = width // 4
    rows = sum(x.shape[0] for x in xs)
    return pl.pallas_call(
        functools.partial(columns_kernel, len(xs), len(gates), local),
        grid=(4,),
        in_specs=[pl.BlockSpec((x.shape[0], piece), lambda i: (0, i)) for x in xs]
        + [held(value) for value in (*gates, *ups)],
        out_specs=pl.BlockSpec((local, piece, width), lambda i: (0, i, 0)),
        out_shape=jax.ShapeDtypeStruct((local, width, width), BF16),
        compiler_params=pltpu.CompilerParams(vmem_limit_bytes=VMEM_LIMIT),
        cost_estimate=pl.CostEstimate(
            flops=4 * rows * width * width, bytes_accessed=rows * width * 6, transcendentals=0
        ),
        name="gate_up_gradient",
    )(*xs, *gates, *ups)


def down_kernel(groups, chunks, *refs):
    acts, dys, out_ref = refs[:groups], refs[groups : groups + chunks], refs[groups + chunks]
    total = None
    for act_ref, dy in zip(acts, grouped(dys, acts)):
        part = product_tn(act_ref[...], dy)
        total = part if total is None else total + part
    out_ref[...] = total.astype(BF16)


def down_gradient(acts, dys, local):
    width = acts[0].shape[1]
    piece = width // 4
    rows = sum(act.shape[0] for act in acts)
    return pl.pallas_call(
        functools.partial(down_kernel, len(acts), len(dys)),
        grid=(4,),
        in_specs=[pl.BlockSpec((act.shape[0], piece), lambda i: (0, i)) for act in acts]
        + [held(dy) for dy in dys],
        out_specs=pl.BlockSpec((piece, width), lambda i: (i, 0)),
        out_shape=jax.ShapeDtypeStruct((width, width), BF16),
        compiler_params=pltpu.CompilerParams(vmem_limit_bytes=VMEM_LIMIT),
        cost_estimate=pl.CostEstimate(
            flops=2 * rows * width * width, bytes_accessed=rows * width * 4, transcendentals=0
        ),
        name="down_gradient",
    )(*acts, *dys).reshape(local, width // local, width)


def row_copies(place_ref, pieces, target, sem):
    copies = []
    for i, piece in enumerate(pieces):
        rows = piece.shape[0]
        first = pl.multiple_of(place_ref[i], 16)
        copies.append(
            pltpu.make_async_copy(piece, target.at[pl.ds(first, rows), :], sem.at[i])
        )
    for copy in copies:
        copy.start()
    return copies


def scale_of(values):
    return lax.rsqrt(jnp.mean(values * values, axis=-1, keepdims=True) + 1e-06)


def rotate(values, cosine, sine):
    lane = lax.broadcasted_iota(jnp.int32, values.shape, 1) % HEAD_DIM
    half = HEAD_DIM // 2
    turned = jnp.where(
        lane < half, pltpu.roll(values, LANES - half, 1), pltpu.roll(values, half, 1)
    )
    return values * cosine + turned * sine


def project_kernel(count, experts, place_ref, x_ref, cos_ref, sin_ref, *refs):
    pieces = refs[:count]
    normed_ref, q_ref, k_ref, v_ref, gains_ref, router_ref, weight, sem = refs[count:]
    copies = row_copies(place_ref, pieces, weight, sem)
    x = x_ref[...].astype(F32)
    scaled = x * scale_of(x)
    cosine, sine = cos_ref[...], sin_ref[...]
    for copy in copies:
        copy.wait()
    q_width, kv_width = q_ref.shape[1], k_ref.shape[1]
    small = weight[:, q_width + 2 * kv_width :]
    lane = lax.broadcasted_iota(jnp.int32, small.shape, 1)
    router_ref[...] = jnp.where(lane < experts, small.astype(F32), 0.0).astype(BF16)
    turned = small.astype(F32).T
    gains_ref[...] = jnp.concatenate(
        [turned[experts : experts + 2], jnp.zeros((6, turned.shape[1]), F32)], axis=0
    )
    normed = (scaled * turned[experts : experts + 1]).astype(BF16)
    normed_ref[...] = normed
    for first in range(0, q_width, 256):
        values = jnp.dot(normed, weight[:, first : first + 256], preferred_element_type=F32)
        for part in (0, LANES):
            q_ref[:, first + part : first + part + LANES] = rotate(
                values[:, part : part + LANES], cosine, sine
            ).astype(BF16)
    for first in range(0, kv_width, 256):
        at = q_width + first
        values = jnp.dot(normed, weight[:, at : at + 256], preferred_element_type=F32)
        for part in (0, LANES):
            k_ref[:, first + part : first + part + LANES] = rotate(
                values[:, part : part + LANES], cosine, sine
            ).astype(BF16)
    at = q_width + kv_width
    v_ref[...] = jnp.dot(
        normed, weight[:, at : at + kv_width], preferred_element_type=F32
    ).astype(BF16)


def simple_call(kernel, name, prefetch, inputs, pieces, outputs, scratch, cost=None):
    def whole(shape):
        return pl.BlockSpec(shape, lambda i, p: (0,) * len(shape))

    return pl.pallas_call(
        kernel,
        grid_spec=pltpu.PrefetchScalarGridSpec(
            num_scalar_prefetch=1,
            grid=(1,),
            in_specs=[whole(value.shape) for value in inputs]
            + [pl.BlockSpec(memory_space=pl.ANY)] * len(pieces),
            out_specs=[whole(shape) for shape, _ in outputs],
            scratch_shapes=scratch,
        ),
        out_shape=[jax.ShapeDtypeStruct(shape, kind) for shape, kind in outputs],
        compiler_params=pltpu.CompilerParams(vmem_limit_bytes=VMEM_LIMIT),
        cost_estimate=cost,
        name=name,
    )(prefetch, *inputs, *pieces)


def key_window(tile, size, rows):
    low = max(0, tile * size - (rows // 2 - 1)) // size * size
    return low, (tile + 1) * size


def tile_mask(start_ref, low, high, first, size):
    shape = (high - low, size)
    key = lax.broadcasted_iota(jnp.int32, shape, 0) + low
    query = lax.broadcasted_iota(jnp.int32, shape, 1) + first
    seen = (key >= start_ref[:, first : first + size]) & (key <= query)
    return jnp.concatenate([seen, seen], axis=1)


def two_heads(values):
    return jnp.concatenate([values[:, :HEAD_DIM], values[:, HEAD_DIM:]], axis=0)


def untwo(values):
    size = values.shape[1] // 2
    return jnp.concatenate([values[:, :size], values[:, size:]], axis=0).T


def attend_kernel(start_ref, q_ref, k_ref, v_ref, out_ref, log_ref):
    rows = q_ref.shape[0]
    size = LANES
    scale = 1.0 / math.sqrt(HEAD_DIM)
    logs = [[], []]
    for tile in range(rows // size):
        low, high = key_window(tile, size, rows)
        first = tile * size
        seen = tile_mask(start_ref, low, high, first, size)
        for pair in range(2):
            q = two_heads(q_ref[first : first + size, pair * LANES : (pair + 1) * LANES])
            q = (q.astype(F32) * scale).astype(BF16)
            at = pair * HEAD_DIM
            scores = product_transposed_right(k_ref[low:high, at : at + HEAD_DIM], q)
            scores = jnp.where(seen, scores, -1e30)
            top = jnp.max(scores, axis=0, keepdims=True)
            powers = jnp.exp(scores - top)
            total = jnp.sum(powers, axis=0, keepdims=True)
            low_chances = (powers * (1.0 / total)).astype(BF16)
            mixed = product_tn(v_ref[low:high, at : at + HEAD_DIM], low_chances)
            out_ref[first : first + size, pair * LANES : (pair + 1) * LANES] = untwo(mixed).astype(
                BF16
            )
            logs[pair].append(top + jnp.log(total))
    lines = []
    for pair in range(2):
        for head in range(2):
            lines.append(
                jnp.concatenate([v[:, head * size : (head + 1) * size] for v in logs[pair]], axis=1)
            )
    log_ref[...] = jnp.concatenate(lines + [jnp.zeros((4, rows), F32)], axis=0)


def attend_back_kernel(
    start_ref, q_ref, k_ref, v_ref, grad_ref, log_ref, cos_ref, sin_ref, qb_ref, kb_ref, vb_ref
):
    rows = q_ref.shape[0]
    size = LANES
    tiles = rows // size
    scale = 1.0 / math.sqrt(HEAD_DIM)
    key_sums = [[None] * tiles, [None] * tiles]
    value_sums = [[None] * tiles, [None] * tiles]

    def add(sums, low, part):
        for i in range(part.shape[0] // size):
            piece = part[i * size : (i + 1) * size]
            at = low // size + i
            sums[at] = piece if sums[at] is None else sums[at] + piece

    for tile in range(tiles):
        low, high = key_window(tile, size, rows)
        first = tile * size
        seen = tile_mask(start_ref, low, high, first, size)
        cosine, sine = cos_ref[first : first + size], sin_ref[first : first + size]
        for pair in range(2):
            lanes = slice(pair * LANES, (pair + 1) * LANES)
            q = two_heads(q_ref[first : first + size, lanes])
            q = (q.astype(F32) * scale).astype(BF16)
            grad = two_heads(grad_ref[first : first + size, lanes])
            at = pair * HEAD_DIM
            keys = k_ref[low:high, at : at + HEAD_DIM]
            scores = jnp.where(seen, product_transposed_right(keys, q), -1e30)
            log_total = jnp.concatenate(
                [
                    log_ref[2 * pair : 2 * pair + 1, first : first + size],
                    log_ref[2 * pair + 1 : 2 * pair + 2, first : first + size],
                ],
                axis=1,
            )
            chances = jnp.exp(scores - log_total)
            chance_grad = product_transposed_right(v_ref[low:high, at : at + HEAD_DIM], grad)
            mean = jnp.sum(chances * chance_grad, axis=0, keepdims=True)
            score_grad = (chances * (chance_grad - mean)).astype(BF16)
            add(value_sums[pair], low, jnp.dot(chances.astype(BF16), grad, preferred_element_type=F32))
            add(key_sums[pair], low, jnp.dot(score_grad, q, preferred_element_type=F32))
            query_grad = untwo(product_tn(keys, score_grad)) * scale
            qb_ref[first : first + size, lanes] = rotate(query_grad, cosine, -sine).astype(BF16)
    for tile in range(tiles):
        here = slice(tile * size, (tile + 1) * size)
        both = jnp.concatenate([key_sums[0][tile], key_sums[1][tile]], axis=1)
        kb_ref[here, :] = rotate(both, cos_ref[here], -sin_ref[here]).astype(BF16)
        both = jnp.concatenate([value_sums[0][tile], value_sums[1][tile]], axis=1)
        vb_ref[here, :] = both.astype(BF16)


def attention_specs(rows):
    return (
        pl.BlockSpec((1, rows), lambda i: (0, 0)),
        pl.BlockSpec((rows, 2 * LANES), lambda i: (0, i)),
        pl.BlockSpec((rows, LANES), lambda i: (0, i)),
        pl.BlockSpec((8, rows), lambda i: (i, 0)),
        pl.BlockSpec((rows, LANES), lambda i: (0, 0)),
    )


def attend(start, q, k, v):
    rows = q.shape[0]
    one, wide, thin, line, _ = attention_specs(rows)
    steps = k.shape[1] // LANES
    return pl.pallas_call(
        attend_kernel,
        grid=(steps,),
        in_specs=[one, wide, thin, thin],
        out_specs=[wide, line],
        out_shape=[
            jax.ShapeDtypeStruct(q.shape, BF16),
            jax.ShapeDtypeStruct((8 * steps, rows), F32),
        ],
        compiler_params=pltpu.CompilerParams(vmem_limit_bytes=VMEM_LIMIT),
        cost_estimate=SMALL_COST,
        name="attend",
    )(start, q, k, v)


def attend_back(start, q, k, v, grad, logs, cosine, sine):
    rows = q.shape[0]
    one, wide, thin, line, table = attention_specs(rows)
    return pl.pallas_call(
        attend_back_kernel,
        grid=(k.shape[1] // LANES,),
        in_specs=[one, wide, thin, thin, wide, line, table, table],
        out_specs=[wide, thin, thin],
        out_shape=[
            jax.ShapeDtypeStruct(q.shape, BF16),
            jax.ShapeDtypeStruct(k.shape, BF16),
            jax.ShapeDtypeStruct(v.shape, BF16),
        ],
        compiler_params=pltpu.CompilerParams(vmem_limit_bytes=VMEM_LIMIT),
        name="attend_back",
    )(start, q, k, v, grad, logs, cosine, sine)


def mix_kernel(count, place_ref, attended_ref, x_ref, mask_ref, router_ref, gains_ref, *refs):
    pieces = refs[:count]
    state_ref, mixed_ref, gates_ref, weight, sem = refs[count:]
    copies = row_copies(place_ref, pieces, weight, sem)
    for copy in copies:
        copy.wait()
    state = x_ref[...].astype(F32) + jnp.dot(
        attended_ref[...], weight[...], preferred_element_type=F32
    )
    state_ref[...] = state
    mixed = (state * scale_of(state) * gains_ref[1:2, :]).astype(BF16)
    mixed_ref[...] = mixed
    logits = jnp.dot(mixed, router_ref[...], preferred_element_type=F32)
    logits = jnp.where(mask_ref[...] > 0, logits, -1e30)
    powers = jnp.exp(logits - jnp.max(logits, axis=1, keepdims=True))
    gates_ref[...] = powers / jnp.sum(powers, axis=1, keepdims=True)


def mix_back_kernel(
    count,
    chunks,
    experts,
    place_ref,
    attended_ref,
    state_ref,
    mixed_ref,
    dy_ref,
    gates_ref,
    gate_grad_ref,
    router_ref,
    gains_ref,
    *refs,
):
    sums = refs[:chunks]
    pieces = refs[chunks : chunks + count]
    state_grad_ref, attended_grad_ref, pack_ref, weight, sem = refs[chunks + count :]
    copies = row_copies(place_ref, pieces, weight, sem)
    gates = gates_ref[...]
    gate_grad = gate_grad_ref[...]
    logit_grad = (
        gates * (gate_grad - jnp.sum(gates * gate_grad, axis=1, keepdims=True))
    ).astype(BF16)
    rows = sum(part[...].astype(F32) for part in sums)
    mixed_grad = product_transposed_right(logit_grad, router_ref[...]) + rows
    state = state_ref[...]
    scale = scale_of(state)
    gain_grad = jnp.sum(mixed_grad * (state * scale), axis=0, keepdims=True)
    scaled = gains_ref[1:2, :] * mixed_grad
    mean = jnp.mean(scaled * state, axis=1, keepdims=True)
    state_grad = dy_ref[...].astype(F32) + scale * scaled - state * (scale * scale * scale * mean)
    state_grad_ref[...] = state_grad
    branch = state_grad.astype(BF16)
    for copy in copies:
        copy.wait()
    attended_grad_ref[...] = product_transposed_right(branch, weight[...]).astype(BF16)
    width = state.shape[1]
    pack_ref[:, :width] = product_tn(attended_ref[...], branch).astype(BF16)
    line = lax.broadcasted_iota(jnp.int32, (LANES, width), 0)
    column = jnp.where(line == experts, gain_grad, 0.0).T
    pack_ref[:, width:] = (product_tn(mixed_ref[...], logit_grad) + column).astype(BF16)


def project_back_kernel(
    count,
    place_ref,
    normed_ref,
    x_ref,
    state_grad_ref,
    gains_ref,
    qb_ref,
    kb_ref,
    vb_ref,
    *refs,
):
    pieces = refs[:count]
    out_ref, pack_ref, weight, sem = refs[count:]
    copies = row_copies(place_ref, pieces, weight, sem)
    normed = normed_ref[...]
    at = 0
    for back_ref in (qb_ref, kb_ref, vb_ref):
        width = back_ref.shape[1]
        pack_ref[:, at : at + width] = product_tn(normed, back_ref[...]).astype(BF16)
        at += width
    for copy in copies:
        copy.wait()
    grad = None
    first = 0
    for back_ref in (qb_ref, kb_ref, vb_ref):
        width = back_ref.shape[1]
        part = product_transposed_right(back_ref[...], weight[:, first : first + width])
        grad = part if grad is None else grad + part
        first += width
    x = x_ref[...].astype(F32)
    scale = scale_of(x)
    gain_grad = jnp.sum(grad * (x * scale), axis=0, keepdims=True)
    scaled = gains_ref[0:1, :] * grad
    mean = jnp.mean(scaled * x, axis=1, keepdims=True)
    out_ref[...] = (
        state_grad_ref[...] + scale * scaled - x * (scale * scale * scale * mean)
    ).astype(BF16)
    line = lax.broadcasted_iota(jnp.int32, (LANES, x.shape[1]), 0)
    pack_ref[:, at:] = jnp.where(line == 0, gain_grad, 0.0).T.astype(BF16)


def per_device(
    tokens,
    gain_attn,
    w_query,
    key_weight,
    value_weight,
    w_out,
    gain_mix,
    router,
    w_gate,
    w_up,
    w_down,
    routes,
    lengths,
    cotangent,
):
    total_rows, model_width = tokens.shape
    experts = router.shape[1]
    local_experts, _, hidden = w_gate.shape
    peers = lax.axis_size("expert")
    part_rows, q_width = w_query.shape
    kv_width = key_weight.shape[1]
    first_width = q_width + 2 * kv_width + LANES

    small = jnp.concatenate(
        [
            router,
            gain_attn[:, None],
            gain_mix[:, None],
            jnp.zeros((part_rows, LANES - experts - 2), BF16),
        ],
        axis=1,
    )
    first_pieces, first_places = fetch_rows(
        jnp.concatenate([w_query, key_weight, value_weight, small], axis=1)
    )
    out_pieces, out_places = fetch_rows(w_out, first_pieces[-1])
    packed = jnp.concatenate([jnp.concatenate([w_gate, w_up], axis=2), w_down], axis=1)
    weights = fetch_experts(packed, out_pieces[-1])

    every_dy = gather_layers(cotangent)
    every_dy = [value for mine in every_dy for value in (mine, swap_cores(mine))]
    expert_ids = jnp.arange(experts, dtype=jnp.int32)
    chosen = jnp.any(routes[:, :, None] == expert_ids[None, None, :], axis=1).astype(BF16)
    every_mask = lax.all_gather(chosen.reshape(-1, model_width), "expert", axis=0)
    every_mask = jnp.pad(
        every_mask.reshape(peers, total_rows, experts), ((0, 0), (0, 0), (0, LANES - experts))
    )
    own_mask = jnp.pad(chosen, ((0, 0), (0, LANES - experts)))

    doc_ends = jnp.cumsum(lengths[0])
    token_index = jnp.arange(total_rows, dtype=jnp.int32)
    past_end = token_index[:, None] >= doc_ends[None, :]
    doc_start = jnp.sum(jnp.where(past_end, lengths[0][None, :], 0), axis=1)
    position = (token_index - doc_start).astype(F32)
    half_head = HEAD_DIM // 2
    inverse = 10000.0 ** (-(jnp.arange(half_head, dtype=F32) * 2.0 / HEAD_DIM))
    angles = position[:, None] * inverse[None, :]
    cosine, sine = jnp.cos(angles), jnp.sin(angles)
    cosine = jnp.concatenate([cosine] * (LANES // half_head), axis=1)
    sine = jnp.concatenate([-sine, sine] * (LANES // HEAD_DIM), axis=1)
    start = doc_start[None, :].astype(jnp.int32)

    normed, q, k, v, gains, router_lanes = simple_call(
        functools.partial(project_kernel, len(first_pieces), experts),
        "project",
        first_places,
        [tokens, cosine, sine],
        first_pieces,
        [
            (tokens.shape, BF16),
            ((total_rows, q_width), BF16),
            ((total_rows, kv_width), BF16),
            ((total_rows, kv_width), BF16),
            ((8, model_width), F32),
            ((model_width, LANES), BF16),
        ],
        [
            pltpu.VMEM((model_width, first_width), BF16),
            pltpu.SemaphoreType.DMA((len(first_pieces),)),
        ],
        SMALL_COST,
    )
    attended, logs = attend(start, q, k, v)
    state, mixed_in, gates = simple_call(
        functools.partial(mix_kernel, len(out_pieces)),
        "mix",
        out_places,
        [attended, tokens, own_mask, router_lanes, gains],
        out_pieces,
        [(tokens.shape, F32), (tokens.shape, BF16), ((total_rows, LANES), F32)],
        [
            pltpu.VMEM((q_width, model_width), BF16),
            pltpu.SemaphoreType.DMA((len(out_pieces),)),
        ],
        SMALL_COST,
    )

    mixed_in, tied_dy, tied_weights = lax.optimization_barrier((mixed_in, every_dy, weights[0]))
    every_dy, weights = tied_dy, (tied_weights, *weights[1:])
    every_x = gather_layers(mixed_in)
    every_x = [value for mine in every_x for value in (mine, swap_cores(mine))]
    layers = peers // 2
    groups = [[0], [1], list(range(2, layers))]
    out_mine, out_other, row_mine, row_other, acts, gate_back, up_back, scores = (
        [] for _ in range(8)
    )
    kept = (out_mine, out_other, row_mine, row_other, acts, gate_back, up_back, scores)
    for flips in groups:
        here = slice(2 * flips[0], 2 * flips[-1] + 2)
        results = run_experts(
            flips, every_x[here], every_dy[here], every_mask, router_lanes, weights
        )
        for values, result in zip(kept, results):
            values.append(result)

    def by_flip(values):
        return [piece for value in values for piece in jnp.split(value, value.shape[0] // total_rows)]

    row_terms = sum_layers(by_flip(row_mine), row_other)
    sent_scores = jnp.concatenate([value[:, :local_experts] for value in scores], axis=0)
    sent_scores = sent_scores.reshape(peers, -1, LANES)
    me = lax.axis_index("expert")
    for bit in range(peers.bit_length() - 1):
        split = sent_scores.reshape(peers >> (bit + 1), 2, 1 << bit, -1, LANES)
        split = jnp.where((me >> bit) % 2 == 1, split[:, ::-1], split)
        sent_scores = split.reshape(peers, -1, LANES)
    gate_grad = lax.all_to_all(sent_scores, "expert", split_axis=0, concat_axis=0, tiled=True)
    gate_grad = (
        gate_grad.reshape(peers, total_rows, local_experts)
        .transpose(1, 0, 2)
        .reshape(total_rows, experts)
    )
    down_grad = down_gradient(acts, every_dy, local_experts)
    gu_grad = gate_up_gradient(every_x, gate_back, up_back, local_experts)
    row_terms, gate_grad, _ = lax.optimization_barrier((row_terms, gate_grad, gu_grad))
    out_mine, out_other, _ = lax.optimization_barrier((out_mine, out_other, row_terms[-1]))
    out_terms = sum_layers(by_flip(out_mine), out_other)

    state_grad, attended_grad, pack = simple_call(
        functools.partial(mix_back_kernel, len(out_pieces), len(row_terms), experts),
        "mix_back",
        out_places,
        [
            attended,
            state,
            mixed_in,
            cotangent,
            gates,
            jnp.pad(gate_grad, ((0, 0), (0, LANES - experts))),
            router_lanes,
            gains,
            *row_terms,
        ],
        out_pieces,
        [
            (tokens.shape, F32),
            ((total_rows, q_width), BF16),
            ((q_width, model_width + LANES), BF16),
        ],
        [
            pltpu.VMEM((q_width, model_width), BF16),
            pltpu.SemaphoreType.DMA((len(out_pieces),)),
        ],
    )
    early = sum_everywhere(pack)
    query_back, key_back, value_back = attend_back(
        start, q, k, v, attended_grad, logs, cosine, sine
    )
    input_grad, late_pack = simple_call(
        functools.partial(project_back_kernel, len(first_pieces)),
        "project_back",
        first_places,
        [normed, tokens, state_grad, gains, query_back, key_back, value_back],
        first_pieces,
        [(tokens.shape, BF16), ((model_width, first_width), BF16)],
        [
            pltpu.VMEM((model_width, first_width), BF16),
            pltpu.SemaphoreType.DMA((len(first_pieces),)),
        ],
    )
    expert_down_sum = scatter_sum(down_grad, 1, value_back)
    gu_sum = scatter_sum(gu_grad, 1, value_back)
    expert_gate_sum = gu_sum[:, :, :hidden]
    expert_up_sum = gu_sum[:, :, hidden:]
    late = sum_everywhere(late_pack)
    state, _ = lax.optimization_barrier((state, value_back))
    output = state + sum(value.astype(F32) for value in out_terms)
    q_end = q_width
    return (
        output.astype(BF16),
        input_grad,
        late[:, q_end + 2 * kv_width],
        late[:, :q_end],
        late[:, q_end : q_end + kv_width],
        late[:, q_end + kv_width : q_end + 2 * kv_width],
        early[:, :model_width],
        early[:, model_width + experts],
        early[:, model_width : model_width + experts],
        expert_gate_sum,
        expert_up_sum,
        expert_down_sum,
    )


def solution(mesh):
    in_specs = (
        P(("expert", "shard"), None),
        P("shard"),
        P("shard", None),
        P("shard", None),
        P("shard", None),
        P("shard", None),
        P("shard"),
        P("shard", None),
        P("expert", "shard", None),
        P("expert", "shard", None),
        P("expert", "shard", None),
        P(("expert", "shard"), None),
        P(("expert", "shard"), None),
        P(("expert", "shard"), None),
    )
    out_specs = (
        P(("expert", "shard"), None),
        P(("expert", "shard"), None),
        P("shard"),
        P("shard", None),
        P("shard", None),
        P("shard", None),
        P("shard", None),
        P("shard"),
        P("shard", None),
        P("expert", "shard", None),
        P("expert", "shard", None),
        P("expert", "shard", None),
    )
    return jax.shard_map(
        per_device, mesh=mesh, in_specs=in_specs, out_specs=out_specs, check_vma=False
    )
```

```python
import functools
import math

import jax
import jax.numpy as jnp
from jax import lax
from jax.experimental import pallas as pl
from jax.experimental.pallas import tpu as pltpu
from jax.sharding import PartitionSpec as P

QUERY_HEADS = 16
KEY_VALUE_HEADS = 8
HEAD_DIM = 64
LANES = 128
VMEM_LIMIT = 58 * 1024 * 1024


def cost(microseconds):
    return pl.CostEstimate(
        flops=int(microseconds * 1.15e9), bytes_accessed=0, transcendentals=0
    )


F32 = jnp.float32
BF16 = jnp.bfloat16


def matrix_product(left_side, right_side):
    return jnp.dot(left_side, right_side, preferred_element_type=jnp.float32)


def product_tn(left_side, right_side):
    return lax.dot_general(
        left_side, right_side, (((0,), (0,)), ((), ())), preferred_element_type=jnp.float32
    )


def product_transposed_right(left_side, right_side):
    return lax.dot_general(
        left_side, right_side, (((1,), (1,)), ((), ())), preferred_element_type=jnp.float32
    )


def pick(blocks, index):
    return lax.dynamic_index_in_dim(blocks, index, 0, keepdims=False)


def flip_shard(value, flip):
    return lax.ppermute(value, "shard", [(i, i ^ flip) for i in range(4)])


def flip_layer(value, flip):
    size = lax.axis_size("expert")
    return lax.ppermute(value, "expert", [(i, i ^ (2 * flip)) for i in range(size)])


def swap_cores(value):
    size = lax.axis_size("expert")
    return lax.ppermute(value, "expert", [(i, i ^ 1) for i in range(size)])


def both_ways(value, first, second, after=None):
    half = value.shape[0] // 2
    one, two = first(value), second(value)
    if after is not None:
        one, two, _ = lax.optimization_barrier((one, two, after))
    return one, two, first(two[:half]), second(one[half:])


def fetch_rows(rows, before_first=None, before_second=None):
    count = lax.axis_size("shard")
    size = rows.shape[0]
    if count != 4:
        return [lax.all_gather(rows, "shard", axis=0, tiled=True)], jnp.zeros((1,), jnp.int32)
    me = lax.axis_index("shard")
    core = lax.axis_index("expert") % 2
    half = size // 2
    mine = lax.dynamic_slice_in_dim(rows, core * half, half, 0)
    if before_first is not None:
        mine, _ = lax.optimization_barrier((mine, before_first))
    one, two, low, high = both_ways(
        mine, lambda v: flip_shard(v, 1), lambda v: flip_shard(v, 2), before_second
    )
    pieces, places = [rows], [me * size]
    for got, flip, skip in ((one, 1, 0), (two, 2, 0), (low, 3, 0), (high, 3, half // 2)):
        first = (me ^ flip) * size + skip
        pieces += [got, swap_cores(got)]
        places += [first + core * half, first + (1 - core) * half]
    return pieces, jnp.stack(places).astype(jnp.int32)


def fetch_experts(packed, before_first, before_second):
    count = lax.axis_size("shard")
    local = packed.shape[0]
    if count != 4 or local != 2:
        every = lax.all_gather(packed, "shard", axis=0)
        arrays = [every[i] for i in range(count)]
        sources = [[(i, j, i) for i in range(count)] for j in range(local)]
        return arrays, sources, [jnp.int32(i) for i in range(count)]
    me = lax.axis_index("shard")
    sent, _ = lax.optimization_barrier((packed, before_first))
    one, two, low, high = both_ways(
        sent, lambda v: flip_shard(v, 1), lambda v: flip_shard(v, 2), before_second
    )
    arrays = [packed, one, two, low, high]
    sources = [[(0, j, 0), (1, j, 1), (2, j, 2), (3 + j, 0, 3)] for j in range(2)]
    return arrays, sources, [me, me ^ 1, me ^ 2, me ^ 3]


def split_parts(values, axis):
    me = lax.axis_index("shard")
    size = values.shape[axis] // lax.axis_size("shard")
    return [
        lax.dynamic_slice_in_dim(values, (me ^ flip) * size, size, axis) for flip in range(4)
    ]


def send_far(far):
    half = far.shape[0] // 2
    return flip_shard(far[:half], 1), flip_shard(far[half:], 2)


def send_near(one, two, low, high):
    half = one.shape[0] // 2
    two = jnp.concatenate([(two[:half].astype(F32) + low.astype(F32)).astype(BF16), two[half:]], axis=0)
    one = jnp.concatenate([one[:half], (one[half:].astype(F32) + high.astype(F32)).astype(BF16)], axis=0)
    return flip_shard(one, 1), flip_shard(two, 2)


def add_up(values):
    return sum(value.astype(F32) for value in values)


def plain_scatter_sum(values, axis):
    return lax.psum_scatter(values, "shard", scatter_dimension=axis, tiled=True).astype(F32)


def pair_cores(grad):
    count = lax.axis_size("shard")
    core = lax.axis_index("expert") % 2
    width = grad.shape[1]
    half = grad.shape[0] // count // 2
    blocks = grad.reshape(count, 2, half, width)
    mine = lax.dynamic_index_in_dim(blocks, core, 1, keepdims=False)
    away = lax.dynamic_index_in_dim(blocks, 1 - core, 1, keepdims=False)
    return (mine.astype(F32) + swap_cores(away).astype(F32)).astype(BF16)


def sum_near(paired):
    count, half, width = paired.shape
    if count != 4:
        return plain_scatter_sum(paired, 0).reshape(half, width).astype(BF16)
    own, one, two, far = (part.reshape(half, width) for part in split_parts(paired, 0))
    total = own.astype(F32)
    for flip, sent in ((1, one), (2, two), (3, far)):
        total = total + flip_shard(sent, flip).astype(F32)
    return total.astype(BF16)


def sum_far(local):
    layers = lax.axis_size("expert") // 2
    core = lax.axis_index("expert") % 2
    if layers != 4:
        groups = [[2 * i + side for i in range(layers)] for side in range(2)]
        total = lax.psum(local, "expert", axis_index_groups=groups)
    else:
        half = local.shape[0] // 2
        low, high = local[:half], local[half:]
        for order in ((1, 3), (3, 1)):
            low, high = (
                (low.astype(F32) + flip_layer(low, order[0]).astype(F32)).astype(BF16),
                (high.astype(F32) + flip_layer(high, order[1]).astype(F32)).astype(BF16),
            )
        total = jnp.concatenate([low, high], axis=0)
    other = swap_cores(total)
    low = jnp.where(core == 0, total, other)
    high = jnp.where(core == 0, other, total)
    return jnp.concatenate([low, high], axis=0).astype(F32)


def expert_kernel(sources, arrays, place_ref, x_ref, dy_ref, mask_ref, router_ref, *refs):
    pieces = refs[:arrays]
    out_ref, row_ref, act_ref, gate_ref, up_ref, score_ref, gu, down, sem = refs[arrays:]
    local, rows, width = pieces[0].shape
    third = rows // 3
    hidden = width // 2
    count = len(sources[0])

    @pl.when(pl.program_id(0) == 0)
    def _():
        copies = []
        for j in range(local):
            for number, (array, index, slot) in enumerate(sources[j]):
                at = place_ref[slot]
                copies.append(
                    pltpu.make_async_copy(
                        pieces[array].at[index, pl.ds(0, 2 * third), :],
                        gu.at[j, pl.ds(pl.multiple_of(at * (2 * third), 16), 2 * third), :],
                        sem.at[j, number, 0],
                    )
                )
                copies.append(
                    pltpu.make_async_copy(
                        pieces[array].at[index, pl.ds(2 * third, third), :],
                        down.at[j, pl.ds(pl.multiple_of(at * third, 16), third), :],
                        sem.at[j, number, 1],
                    )
                )
        for copy in copies:
            copy.start()
        for copy in copies:
            copy.wait()

    x = x_ref[...]
    tile = x.shape[0]
    dy = dy_ref[...].reshape(tile, width)
    mask = mask_ref[...].reshape(tile, LANES)
    lane = lax.broadcasted_iota(jnp.int32, (tile, LANES), 1)
    logits = jnp.where(mask > 0, jnp.dot(x, router_ref[...], preferred_element_type=F32), -1e30)
    powers = jnp.exp(logits - jnp.max(logits, axis=1, keepdims=True))
    chances = powers / jnp.sum(powers, axis=1, keepdims=True)
    out = None
    row = None
    scores = jnp.zeros((tile, LANES), F32)
    for j in range(local):
        own = place_ref[count] * local + j
        gate = jnp.sum(jnp.where(lane == own, chances, 0.0), axis=1, keepdims=True)
        left = gu[j, :, :hidden]
        right = gu[j, :, hidden:]
        back = down[j]
        gate_val = jnp.dot(x, left, preferred_element_type=F32)
        up_val = jnp.dot(x, right, preferred_element_type=F32)
        inner_grad = product_transposed_right(dy, back)
        sigmoid = 0.5 + 0.5 * jnp.tanh(0.5 * gate_val)
        swish = gate_val * sigmoid
        inner = (swish * up_val).astype(BF16).astype(F32)
        score = jnp.sum(inner * inner_grad, axis=1, keepdims=True)
        scores = jnp.where(lane == j, score, scores)
        act = (gate * inner).astype(BF16)
        scaled = gate * inner_grad
        gate_back = (scaled * up_val * (sigmoid + swish * (1.0 - sigmoid))).astype(BF16)
        up_back = (scaled * swish).astype(BF16)
        act_ref[:, j * hidden : (j + 1) * hidden] = act
        gate_ref[:, j * hidden : (j + 1) * hidden] = gate_back
        up_ref[:, j * hidden : (j + 1) * hidden] = up_back
        part = jnp.dot(act, back, preferred_element_type=F32)
        out = part if out is None else out + part
        part = product_transposed_right(gate_back, left) + product_transposed_right(up_back, right)
        row = part if row is None else row + part
    out_ref[...] = out.astype(BF16)
    row_ref[...] = row.astype(BF16)
    score_ref[...] = scores


def run_experts(every_x, every_dy, mask, router, weights, chunk):
    arrays, sources, places = weights
    count = len(sources[0])
    total, width = every_x.shape
    local, rows, _ = arrays[0].shape
    third = rows // 3
    peers = every_dy.shape[0]
    rows_each = total // peers
    group = 2
    tile = group * rows_each
    place = jnp.stack([*places, lax.axis_index("expert")]).astype(jnp.int32)
    block = pl.BlockSpec((tile, width), lambda i, p: (i, 0))
    thin = pl.BlockSpec((tile, LANES), lambda i, p: (i, 0))
    return pl.pallas_call(
        functools.partial(expert_kernel, sources, len(arrays)),
        grid_spec=pltpu.PrefetchScalarGridSpec(
            num_scalar_prefetch=1,
            grid=(peers // group,),
            in_specs=[
                block,
                pl.BlockSpec((group, rows_each, width), lambda i, p: (i, chunk, 0)),
                pl.BlockSpec((group, rows_each, LANES), lambda i, p: (i, chunk, 0)),
                pl.BlockSpec((width, LANES), lambda i, p: (0, 0)),
            ]
            + [pl.BlockSpec(memory_space=pl.ANY)] * len(arrays),
            out_specs=[block, block, block, block, block, thin],
            scratch_shapes=[
                pltpu.VMEM((local, 2 * third * count, width), BF16),
                pltpu.VMEM((local, third * count, width), BF16),
                pltpu.SemaphoreType.DMA((local, count, 2)),
            ],
        ),
        out_shape=[jax.ShapeDtypeStruct((total, width), BF16)] * 5
        + [jax.ShapeDtypeStruct((total, LANES), F32)],
        compiler_params=pltpu.CompilerParams(vmem_limit_bytes=VMEM_LIMIT),
        cost_estimate=pl.CostEstimate(
            flops=2 * total * width * width * 6, bytes_accessed=total * width * 14, transcendentals=0
        ),
        name="experts",
    )(place, every_x, every_dy, mask, router, *arrays)


def columns_kernel(chunks, local, *refs):
    xs, gates, ups = refs[:chunks], refs[chunks : 2 * chunks], refs[2 * chunks : 3 * chunks]
    out_ref = refs[3 * chunks]
    hidden = out_ref.shape[2] // 2
    for j in range(local):
        for side, values in ((0, gates), (1, ups)):
            total = None
            for x_ref, value_ref in zip(xs, values):
                part = product_tn(x_ref[...], value_ref[:, j * hidden : (j + 1) * hidden])
                total = part if total is None else total + part
            out_ref[j, :, side * hidden : (side + 1) * hidden] = total.astype(BF16)


def gate_up_gradient(xs, gates, ups, local):
    rows, width = xs[0].shape
    chunks = len(xs)
    piece = width // 4
    whole = pl.BlockSpec((rows, width), lambda i: (0, 0), pipeline_mode=pl.Buffered(1))
    return pl.pallas_call(
        functools.partial(columns_kernel, chunks, local),
        grid=(4,),
        in_specs=[pl.BlockSpec((rows, piece), lambda i: (0, i))] * chunks + [whole] * (2 * chunks),
        out_specs=pl.BlockSpec((local, piece, width), lambda i: (0, i, 0)),
        out_shape=jax.ShapeDtypeStruct((local, width, width), BF16),
        compiler_params=pltpu.CompilerParams(vmem_limit_bytes=VMEM_LIMIT),
        cost_estimate=pl.CostEstimate(
            flops=4 * chunks * rows * width * width, bytes_accessed=chunks * rows * width * 6, transcendentals=0
        ),
        name="gate_up_gradient",
    )(*xs, *gates, *ups)


def down_kernel(chunks, *refs):
    total = None
    for act_ref, dy_ref in zip(refs[:chunks], refs[chunks : 2 * chunks]):
        dy = dy_ref[...].reshape(act_ref.shape[0], dy_ref.shape[2])
        part = product_tn(act_ref[...], dy)
        total = part if total is None else total + part
    refs[2 * chunks][...] = total.astype(BF16)


def down_gradient(acts, every_dy, local):
    rows, width = acts[0].shape
    chunks = len(acts)
    peers = every_dy.shape[0]
    piece = width // 4

    def spec(chunk):
        return pl.BlockSpec(
            (peers, rows // peers, width),
            lambda i: (0, chunk, 0),
            pipeline_mode=pl.Buffered(1),
        )

    return pl.pallas_call(
        functools.partial(down_kernel, chunks),
        grid=(4,),
        in_specs=[pl.BlockSpec((rows, piece), lambda i: (0, i))] * chunks
        + [spec(chunk) for chunk in range(chunks)],
        out_specs=pl.BlockSpec((piece, width), lambda i: (i, 0)),
        out_shape=jax.ShapeDtypeStruct((width, width), BF16),
        compiler_params=pltpu.CompilerParams(vmem_limit_bytes=VMEM_LIMIT),
        cost_estimate=pl.CostEstimate(
            flops=2 * chunks * rows * width * width, bytes_accessed=chunks * rows * width * 4, transcendentals=0
        ),
        name="down_gradient",
    )(*acts, *([every_dy] * chunks)).reshape(local, width // local, width)


def row_copies(place_ref, pieces, target, sem):
    copies = []
    for i, piece in enumerate(pieces):
        rows = piece.shape[0]
        first = pl.multiple_of(place_ref[i], 16)
        copies.append(
            pltpu.make_async_copy(piece, target.at[pl.ds(first, rows), :], sem.at[i])
        )
    for copy in copies:
        copy.start()
    return copies


def scale_of(values):
    return lax.rsqrt(jnp.mean(values * values, axis=-1, keepdims=True) + 1e-06)


def rotate(values, cosine, sine):
    lane = lax.broadcasted_iota(jnp.int32, values.shape, 1) % HEAD_DIM
    half = HEAD_DIM // 2
    turned = jnp.where(
        lane < half, pltpu.roll(values, LANES - half, 1), pltpu.roll(values, half, 1)
    )
    return values * cosine + turned * sine


def project_kernel(count, experts, place_ref, x_ref, cos_ref, sin_ref, *refs):
    pieces = refs[:count]
    normed_ref, q_ref, k_ref, v_ref, gains_ref, router_ref, weight, sem = refs[count:]
    copies = row_copies(place_ref, pieces, weight, sem)
    x = x_ref[...].astype(F32)
    scaled = x * scale_of(x)
    cosine, sine = cos_ref[...], sin_ref[...]
    for copy in copies:
        copy.wait()
    q_width, kv_width = q_ref.shape[1], k_ref.shape[1]
    small = weight[:, q_width + 2 * kv_width :]
    lane = lax.broadcasted_iota(jnp.int32, small.shape, 1)
    router_ref[...] = jnp.where(lane < experts, small.astype(F32), 0.0).astype(BF16)
    turned = small.astype(F32).T
    gains_ref[...] = jnp.concatenate(
        [turned[experts : experts + 2], jnp.zeros((6, turned.shape[1]), F32)], axis=0
    )
    normed = (scaled * turned[experts : experts + 1]).astype(BF16)
    normed_ref[...] = normed
    for first in range(0, q_width, 256):
        values = jnp.dot(normed, weight[:, first : first + 256], preferred_element_type=F32)
        for part in (0, LANES):
            q_ref[:, first + part : first + part + LANES] = rotate(
                values[:, part : part + LANES], cosine, sine
            ).astype(BF16)
    for first in range(0, kv_width, 256):
        at = q_width + first
        values = jnp.dot(normed, weight[:, at : at + 256], preferred_element_type=F32)
        for part in (0, LANES):
            k_ref[:, first + part : first + part + LANES] = rotate(
                values[:, part : part + LANES], cosine, sine
            ).astype(BF16)
    at = q_width + kv_width
    v_ref[...] = jnp.dot(
        normed, weight[:, at : at + kv_width], preferred_element_type=F32
    ).astype(BF16)


def simple_call(kernel, name, prefetch, inputs, pieces, outputs, scratch, time):
    def whole(shape):
        return pl.BlockSpec(shape, lambda i, p: (0,) * len(shape))

    return pl.pallas_call(
        kernel,
        grid_spec=pltpu.PrefetchScalarGridSpec(
            num_scalar_prefetch=1,
            grid=(1,),
            in_specs=[whole(value.shape) for value in inputs]
            + [pl.BlockSpec(memory_space=pl.ANY)] * len(pieces),
            out_specs=[whole(shape) for shape, _ in outputs],
            scratch_shapes=scratch,
        ),
        out_shape=[jax.ShapeDtypeStruct(shape, kind) for shape, kind in outputs],
        compiler_params=pltpu.CompilerParams(vmem_limit_bytes=VMEM_LIMIT),
        cost_estimate=cost(time),
        name=name,
    )(prefetch, *inputs, *pieces)


def key_window(tile, size, rows):
    low = max(0, tile * size - (rows // 2 - 1)) // size * size
    return low, (tile + 1) * size


def tile_mask(start_ref, low, high, first, size):
    shape = (high - low, size)
    key = lax.broadcasted_iota(jnp.int32, shape, 0) + low
    query = lax.broadcasted_iota(jnp.int32, shape, 1) + first
    seen = (key >= start_ref[:, first : first + size]) & (key <= query)
    return jnp.concatenate([seen, seen], axis=1)


def two_heads(values):
    return jnp.concatenate([values[:, :HEAD_DIM], values[:, HEAD_DIM:]], axis=0)


def untwo(values):
    size = values.shape[1] // 2
    return jnp.concatenate([values[:, :size], values[:, size:]], axis=0).T


def attend_kernel(start_ref, q_ref, k_ref, v_ref, out_ref, log_ref):
    rows = q_ref.shape[0]
    size = LANES
    scale = 1.0 / math.sqrt(HEAD_DIM)
    logs = [[], []]
    for tile in range(rows // size):
        low, high = key_window(tile, size, rows)
        first = tile * size
        seen = tile_mask(start_ref, low, high, first, size)
        for pair in range(2):
            q = two_heads(q_ref[first : first + size, pair * LANES : (pair + 1) * LANES])
            q = (q.astype(F32) * scale).astype(BF16)
            at = pair * HEAD_DIM
            scores = product_transposed_right(k_ref[low:high, at : at + HEAD_DIM], q)
            scores = jnp.where(seen, scores, -1e30)
            top = jnp.max(scores, axis=0, keepdims=True)
            powers = jnp.exp(scores - top)
            total = jnp.sum(powers, axis=0, keepdims=True)
            low_chances = (powers * (1.0 / total)).astype(BF16)
            mixed = product_tn(v_ref[low:high, at : at + HEAD_DIM], low_chances)
            out_ref[first : first + size, pair * LANES : (pair + 1) * LANES] = untwo(mixed).astype(
                BF16
            )
            logs[pair].append(top + jnp.log(total))
    lines = []
    for pair in range(2):
        for head in range(2):
            lines.append(
                jnp.concatenate([v[:, head * size : (head + 1) * size] for v in logs[pair]], axis=1)
            )
    log_ref[...] = jnp.concatenate(lines + [jnp.zeros((4, rows), F32)], axis=0)


def attend_back_kernel(
    start_ref, q_ref, k_ref, v_ref, grad_ref, log_ref, cos_ref, sin_ref, qb_ref, kb_ref, vb_ref
):
    rows = q_ref.shape[0]
    size = LANES
    tiles = rows // size
    scale = 1.0 / math.sqrt(HEAD_DIM)
    key_sums = [[None] * tiles, [None] * tiles]
    value_sums = [[None] * tiles, [None] * tiles]

    def add(sums, low, part):
        for i in range(part.shape[0] // size):
            piece = part[i * size : (i + 1) * size]
            at = low // size + i
            sums[at] = piece if sums[at] is None else sums[at] + piece

    for tile in range(tiles):
        low, high = key_window(tile, size, rows)
        first = tile * size
        seen = tile_mask(start_ref, low, high, first, size)
        cosine, sine = cos_ref[first : first + size], sin_ref[first : first + size]
        for pair in range(2):
            lanes = slice(pair * LANES, (pair + 1) * LANES)
            q = two_heads(q_ref[first : first + size, lanes])
            q = (q.astype(F32) * scale).astype(BF16)
            grad = two_heads(grad_ref[first : first + size, lanes])
            at = pair * HEAD_DIM
            keys = k_ref[low:high, at : at + HEAD_DIM]
            scores = jnp.where(seen, product_transposed_right(keys, q), -1e30)
            log_total = jnp.concatenate(
                [
                    log_ref[2 * pair : 2 * pair + 1, first : first + size],
                    log_ref[2 * pair + 1 : 2 * pair + 2, first : first + size],
                ],
                axis=1,
            )
            chances = jnp.exp(scores - log_total)
            chance_grad = product_transposed_right(v_ref[low:high, at : at + HEAD_DIM], grad)
            mean = jnp.sum(chances * chance_grad, axis=0, keepdims=True)
            score_grad = (chances * (chance_grad - mean)).astype(BF16)
            add(value_sums[pair], low, jnp.dot(chances.astype(BF16), grad, preferred_element_type=F32))
            add(key_sums[pair], low, jnp.dot(score_grad, q, preferred_element_type=F32))
            query_grad = untwo(product_tn(keys, score_grad)) * scale
            qb_ref[first : first + size, lanes] = rotate(query_grad, cosine, -sine).astype(BF16)
    for tile in range(tiles):
        here = slice(tile * size, (tile + 1) * size)
        both = jnp.concatenate([key_sums[0][tile], key_sums[1][tile]], axis=1)
        kb_ref[here, :] = rotate(both, cos_ref[here], -sin_ref[here]).astype(BF16)
        both = jnp.concatenate([value_sums[0][tile], value_sums[1][tile]], axis=1)
        vb_ref[here, :] = both.astype(BF16)


def attention_specs(rows):
    return (
        pl.BlockSpec((1, rows), lambda i: (0, 0)),
        pl.BlockSpec((rows, 2 * LANES), lambda i: (0, i)),
        pl.BlockSpec((rows, LANES), lambda i: (0, i)),
        pl.BlockSpec((8, rows), lambda i: (i, 0)),
        pl.BlockSpec((rows, LANES), lambda i: (0, 0)),
    )


def attend(start, q, k, v):
    rows = q.shape[0]
    one, wide, thin, line, _ = attention_specs(rows)
    steps = k.shape[1] // LANES
    return pl.pallas_call(
        attend_kernel,
        grid=(steps,),
        in_specs=[one, wide, thin, thin],
        out_specs=[wide, line],
        out_shape=[
            jax.ShapeDtypeStruct(q.shape, BF16),
            jax.ShapeDtypeStruct((8 * steps, rows), F32),
        ],
        compiler_params=pltpu.CompilerParams(vmem_limit_bytes=VMEM_LIMIT),
        cost_estimate=cost(13),
        name="attend",
    )(start, q, k, v)


def attend_back(start, q, k, v, grad, logs, cosine, sine):
    rows = q.shape[0]
    one, wide, thin, line, table = attention_specs(rows)
    return pl.pallas_call(
        attend_back_kernel,
        grid=(k.shape[1] // LANES,),
        in_specs=[one, wide, thin, thin, wide, line, table, table],
        out_specs=[wide, thin, thin],
        out_shape=[
            jax.ShapeDtypeStruct(q.shape, BF16),
            jax.ShapeDtypeStruct(k.shape, BF16),
            jax.ShapeDtypeStruct(v.shape, BF16),
        ],
        compiler_params=pltpu.CompilerParams(vmem_limit_bytes=VMEM_LIMIT),
        cost_estimate=cost(15),
        name="attend_back",
    )(start, q, k, v, grad, logs, cosine, sine)


def mix_kernel(count, place_ref, attended_ref, x_ref, mask_ref, router_ref, gains_ref, *refs):
    pieces = refs[:count]
    state_ref, low_ref, high_ref, gates_ref, weight, sem = refs[count:]
    copies = row_copies(place_ref, pieces, weight, sem)
    for copy in copies:
        copy.wait()
    state = x_ref[...].astype(F32) + jnp.dot(
        attended_ref[...], weight[...], preferred_element_type=F32
    )
    state_ref[...] = state
    mixed = (state * scale_of(state) * gains_ref[1:2, :]).astype(BF16)
    low_ref[...] = mixed[: low_ref.shape[0]]
    high_ref[...] = mixed[low_ref.shape[0] :]
    logits = jnp.dot(mixed, router_ref[...], preferred_element_type=F32)
    logits = jnp.where(mask_ref[...] > 0, logits, -1e30)
    powers = jnp.exp(logits - jnp.max(logits, axis=1, keepdims=True))
    gates_ref[...] = powers / jnp.sum(powers, axis=1, keepdims=True)


def mix_back_kernel(
    count,
    chunks,
    experts,
    place_ref,
    attended_ref,
    state_ref,
    low_ref,
    high_ref,
    dy_ref,
    gates_ref,
    gate_grad_ref,
    router_ref,
    gains_ref,
    *refs,
):
    sums = refs[:chunks]
    pieces = refs[chunks : chunks + count]
    state_grad_ref, attended_grad_ref, pack_ref, weight, sem = refs[chunks + count :]
    copies = row_copies(place_ref, pieces, weight, sem)
    gates = gates_ref[...]
    gate_grad = gate_grad_ref[...]
    logit_grad = (
        gates * (gate_grad - jnp.sum(gates * gate_grad, axis=1, keepdims=True))
    ).astype(BF16)
    rows = jnp.concatenate([part[...] for part in sums], axis=0).astype(F32)
    mixed_grad = product_transposed_right(logit_grad, router_ref[...]) + rows
    state = state_ref[...]
    scale = scale_of(state)
    gain_grad = jnp.sum(mixed_grad * (state * scale), axis=0, keepdims=True)
    scaled = gains_ref[1:2, :] * mixed_grad
    mean = jnp.mean(scaled * state, axis=1, keepdims=True)
    state_grad = dy_ref[...].astype(F32) + scale * scaled - state * (scale * scale * scale * mean)
    state_grad_ref[...] = state_grad
    branch = state_grad.astype(BF16)
    for copy in copies:
        copy.wait()
    attended_grad_ref[...] = product_transposed_right(branch, weight[...]).astype(BF16)
    width = state.shape[1]
    pack_ref[:, :width] = product_tn(attended_ref[...], branch).astype(BF16)
    line = lax.broadcasted_iota(jnp.int32, (LANES, width), 0)
    column = jnp.where(line == experts, gain_grad, 0.0).T
    pack_ref[:, width:] = (product_tn(jnp.concatenate([low_ref[...], high_ref[...]], axis=0), logit_grad) + column).astype(BF16)


def project_weights_kernel(place_ref, normed_ref, qb_ref, kb_ref, vb_ref, pack_ref):
    normed = normed_ref[...]
    at = 0
    for back_ref in (qb_ref, kb_ref, vb_ref):
        width = back_ref.shape[1]
        pack_ref[:, at : at + width] = product_tn(normed, back_ref[...]).astype(BF16)
        at += width


def project_back_kernel(
    count, place_ref, x_ref, state_grad_ref, gains_ref, qb_ref, kb_ref, vb_ref, *refs
):
    pieces = refs[:count]
    out_ref, weight, sem = refs[count:]
    copies = row_copies(place_ref, pieces, weight, sem)
    for copy in copies:
        copy.wait()
    grad = None
    first = 0
    for back_ref in (qb_ref, kb_ref, vb_ref):
        width = back_ref.shape[1]
        part = product_transposed_right(back_ref[...], weight[:, first : first + width])
        grad = part if grad is None else grad + part
        first += width
    x = x_ref[...].astype(F32)
    scale = scale_of(x)
    scaled = gains_ref[0:1, :] * grad
    mean = jnp.mean(scaled * x, axis=1, keepdims=True)
    out_ref[...] = (
        state_grad_ref[...] + scale * scaled - x * (scale * scale * scale * mean)
    ).astype(BF16)


def per_device(
    tokens,
    gain_attn,
    w_query,
    key_weight,
    value_weight,
    w_out,
    gain_mix,
    router,
    w_gate,
    w_up,
    w_down,
    routes,
    lengths,
    cotangent,
):
    total_rows, model_width = tokens.shape
    experts = router.shape[1]
    local_experts, _, hidden = w_gate.shape
    peers = lax.axis_size("expert")
    part_rows, q_width = w_query.shape
    kv_width = key_weight.shape[1]
    first_width = q_width + 2 * kv_width + LANES

    small = jnp.concatenate(
        [
            router,
            gain_attn[:, None],
            gain_mix[:, None],
            jnp.zeros((part_rows, LANES - experts - 2), BF16),
        ],
        axis=1,
    )
    first_pieces, first_places = fetch_rows(
        jnp.concatenate([w_query, key_weight, value_weight, small], axis=1)
    )
    expert_ids = jnp.arange(experts, dtype=jnp.int32)
    chosen = jnp.any(routes[:, :, None] == expert_ids[None, None, :], axis=1).astype(BF16)
    mask_rows = total_rows * experts // model_width
    mask_space = -(-mask_rows // 16) * 16
    every_dy = lax.all_gather(
        jnp.concatenate(
            [
                cotangent,
                jnp.pad(
                    chosen.reshape(mask_rows, model_width), ((0, mask_space - mask_rows), (0, 0))
                ),
            ],
            axis=0,
        ),
        "expert",
        axis=0,
    )
    every_mask = jnp.pad(
        every_dy[:, total_rows : total_rows + mask_rows].reshape(peers, total_rows, experts),
        ((0, 0), (0, 0), (0, LANES - experts)),
    )
    own_mask = jnp.pad(chosen, ((0, 0), (0, LANES - experts)))

    doc_ends = jnp.cumsum(lengths[0])
    token_index = jnp.arange(total_rows, dtype=jnp.int32)
    past_end = token_index[:, None] >= doc_ends[None, :]
    doc_start = jnp.sum(jnp.where(past_end, lengths[0][None, :], 0), axis=1)
    position = (token_index - doc_start).astype(F32)
    half_head = HEAD_DIM // 2
    inverse = 10000.0 ** (-(jnp.arange(half_head, dtype=F32) * 2.0 / HEAD_DIM))
    angles = position[:, None] * inverse[None, :]
    cosine, sine = jnp.cos(angles), jnp.sin(angles)
    cosine = jnp.concatenate([cosine] * (LANES // half_head), axis=1)
    sine = jnp.concatenate([-sine, sine] * (LANES // HEAD_DIM), axis=1)
    start = doc_start[None, :].astype(jnp.int32)

    normed, q, k, v, gains, router_lanes = simple_call(
        functools.partial(project_kernel, len(first_pieces), experts),
        "project",
        first_places,
        [tokens, cosine, sine],
        first_pieces,
        [
            (tokens.shape, BF16),
            ((total_rows, q_width), BF16),
            ((total_rows, kv_width), BF16),
            ((total_rows, kv_width), BF16),
            ((8, model_width), F32),
            ((model_width, LANES), BF16),
        ],
        [
            pltpu.VMEM((model_width, first_width), BF16),
            pltpu.SemaphoreType.DMA((len(first_pieces),)),
        ],
        8,
    )
    out_pieces, out_places = fetch_rows(w_out, first_pieces[-1], normed)
    attended, logs = attend(start, q, k, v)
    state, mixed_low, mixed_high, gates = simple_call(
        functools.partial(mix_kernel, len(out_pieces)),
        "mix",
        out_places,
        [attended, tokens, own_mask, router_lanes, gains],
        out_pieces,
        [
            (tokens.shape, F32),
            ((total_rows // 2, model_width), BF16),
            ((total_rows // 2, model_width), BF16),
            ((total_rows, LANES), F32),
        ],
        [
            pltpu.VMEM((q_width, model_width), BF16),
            pltpu.SemaphoreType.DMA((len(out_pieces),)),
        ],
        7,
    )

    packed = jnp.concatenate([jnp.concatenate([w_gate, w_up], axis=2), w_down], axis=1)
    weights = fetch_experts(packed, out_pieces[1:2], mixed_low)
    every_x, out_part, row_part, act, gate_back, up_back, scores_part = [], [], [], [], [], [], []
    for chunk, mixed in enumerate((mixed_low, mixed_high)):
        gathered = lax.all_gather(mixed, "expert", axis=0, tiled=True)
        results = run_experts(gathered, every_dy, every_mask, router_lanes, weights, chunk)
        every_x.append(gathered)
        for kept, result in zip((out_part, row_part, act, gate_back, up_back, scores_part), results):
            kept.append(result)
    row_sum = [
        lax.psum_scatter(rows, "expert", scatter_dimension=0, tiled=True) for rows in row_part
    ]
    sent_scores = jnp.concatenate(
        [values[:, :local_experts].reshape(peers, -1, LANES) for values in scores_part], axis=1
    )
    gate_grad = lax.all_to_all(sent_scores, "expert", split_axis=0, concat_axis=0, tiled=True)
    gate_grad = (
        gate_grad.reshape(peers, total_rows, local_experts)
        .transpose(1, 0, 2)
        .reshape(total_rows, experts)
    )
    down_grad = down_gradient(act, every_dy, local_experts)
    gu_grad = gate_up_gradient(every_x, gate_back, up_back, local_experts)
    four = lax.axis_size("shard") == 4 and local_experts % 2 == 0
    if four:
        gu_own, gu_one, gu_two, gu_far = split_parts(gu_grad, 1)
        gu_low, gu_high = send_far(gu_far)
        (row_sum, gate_grad, down_grad, gu_own, gu_one, gu_two, gu_low, gu_high) = (
            lax.optimization_barrier(
                (row_sum, gate_grad, down_grad, gu_own, gu_one, gu_two, gu_low, gu_high)
            )
        )
        gu_one, gu_two = send_near(gu_one, gu_two, gu_low, gu_high)
    else:
        row_sum, gate_grad, gu_grad, down_grad = lax.optimization_barrier(
            (row_sum, gate_grad, gu_grad, down_grad)
        )
    out_part, _ = lax.optimization_barrier((out_part, row_sum[-1]))
    out_sum = [lax.psum_scatter(rows, "expert", scatter_dimension=0, tiled=True) for rows in out_part]

    state_grad, attended_grad, pack = simple_call(
        functools.partial(mix_back_kernel, len(out_pieces), 2, experts),
        "mix_back",
        out_places,
        [
            attended,
            state,
            mixed_low,
            mixed_high,
            cotangent,
            gates,
            jnp.pad(gate_grad, ((0, 0), (0, LANES - experts))),
            router_lanes,
            gains,
            *row_sum,
        ],
        out_pieces,
        [
            (tokens.shape, F32),
            ((total_rows, q_width), BF16),
            ((q_width, model_width + LANES), BF16),
        ],
        [
            pltpu.VMEM((q_width, model_width), BF16),
            pltpu.SemaphoreType.DMA((len(out_pieces),)),
        ],
        10,
    )
    backs = attend_back(start, q, k, v, attended_grad, logs, cosine, sine)
    early = sum_near(pair_cores(pack))
    (late_pack,) = simple_call(
        project_weights_kernel,
        "project_weights",
        first_places,
        [normed, *backs],
        [],
        [((model_width, first_width - LANES), BF16)],
        [],
        6,
    )
    late = pair_cores(late_pack)
    if four:
        late, early, gu_one, gu_two = lax.optimization_barrier((late, early, gu_one, gu_two))
    backs, state_grad, late, down_grad = lax.optimization_barrier(
        (backs, state_grad, late, down_grad)
    )
    late = sum_near(late)
    if four:
        down_own, down_one, down_two, down_far = split_parts(down_grad, 1)
        down_low, down_high = send_far(down_far)
    (input_grad,) = simple_call(
        functools.partial(project_back_kernel, len(first_pieces)),
        "project_back",
        first_places,
        [tokens, state_grad, gains, *backs],
        first_pieces,
        [(tokens.shape, BF16)],
        [
            pltpu.VMEM((model_width, first_width), BF16),
            pltpu.SemaphoreType.DMA((len(first_pieces),)),
        ],
        7,
    )
    late, early, input_grad = lax.optimization_barrier((late, early, input_grad))
    if four:
        down_low, down_high, _ = lax.optimization_barrier((down_low, down_high, late))
        down_one, down_two = send_near(down_one, down_two, down_low, down_high)
        gu_parts, state, _ = lax.optimization_barrier(((gu_own, gu_one, gu_two), state, late))
        gu_sum, expert_down_sum = add_up(gu_parts), add_up((down_own, down_one, down_two))
    else:
        expert_down_sum = plain_scatter_sum(down_grad, 1)
        gu_sum = plain_scatter_sum(gu_grad, 1)
    expert_gate_sum = gu_sum[:, :, :hidden]
    expert_up_sum = gu_sum[:, :, hidden:]
    whole = sum_far(jnp.concatenate([late, early], axis=1))
    late, early = whole[:, : late.shape[1]], whole[:, late.shape[1] :]
    output = state + jnp.concatenate(out_sum, axis=0).astype(F32)
    projections = (
        (w_query, late[:, :q_width]),
        (key_weight, late[:, q_width : q_width + kv_width]),
        (value_weight, late[:, q_width + kv_width :]),
    )
    gain_sum = add_up(
        jnp.sum(weight.astype(F32) * grad, axis=1) for weight, grad in projections
    ) / gain_attn.astype(F32)
    q_end = q_width
    return (
        output.astype(BF16),
        input_grad,
        gain_sum,
        late[:, :q_end],
        late[:, q_end : q_end + kv_width],
        late[:, q_end + kv_width : q_end + 2 * kv_width],
        early[:, :model_width],
        early[:, model_width + experts],
        early[:, model_width : model_width + experts],
        expert_gate_sum,
        expert_up_sum,
        expert_down_sum,
    )


def solution(mesh):
    in_specs = (
        P(("expert", "shard"), None),
        P("shard"),
        P("shard", None),
        P("shard", None),
        P("shard", None),
        P("shard", None),
        P("shard"),
        P("shard", None),
        P("expert", "shard", None),
        P("expert", "shard", None),
        P("expert", "shard", None),
        P(("expert", "shard"), None),
        P(("expert", "shard"), None),
        P(("expert", "shard"), None),
    )
    out_specs = (
        P(("expert", "shard"), None),
        P(("expert", "shard"), None),
        P("shard"),
        P("shard", None),
        P("shard", None),
        P("shard", None),
        P("shard", None),
        P("shard"),
        P("shard", None),
        P("expert", "shard", None),
        P("expert", "shard", None),
        P("expert", "shard", None),
    )
    return jax.shard_map(
        per_device, mesh=mesh, in_specs=in_specs, out_specs=out_specs, check_vma=False
    )
```

```python
import functools
import math

import jax
import jax.numpy as jnp
from jax import lax
from jax.experimental import pallas as pl
from jax.experimental.pallas import tpu as pltpu
from jax.sharding import PartitionSpec as P

QUERY_HEADS = 16
KEY_VALUE_HEADS = 8
HEAD_DIM = 64
LANES = 128
VMEM_LIMIT = 58 * 1024 * 1024


def cost(microseconds):
    return pl.CostEstimate(
        flops=int(microseconds * 1.15e9), bytes_accessed=0, transcendentals=0
    )


F32 = jnp.float32
BF16 = jnp.bfloat16


def matrix_product(left_side, right_side):
    return jnp.dot(left_side, right_side, preferred_element_type=jnp.float32)


def product_tn(left_side, right_side):
    return lax.dot_general(
        left_side, right_side, (((0,), (0,)), ((), ())), preferred_element_type=jnp.float32
    )


def product_transposed_right(left_side, right_side):
    return lax.dot_general(
        left_side, right_side, (((1,), (1,)), ((), ())), preferred_element_type=jnp.float32
    )


def pick(blocks, index):
    return lax.dynamic_index_in_dim(blocks, index, 0, keepdims=False)


def flip_shard(value, flip):
    return lax.ppermute(value, "shard", [(i, i ^ flip) for i in range(4)])


def flip_layer(value, flip):
    size = lax.axis_size("expert")
    return lax.ppermute(value, "expert", [(i, i ^ (2 * flip)) for i in range(size)])


def swap_cores(value):
    size = lax.axis_size("expert")
    return lax.ppermute(value, "expert", [(i, i ^ 1) for i in range(size)])


def both_ways(value, first, second, after=None):
    half = value.shape[0] // 2
    one, two = first(value), second(value)
    if after is not None:
        one, two, _ = lax.optimization_barrier((one, two, after))
    return one, two, first(two[:half]), second(one[half:])


def fetch_rows(rows, before_first=None, before_second=None):
    count = lax.axis_size("shard")
    size = rows.shape[0]
    if count != 4:
        return [lax.all_gather(rows, "shard", axis=0, tiled=True)], jnp.zeros((1,), jnp.int32)
    me = lax.axis_index("shard")
    core = lax.axis_index("expert") % 2
    half = size // 2
    mine = lax.dynamic_slice_in_dim(rows, core * half, half, 0)
    if before_first is not None:
        mine, _ = lax.optimization_barrier((mine, before_first))
    one, two, low, high = both_ways(
        mine, lambda v: flip_shard(v, 1), lambda v: flip_shard(v, 2), before_second
    )
    pieces, places = [rows], [me * size]
    for got, flip, skip in ((one, 1, 0), (two, 2, 0), (low, 3, 0), (high, 3, half // 2)):
        first = (me ^ flip) * size + skip
        pieces += [got, swap_cores(got)]
        places += [first + core * half, first + (1 - core) * half]
    return pieces, jnp.stack(places).astype(jnp.int32)


def fetch_experts(packed, before_first, before_second):
    count = lax.axis_size("shard")
    local = packed.shape[0]
    if count != 4 or local != 2:
        every = lax.all_gather(packed, "shard", axis=0)
        arrays = [every[i] for i in range(count)]
        sources = [[(i, j, i) for i in range(count)] for j in range(local)]
        return arrays, sources, [jnp.int32(i) for i in range(count)]
    me = lax.axis_index("shard")
    sent, _ = lax.optimization_barrier((packed, before_first))
    one, two, low, high = both_ways(
        sent, lambda v: flip_shard(v, 1), lambda v: flip_shard(v, 2), before_second
    )
    arrays = [packed, one, two, low, high]
    sources = [[(0, j, 0), (1, j, 1), (2, j, 2), (3 + j, 0, 3)] for j in range(2)]
    return arrays, sources, [me, me ^ 1, me ^ 2, me ^ 3]


def split_parts(values, axis):
    me = lax.axis_index("shard")
    size = values.shape[axis] // lax.axis_size("shard")
    return [
        lax.dynamic_slice_in_dim(values, (me ^ flip) * size, size, axis) for flip in range(4)
    ]


def send_far(far):
    half = far.shape[0] // 2
    return flip_shard(far[:half], 1), flip_shard(far[half:], 2)


def join_near(one, two, low, high):
    half = one.shape[0] // 2
    two = jnp.concatenate([(two[:half].astype(F32) + low.astype(F32)).astype(BF16), two[half:]], axis=0)
    one = jnp.concatenate([one[:half], (one[half:].astype(F32) + high.astype(F32)).astype(BF16)], axis=0)
    return one, two


def send_near(one, two):
    return flip_shard(one, 1), flip_shard(two, 2)


def add_up(values):
    return sum(value.astype(F32) for value in values)


def plain_scatter_sum(values, axis):
    return lax.psum_scatter(values, "shard", scatter_dimension=axis, tiled=True).astype(F32)


def pair_cores(grad):
    count = lax.axis_size("shard")
    core = lax.axis_index("expert") % 2
    width = grad.shape[1]
    half = grad.shape[0] // count // 2
    blocks = grad.reshape(count, 2, half, width)
    mine = lax.dynamic_index_in_dim(blocks, core, 1, keepdims=False)
    away = lax.dynamic_index_in_dim(blocks, 1 - core, 1, keepdims=False)
    return (mine.astype(F32) + swap_cores(away).astype(F32)).astype(BF16)


def sum_near(paired, after=None):
    count, half, width = paired.shape
    if count != 4:
        return plain_scatter_sum(paired, 0).reshape(half, width).astype(BF16)
    own, one, two, far = (part.reshape(half, width) for part in split_parts(paired, 0))
    if after is not None:
        own, _ = lax.optimization_barrier((own, after))
    total = own.astype(F32)
    for flip, sent in ((1, one), (2, two), (3, far)):
        total = total + flip_shard(sent, flip).astype(F32)
    return total.astype(BF16)


def sum_far(local, beside, last):
    layers = lax.axis_size("expert") // 2
    core = lax.axis_index("expert") % 2
    if layers != 4:
        groups = [[2 * i + side for i in range(layers)] for side in range(2)]
        total = lax.psum(local, "expert", axis_index_groups=groups)
    else:
        half = local.shape[0] // 2
        low, high = local[:half], local[half:]
        for order in ((1, 3), (3, 1)):
            low, high = (
                (low.astype(F32) + flip_layer(low, order[0]).astype(F32)).astype(BF16),
                (high.astype(F32) + flip_layer(high, order[1]).astype(F32)).astype(BF16),
            )
            if order == (1, 3):
                low, high, beside = lax.optimization_barrier((low, high, beside))
        total = jnp.concatenate([low, high], axis=0)
    total, last = lax.optimization_barrier((total, last))
    other = swap_cores(total)
    low = jnp.where(core == 0, total, other)
    high = jnp.where(core == 0, other, total)
    return jnp.concatenate([low, high], axis=0).astype(F32), beside, last


def expert_kernel(sources, arrays, earlier, place_ref, x_ref, dy_ref, mask_ref, router_ref, *refs):
    pieces, refs = refs[:arrays], refs[earlier:]
    out_ref, row_ref, act_ref, gate_ref, up_ref, score_ref, gu, down, sem = refs[arrays:]
    local, rows, width = pieces[0].shape
    third = rows // 3
    hidden = width // 2
    count = len(sources[0])

    @pl.when(pl.program_id(0) == 0)
    def _():
        copies = []
        for j in range(local):
            for number, (array, index, slot) in enumerate(sources[j]):
                at = place_ref[slot]
                copies.append(
                    pltpu.make_async_copy(
                        pieces[array].at[index, pl.ds(0, 2 * third), :],
                        gu.at[j, pl.ds(pl.multiple_of(at * (2 * third), 16), 2 * third), :],
                        sem.at[j, number, 0],
                    )
                )
                copies.append(
                    pltpu.make_async_copy(
                        pieces[array].at[index, pl.ds(2 * third, third), :],
                        down.at[j, pl.ds(pl.multiple_of(at * third, 16), third), :],
                        sem.at[j, number, 1],
                    )
                )
        for copy in copies:
            copy.start()
        for copy in copies:
            copy.wait()

    x = x_ref[...]
    tile = x.shape[0]
    dy = dy_ref[...].reshape(tile, width)
    mask = mask_ref[...].reshape(tile, LANES)
    lane = lax.broadcasted_iota(jnp.int32, (tile, LANES), 1)
    logits = jnp.where(mask > 0, jnp.dot(x, router_ref[...], preferred_element_type=F32), -1e30)
    powers = jnp.exp(logits - jnp.max(logits, axis=1, keepdims=True))
    chances = powers / jnp.sum(powers, axis=1, keepdims=True)
    out = None
    row = None
    scores = jnp.zeros((tile, LANES), F32)
    for j in range(local):
        own = place_ref[count] * local + j
        gate = jnp.sum(jnp.where(lane == own, chances, 0.0), axis=1, keepdims=True)
        left = gu[j, :, :hidden]
        right = gu[j, :, hidden:]
        back = down[j]
        gate_val = jnp.dot(x, left, preferred_element_type=F32)
        up_val = jnp.dot(x, right, preferred_element_type=F32)
        inner_grad = product_transposed_right(dy, back)
        sigmoid = 0.5 + 0.5 * jnp.tanh(0.5 * gate_val)
        swish = gate_val * sigmoid
        inner = (swish * up_val).astype(BF16).astype(F32)
        score = jnp.sum(inner * inner_grad, axis=1, keepdims=True)
        scores = jnp.where(lane == j, score, scores)
        act = (gate * inner).astype(BF16)
        scaled = gate * inner_grad
        gate_back = (scaled * up_val * (sigmoid + swish * (1.0 - sigmoid))).astype(BF16)
        up_back = (scaled * swish).astype(BF16)
        act_ref[:, j * hidden : (j + 1) * hidden] = act
        gate_ref[:, j * hidden : (j + 1) * hidden] = gate_back
        up_ref[:, j * hidden : (j + 1) * hidden] = up_back
        part = jnp.dot(act, back, preferred_element_type=F32)
        out = part if out is None else out + part
        part = product_transposed_right(gate_back, left) + product_transposed_right(up_back, right)
        row = part if row is None else row + part
    out_ref[...] = out.astype(BF16).reshape(out_ref.shape)
    row_ref[...] = row.astype(BF16)
    score_ref[...] = scores


def run_experts(every_x, every_dy, mask, router, weights, chunk, earlier):
    arrays, sources, places = weights
    count = len(sources[0])
    total, width = every_x.shape
    local, rows, _ = arrays[0].shape
    third = rows // 3
    peers = every_dy.shape[0]
    rows_each = total // peers
    group = 2
    tile = group * rows_each
    place = jnp.stack([*places, lax.axis_index("expert")]).astype(jnp.int32)
    block = pl.BlockSpec((tile, width), lambda i, p: (i, 0))
    thin = pl.BlockSpec((tile, LANES), lambda i, p: (i, 0))
    return pl.pallas_call(
        functools.partial(expert_kernel, sources, len(arrays), len(earlier)),
        grid_spec=pltpu.PrefetchScalarGridSpec(
            num_scalar_prefetch=1,
            grid=(peers // group,),
            in_specs=[
                block,
                pl.BlockSpec((group, rows_each, width), lambda i, p: (i, chunk, 0)),
                pl.BlockSpec((group, rows_each, LANES), lambda i, p: (i, chunk, 0)),
                pl.BlockSpec((width, LANES), lambda i, p: (0, 0)),
            ]
            + [pl.BlockSpec(memory_space=pl.ANY)] * (len(arrays) + len(earlier)),
            out_specs=[
                pl.BlockSpec((group, rows_each, width), lambda i, p: (i, chunk, 0)),
                block,
                block,
                block,
                block,
                thin,
            ],
            scratch_shapes=[
                pltpu.VMEM((local, 2 * third * count, width), BF16),
                pltpu.VMEM((local, third * count, width), BF16),
                pltpu.SemaphoreType.DMA((local, count, 2)),
            ],
        ),
        out_shape=[jax.ShapeDtypeStruct((peers, 2 * rows_each, width), BF16)]
        + [jax.ShapeDtypeStruct((total, width), BF16)] * 4
        + [jax.ShapeDtypeStruct((total, LANES), F32)],
        compiler_params=pltpu.CompilerParams(vmem_limit_bytes=VMEM_LIMIT),
        cost_estimate=pl.CostEstimate(
            flops=2 * total * width * width * 6, bytes_accessed=total * width * 14, transcendentals=0
        ),
        input_output_aliases={5 + len(arrays): 0} if earlier else {},
        name="experts",
    )(place, every_x, every_dy, mask, router, *arrays, *earlier)


def columns_kernel(chunks, local, *refs):
    xs, gates, ups = refs[:chunks], refs[chunks : 2 * chunks], refs[2 * chunks : 3 * chunks]
    out_ref = refs[3 * chunks]
    hidden = out_ref.shape[2] // 2
    for j in range(local):
        for side, values in ((0, gates), (1, ups)):
            total = None
            for x_ref, value_ref in zip(xs, values):
                part = product_tn(x_ref[...], value_ref[:, j * hidden : (j + 1) * hidden])
                total = part if total is None else total + part
            out_ref[j, :, side * hidden : (side + 1) * hidden] = total.astype(BF16)


def gate_up_gradient(xs, gates, ups, local):
    rows, width = xs[0].shape
    chunks = len(xs)
    piece = width // 4
    whole = pl.BlockSpec((rows, width), lambda i: (0, 0), pipeline_mode=pl.Buffered(1))
    return pl.pallas_call(
        functools.partial(columns_kernel, chunks, local),
        grid=(4,),
        in_specs=[pl.BlockSpec((rows, piece), lambda i: (0, i))] * chunks + [whole] * (2 * chunks),
        out_specs=pl.BlockSpec((local, piece, width), lambda i: (0, i, 0)),
        out_shape=jax.ShapeDtypeStruct((local, width, width), BF16),
        compiler_params=pltpu.CompilerParams(vmem_limit_bytes=VMEM_LIMIT),
        cost_estimate=pl.CostEstimate(
            flops=4 * chunks * rows * width * width, bytes_accessed=chunks * rows * width * 6, transcendentals=0
        ),
        name="gate_up_gradient",
    )(*xs, *gates, *ups)


def down_kernel(chunks, *refs):
    total = None
    for act_ref, dy_ref in zip(refs[:chunks], refs[chunks : 2 * chunks]):
        dy = dy_ref[...].reshape(act_ref.shape[0], dy_ref.shape[2])
        part = product_tn(act_ref[...], dy)
        total = part if total is None else total + part
    refs[2 * chunks][...] = total.astype(BF16)


def down_gradient(acts, every_dy, local):
    rows, width = acts[0].shape
    chunks = len(acts)
    peers = every_dy.shape[0]
    piece = width // 4

    def spec(chunk):
        return pl.BlockSpec(
            (peers, rows // peers, width),
            lambda i: (0, chunk, 0),
            pipeline_mode=pl.Buffered(1),
        )

    return pl.pallas_call(
        functools.partial(down_kernel, chunks),
        grid=(4,),
        in_specs=[pl.BlockSpec((rows, piece), lambda i: (0, i))] * chunks
        + [spec(chunk) for chunk in range(chunks)],
        out_specs=pl.BlockSpec((piece, width), lambda i: (i, 0)),
        out_shape=jax.ShapeDtypeStruct((width, width), BF16),
        compiler_params=pltpu.CompilerParams(vmem_limit_bytes=VMEM_LIMIT),
        cost_estimate=pl.CostEstimate(
            flops=2 * chunks * rows * width * width, bytes_accessed=chunks * rows * width * 4, transcendentals=0
        ),
        name="down_gradient",
    )(*acts, *([every_dy] * chunks)).reshape(local, width // local, width)


def row_copies(place_ref, pieces, target, sem):
    copies = []
    for i, piece in enumerate(pieces):
        rows = piece.shape[0]
        first = pl.multiple_of(place_ref[i], 16)
        copies.append(
            pltpu.make_async_copy(piece, target.at[pl.ds(first, rows), :], sem.at[i])
        )
    for copy in copies:
        copy.start()
    return copies


def scale_of(values):
    return lax.rsqrt(jnp.mean(values * values, axis=-1, keepdims=True) + 1e-06)


def rotate(values, cosine, sine):
    lane = lax.broadcasted_iota(jnp.int32, values.shape, 1) % HEAD_DIM
    half = HEAD_DIM // 2
    turned = jnp.where(
        lane < half, pltpu.roll(values, LANES - half, 1), pltpu.roll(values, half, 1)
    )
    return values * cosine + turned * sine


def project_kernel(count, experts, place_ref, x_ref, cos_ref, sin_ref, *refs):
    pieces = refs[:count]
    normed_ref, q_ref, k_ref, v_ref, gains_ref, router_ref, weight, sem = refs[count:]
    copies = row_copies(place_ref, pieces, weight, sem)
    x = x_ref[...].astype(F32)
    scaled = x * scale_of(x)
    cosine, sine = cos_ref[...], sin_ref[...]
    for copy in copies:
        copy.wait()
    q_width, kv_width = q_ref.shape[1], k_ref.shape[1]
    small = weight[:, q_width + 2 * kv_width :]
    lane = lax.broadcasted_iota(jnp.int32, small.shape, 1)
    router_ref[...] = jnp.where(lane < experts, small.astype(F32), 0.0).astype(BF16)
    turned = small.astype(F32).T
    gains_ref[...] = jnp.concatenate(
        [turned[experts : experts + 2], jnp.zeros((6, turned.shape[1]), F32)], axis=0
    )
    normed = (scaled * turned[experts : experts + 1]).astype(BF16)
    normed_ref[...] = normed
    for first in range(0, q_width, 256):
        values = jnp.dot(normed, weight[:, first : first + 256], preferred_element_type=F32)
        for part in (0, LANES):
            q_ref[:, first + part : first + part + LANES] = rotate(
                values[:, part : part + LANES], cosine, sine
            ).astype(BF16)
    for first in range(0, kv_width, 256):
        at = q_width + first
        values = jnp.dot(normed, weight[:, at : at + 256], preferred_element_type=F32)
        for part in (0, LANES):
            k_ref[:, first + part : first + part + LANES] = rotate(
                values[:, part : part + LANES], cosine, sine
            ).astype(BF16)
    at = q_width + kv_width
    v_ref[...] = jnp.dot(
        normed, weight[:, at : at + kv_width], preferred_element_type=F32
    ).astype(BF16)


def simple_call(kernel, name, prefetch, inputs, pieces, outputs, scratch, time):
    def whole(shape):
        return pl.BlockSpec(shape, lambda i, p: (0,) * len(shape))

    return pl.pallas_call(
        kernel,
        grid_spec=pltpu.PrefetchScalarGridSpec(
            num_scalar_prefetch=1,
            grid=(1,),
            in_specs=[whole(value.shape) for value in inputs]
            + [pl.BlockSpec(memory_space=pl.ANY)] * len(pieces),
            out_specs=[whole(shape) for shape, _ in outputs],
            scratch_shapes=scratch,
        ),
        out_shape=[jax.ShapeDtypeStruct(shape, kind) for shape, kind in outputs],
        compiler_params=pltpu.CompilerParams(vmem_limit_bytes=VMEM_LIMIT),
        cost_estimate=cost(time),
        name=name,
    )(prefetch, *inputs, *pieces)


def key_window(tile, size, rows):
    low = max(0, tile * size - (rows // 2 - 1)) // size * size
    return low, (tile + 1) * size


def tile_mask(start_ref, low, high, first, size):
    shape = (high - low, size)
    key = lax.broadcasted_iota(jnp.int32, shape, 0) + low
    query = lax.broadcasted_iota(jnp.int32, shape, 1) + first
    seen = (key >= start_ref[:, first : first + size]) & (key <= query)
    return jnp.concatenate([seen, seen], axis=1)


def two_heads(values):
    return jnp.concatenate([values[:, :HEAD_DIM], values[:, HEAD_DIM:]], axis=0)


def untwo(values):
    size = values.shape[1] // 2
    return jnp.concatenate([values[:, :size], values[:, size:]], axis=0).T


def attend_kernel(start_ref, q_ref, k_ref, v_ref, out_ref, log_ref):
    rows = q_ref.shape[0]
    size = LANES
    scale = 1.0 / math.sqrt(HEAD_DIM)
    logs = [[], []]
    for tile in range(rows // size):
        low, high = key_window(tile, size, rows)
        first = tile * size
        seen = tile_mask(start_ref, low, high, first, size)
        for pair in range(2):
            q = two_heads(q_ref[first : first + size, pair * LANES : (pair + 1) * LANES])
            q = (q.astype(F32) * scale).astype(BF16)
            at = pair * HEAD_DIM
            scores = product_transposed_right(k_ref[low:high, at : at + HEAD_DIM], q)
            scores = jnp.where(seen, scores, -1e30)
            top = jnp.max(scores, axis=0, keepdims=True)
            powers = jnp.exp(scores - top)
            total = jnp.sum(powers, axis=0, keepdims=True)
            low_chances = (powers * (1.0 / total)).astype(BF16)
            mixed = product_tn(v_ref[low:high, at : at + HEAD_DIM], low_chances)
            out_ref[first : first + size, pair * LANES : (pair + 1) * LANES] = untwo(mixed).astype(
                BF16
            )
            logs[pair].append(top + jnp.log(total))
    lines = []
    for pair in range(2):
        for head in range(2):
            lines.append(
                jnp.concatenate([v[:, head * size : (head + 1) * size] for v in logs[pair]], axis=1)
            )
    log_ref[...] = jnp.concatenate(lines + [jnp.zeros((4, rows), F32)], axis=0)


def attend_back_kernel(
    start_ref, q_ref, k_ref, v_ref, grad_ref, log_ref, cos_ref, sin_ref, qb_ref, kb_ref, vb_ref
):
    rows = q_ref.shape[0]
    size = LANES
    tiles = rows // size
    scale = 1.0 / math.sqrt(HEAD_DIM)
    key_sums = [[None] * tiles, [None] * tiles]
    value_sums = [[None] * tiles, [None] * tiles]

    def add(sums, low, part):
        for i in range(part.shape[0] // size):
            piece = part[i * size : (i + 1) * size]
            at = low // size + i
            sums[at] = piece if sums[at] is None else sums[at] + piece

    for tile in range(tiles):
        low, high = key_window(tile, size, rows)
        first = tile * size
        seen = tile_mask(start_ref, low, high, first, size)
        cosine, sine = cos_ref[first : first + size], sin_ref[first : first + size]
        for pair in range(2):
            lanes = slice(pair * LANES, (pair + 1) * LANES)
            q = two_heads(q_ref[first : first + size, lanes])
            q = (q.astype(F32) * scale).astype(BF16)
            grad = two_heads(grad_ref[first : first + size, lanes])
            at = pair * HEAD_DIM
            keys = k_ref[low:high, at : at + HEAD_DIM]
            scores = jnp.where(seen, product_transposed_right(keys, q), -1e30)
            log_total = jnp.concatenate(
                [
                    log_ref[2 * pair : 2 * pair + 1, first : first + size],
                    log_ref[2 * pair + 1 : 2 * pair + 2, first : first + size],
                ],
                axis=1,
            )
            chances = jnp.exp(scores - log_total)
            chance_grad = product_transposed_right(v_ref[low:high, at : at + HEAD_DIM], grad)
            mean = jnp.sum(chances * chance_grad, axis=0, keepdims=True)
            score_grad = (chances * (chance_grad - mean)).astype(BF16)
            add(value_sums[pair], low, jnp.dot(chances.astype(BF16), grad, preferred_element_type=F32))
            add(key_sums[pair], low, jnp.dot(score_grad, q, preferred_element_type=F32))
            query_grad = untwo(product_tn(keys, score_grad)) * scale
            qb_ref[first : first + size, lanes] = rotate(query_grad, cosine, -sine).astype(BF16)
    for tile in range(tiles):
        here = slice(tile * size, (tile + 1) * size)
        both = jnp.concatenate([key_sums[0][tile], key_sums[1][tile]], axis=1)
        kb_ref[here, :] = rotate(both, cos_ref[here], -sin_ref[here]).astype(BF16)
        both = jnp.concatenate([value_sums[0][tile], value_sums[1][tile]], axis=1)
        vb_ref[here, :] = both.astype(BF16)


def attention_specs(rows):
    return (
        pl.BlockSpec((1, rows), lambda i: (0, 0)),
        pl.BlockSpec((rows, 2 * LANES), lambda i: (0, i)),
        pl.BlockSpec((rows, LANES), lambda i: (0, i)),
        pl.BlockSpec((8, rows), lambda i: (i, 0)),
        pl.BlockSpec((rows, LANES), lambda i: (0, 0)),
    )


def attend(start, q, k, v):
    rows = q.shape[0]
    one, wide, thin, line, _ = attention_specs(rows)
    steps = k.shape[1] // LANES
    return pl.pallas_call(
        attend_kernel,
        grid=(steps,),
        in_specs=[one, wide, thin, thin],
        out_specs=[wide, line],
        out_shape=[
            jax.ShapeDtypeStruct(q.shape, BF16),
            jax.ShapeDtypeStruct((8 * steps, rows), F32),
        ],
        compiler_params=pltpu.CompilerParams(vmem_limit_bytes=VMEM_LIMIT),
        cost_estimate=cost(13),
        name="attend",
    )(start, q, k, v)


def attend_back(start, q, k, v, grad, logs, cosine, sine):
    rows = q.shape[0]
    one, wide, thin, line, table = attention_specs(rows)
    return pl.pallas_call(
        attend_back_kernel,
        grid=(k.shape[1] // LANES,),
        in_specs=[one, wide, thin, thin, wide, line, table, table],
        out_specs=[wide, thin, thin],
        out_shape=[
            jax.ShapeDtypeStruct(q.shape, BF16),
            jax.ShapeDtypeStruct(k.shape, BF16),
            jax.ShapeDtypeStruct(v.shape, BF16),
        ],
        compiler_params=pltpu.CompilerParams(vmem_limit_bytes=VMEM_LIMIT),
        cost_estimate=cost(15),
        name="attend_back",
    )(start, q, k, v, grad, logs, cosine, sine)


def mix_kernel(count, place_ref, attended_ref, x_ref, mask_ref, router_ref, gains_ref, *refs):
    pieces = refs[:count]
    state_ref, low_ref, high_ref, gates_ref, weight, sem = refs[count:]
    copies = row_copies(place_ref, pieces, weight, sem)
    for copy in copies:
        copy.wait()
    state = x_ref[...].astype(F32) + jnp.dot(
        attended_ref[...], weight[...], preferred_element_type=F32
    )
    state_ref[...] = state
    mixed = (state * scale_of(state) * gains_ref[1:2, :]).astype(BF16)
    low_ref[...] = mixed[: low_ref.shape[0]]
    high_ref[...] = mixed[low_ref.shape[0] :]
    logits = jnp.dot(mixed, router_ref[...], preferred_element_type=F32)
    logits = jnp.where(mask_ref[...] > 0, logits, -1e30)
    powers = jnp.exp(logits - jnp.max(logits, axis=1, keepdims=True))
    gates_ref[...] = powers / jnp.sum(powers, axis=1, keepdims=True)


def mix_back_kernel(
    count,
    chunks,
    experts,
    place_ref,
    attended_ref,
    state_ref,
    low_ref,
    high_ref,
    dy_ref,
    gates_ref,
    gate_grad_ref,
    router_ref,
    gains_ref,
    *refs,
):
    sums = refs[:chunks]
    pieces = refs[chunks : chunks + count]
    state_grad_ref, attended_grad_ref, pack_ref, weight, sem = refs[chunks + count :]
    copies = row_copies(place_ref, pieces, weight, sem)
    gates = gates_ref[...]
    gate_grad = gate_grad_ref[...]
    logit_grad = (
        gates * (gate_grad - jnp.sum(gates * gate_grad, axis=1, keepdims=True))
    ).astype(BF16)
    rows = jnp.concatenate([part[...] for part in sums], axis=0).astype(F32)
    mixed_grad = product_transposed_right(logit_grad, router_ref[...]) + rows
    state = state_ref[...]
    scale = scale_of(state)
    gain_grad = jnp.sum(mixed_grad * (state * scale), axis=0, keepdims=True)
    scaled = gains_ref[1:2, :] * mixed_grad
    mean = jnp.mean(scaled * state, axis=1, keepdims=True)
    state_grad = dy_ref[...].astype(F32) + scale * scaled - state * (scale * scale * scale * mean)
    state_grad_ref[...] = state_grad
    branch = state_grad.astype(BF16)
    for copy in copies:
        copy.wait()
    attended_grad_ref[...] = product_transposed_right(branch, weight[...]).astype(BF16)
    width = state.shape[1]
    pack_ref[:, :width] = product_tn(attended_ref[...], branch).astype(BF16)
    line = lax.broadcasted_iota(jnp.int32, (LANES, width), 0)
    column = jnp.where(line == experts, gain_grad, 0.0).T
    pack_ref[:, width:] = (product_tn(jnp.concatenate([low_ref[...], high_ref[...]], axis=0), logit_grad) + column).astype(BF16)


def project_weights_kernel(place_ref, normed_ref, qb_ref, kb_ref, vb_ref, pack_ref):
    normed = normed_ref[...]
    at = 0
    for back_ref in (qb_ref, kb_ref, vb_ref):
        width = back_ref.shape[1]
        pack_ref[:, at : at + width] = product_tn(normed, back_ref[...]).astype(BF16)
        at += width


def project_back_kernel(
    count, place_ref, x_ref, state_grad_ref, gains_ref, qb_ref, kb_ref, vb_ref, *refs
):
    pieces = refs[:count]
    out_ref, weight, sem = refs[count:]
    copies = row_copies(place_ref, pieces, weight, sem)
    for copy in copies:
        copy.wait()
    grad = None
    first = 0
    for back_ref in (qb_ref, kb_ref, vb_ref):
        width = back_ref.shape[1]
        part = product_transposed_right(back_ref[...], weight[:, first : first + width])
        grad = part if grad is None else grad + part
        first += width
    x = x_ref[...].astype(F32)
    scale = scale_of(x)
    scaled = gains_ref[0:1, :] * grad
    mean = jnp.mean(scaled * x, axis=1, keepdims=True)
    out_ref[...] = (
        state_grad_ref[...] + scale * scaled - x * (scale * scale * scale * mean)
    ).astype(BF16)


def per_device(
    tokens,
    gain_attn,
    w_query,
    key_weight,
    value_weight,
    w_out,
    gain_mix,
    router,
    w_gate,
    w_up,
    w_down,
    routes,
    lengths,
    cotangent,
):
    total_rows, model_width = tokens.shape
    experts = router.shape[1]
    local_experts, _, hidden = w_gate.shape
    peers = lax.axis_size("expert")
    part_rows, q_width = w_query.shape
    kv_width = key_weight.shape[1]
    first_width = q_width + 2 * kv_width + LANES

    small = jnp.concatenate(
        [
            router,
            gain_attn[:, None],
            gain_mix[:, None],
            jnp.zeros((part_rows, LANES - experts - 2), BF16),
        ],
        axis=1,
    )
    first_pieces, first_places = fetch_rows(
        jnp.concatenate([w_query, key_weight, value_weight, small], axis=1)
    )
    expert_ids = jnp.arange(experts, dtype=jnp.int32)
    chosen = jnp.any(routes[:, :, None] == expert_ids[None, None, :], axis=1).astype(BF16)
    mask_rows = total_rows * experts // model_width
    mask_space = -(-mask_rows // 16) * 16
    every_dy = lax.all_gather(
        jnp.concatenate(
            [
                cotangent,
                jnp.pad(
                    chosen.reshape(mask_rows, model_width), ((0, mask_space - mask_rows), (0, 0))
                ),
            ],
            axis=0,
        ),
        "expert",
        axis=0,
    )
    every_mask = jnp.pad(
        every_dy[:, total_rows : total_rows + mask_rows].reshape(peers, total_rows, experts),
        ((0, 0), (0, 0), (0, LANES - experts)),
    )
    own_mask = jnp.pad(chosen, ((0, 0), (0, LANES - experts)))

    doc_ends = jnp.cumsum(lengths[0])
    token_index = jnp.arange(total_rows, dtype=jnp.int32)
    past_end = token_index[:, None] >= doc_ends[None, :]
    doc_start = jnp.sum(jnp.where(past_end, lengths[0][None, :], 0), axis=1)
    position = (token_index - doc_start).astype(F32)
    half_head = HEAD_DIM // 2
    inverse = 10000.0 ** (-(jnp.arange(half_head, dtype=F32) * 2.0 / HEAD_DIM))
    angles = position[:, None] * inverse[None, :]
    cosine, sine = jnp.cos(angles), jnp.sin(angles)
    cosine = jnp.concatenate([cosine] * (LANES // half_head), axis=1)
    sine = jnp.concatenate([-sine, sine] * (LANES // HEAD_DIM), axis=1)
    start = doc_start[None, :].astype(jnp.int32)

    normed, q, k, v, gains, router_lanes = simple_call(
        functools.partial(project_kernel, len(first_pieces), experts),
        "project",
        first_places,
        [tokens, cosine, sine],
        first_pieces,
        [
            (tokens.shape, BF16),
            ((total_rows, q_width), BF16),
            ((total_rows, kv_width), BF16),
            ((total_rows, kv_width), BF16),
            ((8, model_width), F32),
            ((model_width, LANES), BF16),
        ],
        [
            pltpu.VMEM((model_width, first_width), BF16),
            pltpu.SemaphoreType.DMA((len(first_pieces),)),
        ],
        8,
    )
    out_pieces, out_places = fetch_rows(w_out, first_pieces[-1], normed)
    attended, logs = attend(start, q, k, v)
    state, mixed_low, mixed_high, gates = simple_call(
        functools.partial(mix_kernel, len(out_pieces)),
        "mix",
        out_places,
        [attended, tokens, own_mask, router_lanes, gains],
        out_pieces,
        [
            (tokens.shape, F32),
            ((total_rows // 2, model_width), BF16),
            ((total_rows // 2, model_width), BF16),
            ((total_rows, LANES), F32),
        ],
        [
            pltpu.VMEM((q_width, model_width), BF16),
            pltpu.SemaphoreType.DMA((len(out_pieces),)),
        ],
        7,
    )

    packed = jnp.concatenate([jnp.concatenate([w_gate, w_up], axis=2), w_down], axis=1)
    weights = fetch_experts(packed, out_pieces[1:2], mixed_low)
    every_x, out_part, row_part, act, gate_back, up_back, scores_part = [], [], [], [], [], [], []
    for chunk, mixed in enumerate((mixed_low, mixed_high)):
        gathered = lax.all_gather(mixed, "expert", axis=0, tiled=True)
        results = run_experts(
            gathered, every_dy, every_mask, router_lanes, weights, chunk, out_part[-1:]
        )
        every_x.append(gathered)
        for kept, result in zip((out_part, row_part, act, gate_back, up_back, scores_part), results):
            kept.append(result)
    row_sum = [
        lax.psum_scatter(rows, "expert", scatter_dimension=0, tiled=True) for rows in row_part
    ]
    sent_scores = jnp.concatenate(
        [values[:, :local_experts].reshape(peers, -1, LANES) for values in scores_part], axis=1
    )
    gate_grad = lax.all_to_all(sent_scores, "expert", split_axis=0, concat_axis=0, tiled=True)
    gate_grad = (
        gate_grad.reshape(peers, total_rows, local_experts)
        .transpose(1, 0, 2)
        .reshape(total_rows, experts)
    )
    gate_grad = jnp.pad(gate_grad, ((0, 0), (0, LANES - experts)))
    act, gate_grad = lax.optimization_barrier((act, gate_grad))
    down_grad = down_gradient(act, every_dy, local_experts)
    gu_grad = gate_up_gradient(every_x, gate_back, up_back, local_experts)
    four = lax.axis_size("shard") == 4 and local_experts % 2 == 0
    if four:
        gu_own, gu_one, gu_two, gu_far = split_parts(gu_grad, 1)
        gu_low, gu_high = send_far(gu_far)
        down_own, down_one, down_two, down_far = split_parts(down_grad, 1)
        (row_sum, gate_grad, gu_own, gu_one, gu_two, gu_low, gu_high, down_far) = (
            lax.optimization_barrier(
                (row_sum, gate_grad, gu_own, gu_one, gu_two, gu_low, gu_high, down_far)
            )
        )
        down_low, down_high = send_far(down_far)
    else:
        row_sum, gate_grad, gu_grad, down_grad = lax.optimization_barrier(
            (row_sum, gate_grad, gu_grad, down_grad)
        )
    out_whole, _ = lax.optimization_barrier((out_part[-1], row_sum[-1]))
    out_sum = lax.psum_scatter(out_whole, "expert", scatter_dimension=0)

    state_grad, attended_grad, pack = simple_call(
        functools.partial(mix_back_kernel, len(out_pieces), 2, experts),
        "mix_back",
        out_places,
        [
            attended,
            state,
            mixed_low,
            mixed_high,
            cotangent,
            gates,
            gate_grad,
            router_lanes,
            gains,
            *row_sum,
        ],
        out_pieces,
        [
            (tokens.shape, F32),
            ((total_rows, q_width), BF16),
            ((q_width, model_width + LANES), BF16),
        ],
        [
            pltpu.VMEM((q_width, model_width), BF16),
            pltpu.SemaphoreType.DMA((len(out_pieces),)),
        ],
        10,
    )
    backs = attend_back(start, q, k, v, attended_grad, logs, cosine, sine)
    early = pair_cores(pack)
    backs, early = lax.optimization_barrier((backs, early))
    (late_pack,) = simple_call(
        project_weights_kernel,
        "project_weights",
        first_places,
        [normed, *backs],
        [],
        [((model_width, first_width - LANES), BF16)],
        [],
        6,
    )
    late = pair_cores(late_pack)
    backs, state_grad, late = lax.optimization_barrier((backs, state_grad, late))
    if four:
        gu_low, gu_high, down_low, down_high, late = lax.optimization_barrier(
            (gu_low, gu_high, down_low, down_high, late)
        )
    sent = late
    late = sum_near(late)
    early = sum_near(early, late)
    if four:
        gu_low, gu_high, down_low, down_high, _ = lax.optimization_barrier(
            (gu_low, gu_high, down_low, down_high, sent)
        )
        gu_one, gu_two = send_near(*join_near(gu_one, gu_two, gu_low, gu_high))
        down_one, down_two = send_near(*join_near(down_one, down_two, down_low, down_high))
    (input_grad,) = simple_call(
        functools.partial(project_back_kernel, len(first_pieces)),
        "project_back",
        first_places,
        [tokens, state_grad, gains, *backs],
        first_pieces,
        [(tokens.shape, BF16)],
        [
            pltpu.VMEM((model_width, first_width), BF16),
            pltpu.SemaphoreType.DMA((len(first_pieces),)),
        ],
        7,
    )
    late, early, input_grad = lax.optimization_barrier((late, early, input_grad))
    state, _ = lax.optimization_barrier((state, late))
    output = (state + out_sum.astype(F32)).astype(BF16)
    if four:
        gu_parts, _ = lax.optimization_barrier(((gu_own, gu_one, gu_two), late))
        gu_sum, expert_down_sum = add_up(gu_parts), add_up((down_own, down_one, down_two))
    else:
        gu_sum, expert_down_sum = plain_scatter_sum(gu_grad, 1), plain_scatter_sum(down_grad, 1)
    expert_gate_sum = gu_sum[:, :, :hidden]
    expert_up_sum = gu_sum[:, :, hidden:]
    whole, output, (expert_gate_sum, expert_up_sum, expert_down_sum) = sum_far(
        jnp.concatenate([late, early], axis=1),
        output,
        (expert_gate_sum, expert_up_sum, expert_down_sum),
    )
    late, early = whole[:, : late.shape[1]], whole[:, late.shape[1] :]
    projections = (
        (w_query, late[:, :q_width]),
        (key_weight, late[:, q_width : q_width + kv_width]),
        (value_weight, late[:, q_width + kv_width :]),
    )
    gain_sum = add_up(
        jnp.sum(weight.astype(F32) * grad, axis=1) for weight, grad in projections
    ) / gain_attn.astype(F32)
    q_end = q_width
    return (
        output,
        input_grad,
        gain_sum,
        late[:, :q_end],
        late[:, q_end : q_end + kv_width],
        late[:, q_end + kv_width : q_end + 2 * kv_width],
        early[:, :model_width],
        early[:, model_width + experts],
        early[:, model_width : model_width + experts],
        expert_gate_sum,
        expert_up_sum,
        expert_down_sum,
    )


def solution(mesh):
    in_specs = (
        P(("expert", "shard"), None),
        P("shard"),
        P("shard", None),
        P("shard", None),
        P("shard", None),
        P("shard", None),
        P("shard"),
        P("shard", None),
        P("expert", "shard", None),
        P("expert", "shard", None),
        P("expert", "shard", None),
        P(("expert", "shard"), None),
        P(("expert", "shard"), None),
        P(("expert", "shard"), None),
    )
    out_specs = (
        P(("expert", "shard"), None),
        P(("expert", "shard"), None),
        P("shard"),
        P("shard", None),
        P("shard", None),
        P("shard", None),
        P("shard", None),
        P("shard"),
        P("shard", None),
        P("expert", "shard", None),
        P("expert", "shard", None),
        P("expert", "shard", None),
    )
    return jax.shard_map(
        per_device, mesh=mesh, in_specs=in_specs, out_specs=out_specs, check_vma=False
    )
```
